32 devices in a mesh: section: 4 (over y, core), dp: 8 (over z, x).
Axes of the slice: x: 2, y: 2, z: 4, core: 2. Of those that a mesh axis runs over, the one named last changes fastest.
Arguments:
- table: bfloat16 [32000, 512], P(('section', 'dp')), may hold values from -6 to 6
- piece_ids: int32 [1024, 8], P('dp'), may hold values from 0 to 31999
- piece_counts: int32 [1024], P('dp'), may hold values from 1 to 8
- vocab_size: int32 [1], replicated, may hold values from 768 to 1024
- norm_gain: float32 [4, 2, 512], P('section'), may hold values from 0.5 to 1.5
- shift_bias: float32 [4, 4, 512], P('section'), may hold values from -2.5 to 2.5
- up_bias: float32 [4, 2048], P('section'), may hold values from -2.5 to 2.5
- qkv_weight: bfloat16 [4, 512, 1536], P('section'), may hold values from -0.25 to 0.25
- out_weight: bfloat16 [4, 512, 512], P('section'), may hold values from -0.5 to 0.5
- up_weight: bfloat16 [4, 512, 2048], P('section'), may hold values from -0.25 to 0.25
- down_weight: bfloat16 [4, 2048, 512], P('section'), may hold values from -0.125 to 0.125
- proj_weight: bfloat16 [512, 2048], P(None, 'section'), may hold values from -0.25 to 0.25
- embed_cotangent: bfloat16 [1024, 2048], P('dp', 'section'), may hold values from -6 to 6
Outputs:
- embeddings: float32 [1024, 2048], P('dp', 'section')
- table_grad: float32 [32000, 512], P(('section', 'dp'))
- norm_gain_grad: float32 [4, 2, 512], P('section', None, 'dp')
- shift_bias_grad: float32 [4, 4, 512], P('section', None, 'dp')
- up_bias_grad: float32 [4, 2048], P('section', 'dp')
- qkv_grad: float32 [4, 512, 1536], P('section', 'dp')
- out_grad: float32 [4, 512, 512], P('section', 'dp')
- up_grad: float32 [4, 512, 2048], P('section', 'dp')
- down_grad: float32 [4, 2048, 512], P('section', 'dp')
- proj_grad: float32 [512, 2048], P('dp', 'section')
The draws below stay inside these ranges and needn't reach their ends.
Inputs may be any that keep to these rules, and one draw needn't show every extreme that they name: Entries numbered vocab_size and above are padding. `piece_counts`: slots at or beyond an entry's count are padding.
All inputs are finite; a program needn't handle non-finite values.
Results may differ from the reference program's by a relative error of at most 0.024.
Values may be sent and summed in bfloat16 or wider, within the bound.
A program may use at most 192 MiB of HBM per device.

```python
import math
import jax
import jax.numpy as jnp
import numpy as np
from jax import lax

D = 512
HEADS = 8
FF = 2048
OUT = 2048
PIECES = 32000
P_SIZE = 8
LAYERS = 4
ENTRIES = 1024


def place_ends(values, own_key, least, top_value):
    shape = values.shape
    index_at = [jax.random.randint(jax.random.fold_in(own_key, axis), (), 0, shape[axis]) for axis in range(len(shape))]
    values = values.at[tuple(index_at)].set(least)
    longest = shape.index(max(shape))
    index_at[longest] = (index_at[longest] + 1) % shape[longest]
    return values.at[tuple(index_at)].set(top_value)


def shard_levels(own_key, dims, cuts, least, top_value):
    def one(axis_at, shards_of):
        steps = jax.random.uniform(jax.random.fold_in(jax.random.fold_in(own_key, 6), axis_at), (shards_of,), jnp.float32, least / len(cuts), top_value / len(cuts))
        return jnp.repeat(jnp.exp(steps), dims[axis_at] // shards_of).reshape((-1,) + (1,) * (len(dims) - axis_at - 1))

    loudness = one(*cuts[0])
    for cut in cuts[1:]:
        loudness = loudness * one(*cut)
    return loudness


def rank_bounds(number_of, slope):
    portions = [(1 << 20) // math.isqrt(rank ** slope) + 1 for rank in range(1, number_of + 1)]
    deviation = 1 + sum(portions) // (1 << 30)
    return np.cumsum(np.array([max(1, weight // deviation) for weight in portions]))


def ranked_ids(key, shape, amount, slope):
    listing = rank_bounds(amount, slope)
    lot = jax.random.randint(jax.random.fold_in(key, 1), shape, 0, int(listing[amount - 1]))
    rank = jnp.searchsorted(jnp.asarray(listing, jnp.int32), lot, side="right")
    return jax.random.permutation(jax.random.fold_in(key, 2), amount)[rank].astype(jnp.int32)


def centred(own_key, shape, width, limit, cuts=(), kind=jnp.bfloat16):
    values = jax.random.normal(own_key, shape, jnp.float32) * width
    if len(cuts) > 0:
        values = shard_levels(own_key, shape, cuts, -0.22, 0.18) * values
    return jnp.clip(values, min=-limit, max=limit).astype(kind)


def setup_inputs(seed: int = 0) -> dict:
    seeds = jax.random.split(jax.random.key(seed), 14)
    return {
        "table": centred(seeds[0], (PIECES, D), 1.0, 6.0, ((0, 32),)),
        "piece_ids": place_ends(ranked_ids(seeds[1], (ENTRIES, P_SIZE), PIECES, 2), jax.random.fold_in(seeds[1], 3), 0, PIECES - 1).astype(jnp.int32),
        "piece_counts": place_ends(jax.random.randint(seeds[2], (ENTRIES,), 1, P_SIZE + 1), jax.random.fold_in(seeds[2], 1), 1, P_SIZE).astype(jnp.int32),
        "vocab_size": jax.random.randint(seeds[3], (1,), 3 * ENTRIES // 4, ENTRIES + 1).astype(jnp.int32),
        "norm_gain": jnp.clip(1.0 + 0.1 * jax.random.normal(seeds[4], (LAYERS, 2, D), jnp.float32), 0.5, 1.5),
        "shift_bias": centred(seeds[5], (LAYERS, 4, D), 0.3, 2.5, ((0, 4),), jnp.float32),
        "up_bias": centred(seeds[6], (LAYERS, FF), 0.3, 2.5, ((0, 4),), jnp.float32),
        "qkv_weight": centred(seeds[7], (LAYERS, D, 3 * D), D ** -0.5, 0.25, ((0, 4),)),
        "out_weight": centred(seeds[8], (LAYERS, D, D), (D // 4) ** -0.5, 0.5, ((0, 4),)),
        "up_weight": centred(seeds[9], (LAYERS, D, FF), D ** -0.5, 0.25, ((0, 4),)),
        "down_weight": centred(seeds[10], (LAYERS, FF, D), FF ** -0.5, 0.125, ((0, 4),)),
        "proj_weight": centred(seeds[11], (D, OUT), D ** -0.5, 0.25, ((1, 4),)),
        "embed_cotangent": centred(seeds[12], (ENTRIES, OUT), 1.0, 6.0, ((0, 8), (1, 4))),
    }


@jax.custom_vjp
def low(v):
    return lax.optimization_barrier(v.astype(jnp.bfloat16)).astype(jnp.float32)

@jax.custom_vjp
def low_back(v):
    return v

def low_keep(v):
    return (low(v), None)

def low_pass(kept, grad):
    return (grad,)

def back_keep(v):
    return (v, None)

def back_low(kept, grad):
    return (low(grad),)
low.defvjp(low_keep, low_pass)
low_back.defvjp(back_keep, back_low)
PRECISE = lax.Precision.HIGHEST
EPSILON = 1e-05
MASKED = -1e+30

def normalize(values, gain, offset):
    centered = values - lax.optimization_barrier(jnp.mean(values, axis=-1, keepdims=True))
    spread = lax.optimization_barrier(jnp.mean(centered * centered, axis=-1, keepdims=True))
    return centered * lax.rsqrt(spread + EPSILON) * gain + offset

def project(values, weight):
    return jnp.einsum('bpd,df->bpf', values, weight, precision=PRECISE)

def encoder_layer(hidden_in, key_mask, gains, offsets, w_qkv, w_out, w_up, b_up, w_down):
    blocks, pieces, model_width = hidden_in.shape
    head_size = model_width // HEADS
    normed = low(normalize(hidden_in, gains[0], offsets[0]))
    joined = low_back(low(project(normed, w_qkv)))
    heads_split = joined.reshape(blocks, pieces, 3, HEADS, head_size)
    queries = heads_split[:, :, 0]
    key_rows = heads_split[:, :, 1]
    value_rows = heads_split[:, :, 2]
    scores = low_back(jnp.einsum('bihe,bjhe->bhij', queries, key_rows, precision=PRECISE) * head_size ** (-0.5))
    scores = jnp.where(key_mask[:, None, None, :], scores, MASKED)
    shifted = jnp.exp(scores - lax.optimization_barrier(jnp.max(scores, axis=-1, keepdims=True)))
    attn_prob = low(shifted / lax.optimization_barrier(jnp.sum(shifted, axis=-1, keepdims=True)))
    mixed_heads = jnp.einsum('bhij,bjhe->bihe', attn_prob, value_rows, precision=PRECISE)
    mixed_heads = low_back(low(mixed_heads.reshape(blocks, pieces, model_width)))
    residual = hidden_in + low_back(project(mixed_heads, w_out) + offsets[1])
    normed_two = low(normalize(residual, gains[1], offsets[2]))
    pre_act = low_back(project(normed_two, w_up) + b_up)
    activated = low(jax.nn.gelu(pre_act, approximate=False))
    return low_back(low(residual + project(activated, w_down) + offsets[3]))

def forward(arrays, piece_ids, piece_counts, live):
    table, norm_gain, shift_bias, up_bias, qkv_weight, out_weight, up_weight, down_weight, proj_weight = arrays
    entries, pieces = piece_ids.shape
    block_size = math.gcd(entries, 512)
    groups = entries // block_size

    def one_block(items):
        ids_block, counts_block, alive = items
        key_mask = jnp.arange(pieces, dtype=jnp.int32)[None, :] < counts_block[:, None]
        hidden = table[ids_block]
        for layer_index in range(LAYERS):
            hidden = encoder_layer(hidden, key_mask, norm_gain[layer_index], shift_bias[layer_index], qkv_weight[layer_index], out_weight[layer_index], up_weight[layer_index], up_bias[layer_index], down_weight[layer_index])
        weighted = lax.optimization_barrier(jnp.sum(hidden * key_mask[:, :, None].astype(jnp.float32), axis=1))
        pooled = low(weighted / counts_block[:, None].astype(jnp.float32))
        return jnp.dot(pooled, proj_weight, precision=PRECISE, preferred_element_type=jnp.float32) * alive[:, None]
    result = lax.map(jax.checkpoint(one_block), (piece_ids.reshape(groups, block_size, pieces), piece_counts.reshape(groups, block_size), live.reshape(groups, block_size)))
    return result.reshape(entries, proj_weight.shape[1])

def reference(table, piece_ids, piece_counts, vocab_size, norm_gain, shift_bias, up_bias, qkv_weight, out_weight, up_weight, down_weight, proj_weight, embed_cotangent):
    entries = piece_ids.shape[0]
    live = (jnp.arange(entries, dtype=jnp.int32) < vocab_size[0]).astype(jnp.float32)
    weights = (table, norm_gain, shift_bias, up_bias, qkv_weight, out_weight, up_weight, down_weight, proj_weight)
    floats = tuple((array_item.astype(jnp.float32) for array_item in weights))

    def run(arrays):
        return forward(arrays, piece_ids, piece_counts, live)
    embeddings, pullback = jax.vjp(run, floats)
    grads = pullback(embed_cotangent.astype(jnp.float32))[0]
    return (embeddings, grads[0], grads[1], grads[2], grads[3], grads[4], grads[5], grads[6], grads[7], grads[8])
```

```python
import functools
import jax
import jax.numpy as jnp
from jax import lax
from jax.experimental import pallas as pl
from jax.experimental.pallas import tpu as pltpu
from jax.sharding import PartitionSpec as P

HEADS = 8
LANES = 128
EPSILON = 1e-05
MASKED = -1e30
ROOT_HALF = 0.7071067811865476
DENSITY_SCALE = 0.3989422804014327
MESH = pl.DeviceIdType.MESH
F32 = jnp.float32
BF16 = jnp.bfloat16
MICRO = 128
VMEM_BYTES = 60 * 2**20


def dot_nn(left, right):
    return lax.dot_general(left, right, (((1,), (0,)), ((), ())), preferred_element_type=F32)


def dot_nt(left, right):
    return lax.dot_general(left, right, (((1,), (1,)), ((), ())), preferred_element_type=F32)


def dot_tn(left, right):
    return lax.dot_general(left, right, (((0,), (0,)), ((), ())), preferred_element_type=F32)


def statistics(values):
    centered = values - jnp.mean(values, axis=-1, keepdims=True)
    inverse = lax.rsqrt(jnp.mean(centered * centered, axis=-1, keepdims=True) + EPSILON)
    return centered * inverse, inverse


def norm_backward(weighted, normed, inverse):
    return inverse * (
        weighted
        - jnp.mean(weighted, axis=-1, keepdims=True)
        - normed * jnp.mean(weighted * normed, axis=-1, keepdims=True)
    )


def column_sum(values):
    return jnp.sum(values, axis=0, keepdims=True)


def entry_masks():
    lane = lax.broadcasted_iota(jnp.int32, (8, LANES), 1) // 8
    return [lane == e for e in range(LANES // 8)]


def compress(tall, masks):
    tall = tall.reshape(2, LANES // 8, 8, LANES)
    kept = []
    for h in range(2):
        one = tall[h, 0]
        for e in range(1, LANES // 8):
            one = jnp.where(masks[e], tall[h, e], one)
        kept.append(one)
    return kept


def expand(flat, masks):
    zero = jnp.zeros_like(flat)
    return jnp.concatenate([jnp.where(mask, flat, zero) for mask in masks], axis=0).astype(BF16)


def half_masks():
    lane = lax.broadcasted_iota(jnp.int32, (1, LANES), 1)
    low = jnp.where(lane < LANES // 2, 1.0, 0.0)
    return low.astype(BF16), (1.0 - low).astype(BF16)


def by_head(pair, halves):
    return jnp.concatenate([pair * halves[0], pair * halves[1]], axis=0)


def head_mask(count_row):
    return lax.broadcasted_iota(jnp.int32, (8, LANES), 0) < count_row


def pool_matrix(count_row):
    lane = lax.broadcasted_iota(jnp.int32, (LANES // 8, LANES), 1)
    entry = lax.broadcasted_iota(jnp.int32, (LANES // 8, LANES), 0)
    return jnp.where((lane // 8 == entry) & (lane % 8 < count_row), 1.0, 0.0)


def trunk_kernel(
    micros, width, hidden,
    x0, counts, pool_grad, gains, shifts, up_bias, w_qkv, w_out, w_up, w_down,
    a_out, dqkv_out, att_out, dbr_out, h_out, dpre_out, act_out, dy_out, dx_out, pooled_out, vec_out, upb_out,
    x_in, x_mid, resid, prob, y_out, dy_in,
    f_send, f_recv, b_send, b_recv,
):
    section = lax.axis_index("section")
    column = lax.axis_index("dp")
    stage = section // 2
    other = (lax.rem(section + 2, 4), column)
    blocks = MICRO // LANES
    score_scale = (width // HEADS) ** (-0.5)
    tiles = hidden // width

    barrier = pltpu.get_barrier_semaphore()
    pl.semaphore_signal(barrier, inc=1, device_id=other, device_id_type=MESH)
    pl.semaphore_wait(barrier, 1)

    def rows_of(m):
        return pl.ds(pl.multiple_of(m * MICRO, MICRO), MICRO)

    def forward_copy(m):
        return pltpu.make_async_remote_copy(
            y_out.at[rows_of(m)], x_in.at[rows_of(m)], f_send.at[m], f_recv.at[m],
            device_id=other, device_id_type=MESH)

    def backward_copy(m):
        return pltpu.make_async_remote_copy(
            y_out.at[rows_of(m)], dy_in.at[rows_of(m)], b_send.at[m], b_recv.at[m],
            device_id=other, device_id_type=MESH)

    def count_row(m, b):
        return counts[pl.ds(m * blocks + b, 1), :]

    vec_out[...] = jnp.zeros_like(vec_out)
    upb_out[...] = jnp.zeros_like(upb_out)

    def layer_forward(layer, m, x):
        rows = rows_of(m)
        masks, halves = entry_masks(), half_masks()
        xf = x.astype(F32)
        normed, _ = statistics(xf)
        a = (normed * gains[layer, pl.ds(0, 1), :] + shifts[layer, pl.ds(0, 1), :]).astype(BF16)
        a_out[layer, rows, :] = a
        for t in range(3):
            cols = slice(t * width, (t + 1) * width)
            dqkv_out[layer, rows, cols] = dot_nn(a, w_qkv[layer, :, cols]).astype(BF16)
        for b in range(blocks):
            block = pl.ds(pl.multiple_of(m * MICRO + b * LANES, LANES), LANES)
            keys_on = head_mask(count_row(m, b))
            for pair in range(HEADS // 2):
                cols = slice(pair * LANES, (pair + 1) * LANES)
                q = dqkv_out[layer, block, cols]
                k = dqkv_out[layer, block, slice(width + pair * LANES, width + (pair + 1) * LANES)]
                v = dqkv_out[layer, block, slice(2 * width + pair * LANES, 2 * width + (pair + 1) * LANES)]
                flats = compress(dot_nt(by_head(k, halves), q), masks)
                wide = []
                for h in range(2):
                    s = jnp.where(keys_on, flats[h] * score_scale, MASKED)
                    e = jnp.exp(s - jnp.max(s, axis=0, keepdims=True))
                    p = e / jnp.sum(e, axis=0, keepdims=True)
                    prob[layer, m * blocks + b, pl.ds((2 * pair + h) * 8, 8), :] = p
                    wide.append(expand(p, masks))
                mixed = dot_tn(jnp.concatenate(wide, axis=0), by_head(v, halves))
                att_out[layer, block, cols] = mixed.astype(BF16)
        res = xf + dot_nn(att_out[layer, rows, :], w_out[layer]) + shifts[layer, pl.ds(1, 1), :]
        resid[layer, rows, :] = res
        normed_two, _ = statistics(res)
        h_in = (normed_two * gains[layer, pl.ds(1, 1), :] + shifts[layer, pl.ds(2, 1), :]).astype(BF16)
        h_out[layer, rows, :] = h_in
        total = res + shifts[layer, pl.ds(3, 1), :]
        for t in range(tiles):
            cols = slice(t * width, (t + 1) * width)
            pre = dot_nn(h_in, w_up[layer, :, cols]) + up_bias[layer, :, cols]
            dpre_out[layer, rows, cols] = pre.astype(BF16)
            act = (pre * (0.5 * (1.0 + lax.erf(pre * ROOT_HALF)))).astype(BF16)
            total = total + dot_nn(act, w_down[layer, cols, :])
        return total.astype(BF16)

    def layer_backward(layer, m, dy):
        rows = rows_of(m)
        masks, halves = entry_masks(), half_masks()
        dyf = dy.astype(F32)
        vec_out[layer, pl.ds(5, 1), :] += column_sum(dyf)
        d_hidden = jnp.zeros((MICRO, width), F32)
        for t in range(tiles):
            cols = slice(t * width, (t + 1) * width)
            d_act = dot_nt(dy, w_down[layer, cols, :])
            pre = dpre_out[layer, rows, cols].astype(F32)
            phi = 0.5 * (1.0 + lax.erf(pre * ROOT_HALF))
            density = jnp.exp(-0.5 * pre * pre) * DENSITY_SCALE
            act_out[layer, rows, cols] = (pre * phi).astype(BF16)
            d_pre = (d_act * (phi + pre * density)).astype(BF16)
            dpre_out[layer, rows, cols] = d_pre
            upb_out[layer, :, cols] += column_sum(d_pre.astype(F32))
            d_hidden = d_hidden + dot_nt(d_pre, w_up[layer, :, cols])
        normed_two, inverse_two = statistics(resid[layer, rows, :])
        vec_out[layer, pl.ds(1, 1), :] += column_sum(d_hidden * normed_two)
        vec_out[layer, pl.ds(4, 1), :] += column_sum(d_hidden)
        d_resid = dyf + norm_backward(d_hidden * gains[layer, pl.ds(1, 1), :], normed_two, inverse_two)
        d_branch = d_resid.astype(BF16)
        dbr_out[layer, rows, :] = d_branch
        vec_out[layer, pl.ds(3, 1), :] += column_sum(d_branch.astype(F32))
        d_att = dot_nt(d_branch, w_out[layer]).astype(BF16)
        for b in range(blocks):
            block = pl.ds(pl.multiple_of(m * MICRO + b * LANES, LANES), LANES)
            for pair in range(HEADS // 2):
                c_q = slice(pair * LANES, (pair + 1) * LANES)
                c_k = slice(width + pair * LANES, width + (pair + 1) * LANES)
                c_v = slice(2 * width + pair * LANES, 2 * width + (pair + 1) * LANES)
                q = dqkv_out[layer, block, c_q]
                k = dqkv_out[layer, block, c_k]
                v = dqkv_out[layer, block, c_v]
                da = d_att[b * LANES:(b + 1) * LANES, c_q]
                flats = compress(dot_nt(by_head(v, halves), da), masks)
                wide_p, wide_s = [], []
                for h in range(2):
                    p = prob[layer, m * blocks + b, pl.ds((2 * pair + h) * 8, 8), :]
                    ds = p * (flats[h] - jnp.sum(flats[h] * p, axis=0, keepdims=True))
                    wide_p.append(expand(p, masks))
                    wide_s.append(expand(ds, masks))
                d_v = dot_nn(jnp.concatenate(wide_p, axis=1), by_head(da, halves))
                d_k = dot_nn(jnp.concatenate(wide_s, axis=1), by_head(q, halves)) * score_scale
                d_q = dot_tn(jnp.concatenate(wide_s, axis=0), by_head(k, halves)) * score_scale
                dqkv_out[layer, block, c_q] = d_q.astype(BF16)
                dqkv_out[layer, block, c_k] = d_k.astype(BF16)
                dqkv_out[layer, block, c_v] = d_v.astype(BF16)
        d_a = jnp.zeros((MICRO, width), F32)
        for t in range(3):
            cols = slice(t * width, (t + 1) * width)
            d_a = d_a + dot_nt(dqkv_out[layer, rows, cols], w_qkv[layer, :, cols])
        x = jnp.where(layer == 0, x_in[rows, :], x_mid[rows, :])
        normed, inverse = statistics(x.astype(F32))
        vec_out[layer, pl.ds(0, 1), :] += column_sum(d_a * normed)
        vec_out[layer, pl.ds(2, 1), :] += column_sum(d_a)
        dx = d_resid + norm_backward(d_a * gains[layer, pl.ds(0, 1), :], normed, inverse)
        return dx.astype(BF16)

    @pl.when(stage == 0)
    def _():
        x_in[...] = x0[...]

    def forward_step(m, carry):
        rows = rows_of(m)

        @pl.when(stage == 1)
        def _():
            forward_copy(m).wait_recv()

        x = lax.fori_loop(0, 2, lambda layer, x: forward_layer(layer, m, x), x_in[rows, :])
        y_out[rows, :] = x

        @pl.when(stage == 0)
        def _():
            forward_copy(m).start()

        @pl.when(stage == 1)
        def _():
            for b in range(blocks):
                matrix = pool_matrix(count_row(m, b))
                summed = dot_nn(matrix.astype(BF16), x[b * LANES:(b + 1) * LANES, :])
                mean = summed / jnp.sum(matrix, axis=1, keepdims=True)
                entries = pl.ds(pl.multiple_of((m * blocks + b) * (LANES // 8), LANES // 8), LANES // 8)
                pooled_out[entries, :] = mean.astype(BF16)
        return carry

    def forward_layer(layer, m, x):
        @pl.when(layer == 1)
        def _():
            x_mid[rows_of(m), :] = x

        return layer_forward(layer, m, x)

    lax.fori_loop(0, micros, forward_step, 0)

    @pl.when(stage == 0)
    def _():
        for m in range(micros):
            forward_copy(m).wait_send()

    def backward_step(m, carry):
        rows = rows_of(m)

        @pl.when(stage == 0)
        def _():
            backward_copy(m).wait_recv()
            dy_out[1, rows, :] = dy_in[rows, :]

        @pl.when(stage == 1)
        def _():
            for b in range(blocks):
                matrix = pool_matrix(count_row(m, b))
                entries = pl.ds(pl.multiple_of((m * blocks + b) * (LANES // 8), LANES // 8), LANES // 8)
                share = (pool_grad[entries, :] / jnp.sum(matrix, axis=1, keepdims=True)).astype(BF16)
                block = pl.ds(pl.multiple_of(m * MICRO + b * LANES, LANES), LANES)
                dy_out[1, block, :] = dot_tn(matrix.astype(BF16), share).astype(BF16)

        def step(i, dy):
            layer = 1 - i

            @pl.when(i == 1)
            def _():
                dy_out[0, rows, :] = dy

            return layer_backward(layer, m, dy)

        dx = lax.fori_loop(0, 2, step, dy_out[1, rows, :])
        dx_out[rows, :] = dx

        @pl.when(stage == 1)
        def _():
            y_out[rows, :] = dx
            backward_copy(m).start()
        return carry

    lax.fori_loop(0, micros, backward_step, 0)

    @pl.when(stage == 1)
    def _():
        for m in range(micros):
            backward_copy(m).wait_send()


def trunk(x0, counts, pool_grad, gains, shifts, up_bias, w_qkv, w_out, w_up, w_down):
    rows, width = x0.shape
    hidden = w_up.shape[2]
    micros = rows // MICRO
    vmem = pl.BlockSpec(memory_space=pltpu.VMEM)
    shape = jax.ShapeDtypeStruct
    outs = [
        shape((2, rows, width), BF16), shape((2, rows, 3 * width), BF16), shape((2, rows, width), BF16),
        shape((2, rows, width), BF16), shape((2, rows, width), BF16), shape((2, rows, hidden), BF16),
        shape((2, rows, hidden), BF16), shape((2, rows, width), BF16), shape((rows, width), BF16),
        shape((rows // 8, width), BF16), shape((2, 8, width), F32), shape((2, 1, hidden), F32),
    ]
    return pl.pallas_call(
        functools.partial(trunk_kernel, micros, width, hidden),
        out_shape=outs,
        in_specs=[vmem] * 10,
        out_specs=[vmem] * len(outs),
        scratch_shapes=[
            pltpu.VMEM((rows, width), BF16), pltpu.VMEM((rows, width), BF16), pltpu.VMEM((2, rows, width), F32),
            pltpu.VMEM((2, rows // LANES, 8 * HEADS, LANES), F32), pltpu.VMEM((rows, width), BF16),
            pltpu.VMEM((rows, width), BF16),
        ] + [pltpu.SemaphoreType.DMA((micros,))] * 4,
        compiler_params=pltpu.CompilerParams(collective_id=1, has_side_effects=True, vmem_limit_bytes=VMEM_BYTES),
    )(x0, counts, pool_grad, gains, shifts, up_bias, w_qkv, w_out, w_up, w_down)


def contract_rows(left, right):
    return lax.dot_general(left, right, (((0,), (0,)), ((), ())), preferred_element_type=F32)


def local(table, piece_ids, piece_counts, vocab_size, norm_gain, shift_bias, up_bias, qkv_weight, out_weight,
          up_weight, down_weight, proj_weight, embed_cotangent):
    section = lax.axis_index("section")
    column = lax.axis_index("dp")
    columns = lax.axis_size("dp")
    core = lax.rem(section, 2)
    entries, pieces = piece_ids.shape
    width = qkv_weight.shape[1]
    half = entries // 2
    positions = column * entries + jnp.arange(entries, dtype=jnp.int32)
    live = positions < vocab_size[0]
    flat_ids = piece_ids.reshape(entries * pieces)
    quarter = lax.all_gather(table, "dp", axis=0, tiled=True)
    span = quarter.shape[0]
    local_ids = flat_ids - section * span
    inside = (local_ids >= 0) & (local_ids < span)
    safe_ids = jnp.clip(local_ids, 0, span - 1)
    picked = jnp.where(inside[:, None], jnp.take(quarter, safe_ids, axis=0), 0)
    embedded = lax.psum(picked, "section")
    x0 = lax.dynamic_slice_in_dim(embedded, core * half * pieces, half * pieces, 0)
    cotangent = jnp.where(live[:, None], embed_cotangent, jnp.zeros_like(embed_cotangent))
    pool_grad = lax.psum(dot_nt(cotangent, proj_weight).astype(BF16), "section").astype(F32)
    pool_half = lax.dynamic_slice_in_dim(pool_grad, core * half, half, 0)
    my_counts = lax.dynamic_slice_in_dim(piece_counts, core * half, half, 0)
    count_rows = jnp.repeat(my_counts, pieces).reshape(-1, LANES)

    def both(value):
        swapped = lax.ppermute(value, "section", [(0, 1), (1, 0), (2, 3), (3, 2)])
        return jnp.where(core == 0, jnp.concatenate([value, swapped]), jnp.concatenate([swapped, value]))

    gains, shifts, bias = both(norm_gain), both(shift_bias), both(up_bias)[:, None, :]
    w_qkv, w_out, w_up, w_down = both(qkv_weight), both(out_weight), both(up_weight), both(down_weight)
    a, dqkv, att, dbr, h, dpre, act, dy, dx, pooled, vec, upb = trunk(
        x0, count_rows, pool_half, gains, shifts, bias, w_qkv, w_out, w_up, w_down)
    whole_pooled = lax.all_gather(pooled, "section", axis=0, tiled=True)[2 * half:]
    embeddings = jnp.dot(whole_pooled, proj_weight, preferred_element_type=F32) * live[:, None].astype(F32)
    grad_proj = contract_rows(whole_pooled, cotangent)

    def mine(value):
        own = lax.dynamic_index_in_dim(value, core, 0)
        gone = lax.dynamic_index_in_dim(value, 1 - core, 0)
        return own + lax.ppermute(gone, "section", [(0, 1), (1, 0), (2, 3), (3, 2)])

    batched = lambda left, right: lax.dot_general(
        left, right, (((1,), (1,)), ((0,), (0,))), preferred_element_type=F32)
    g_qkv, g_out, g_up, g_down = mine(batched(a, dqkv)), mine(batched(att, dbr)), mine(batched(h, dpre)), mine(batched(act, dy))
    vec, upb = mine(vec), mine(upb)
    scatter = lambda value, axis: lax.psum_scatter(value, "dp", scatter_dimension=axis, tiled=True)
    low = lambda value, axis: scatter(value.astype(BF16), axis).astype(F32)
    spread = jnp.where(section < 2, dx, jnp.zeros_like(dx))
    spread = lax.all_gather(spread, "section", axis=0, tiled=True)[: 2 * half * pieces].astype(F32)
    partial = jax.ops.segment_sum(jnp.where(inside[:, None], spread, 0.0), safe_ids, num_segments=span)
    table_grad = scatter(partial, 0)
    return (
        embeddings, table_grad, scatter(vec[:, 0:2], 2), scatter(vec[:, 2:6], 2), scatter(upb[:, 0], 1),
        low(g_qkv, 1), low(g_out, 1), low(g_up, 1), low(g_down, 1), low(grad_proj, 0),
    )


def solution(mesh):
    return jax.shard_map(
        local,
        mesh=mesh,
        in_specs=(
            P(("section", "dp"), None), P("dp", None), P("dp"), P(), P("section", None, None),
            P("section", None, None), P("section", None), P("section", None, None), P("section", None, None),
            P("section", None, None), P("section", None, None), P(None, "section"), P("dp", "section"),
        ),
        out_specs=(
            P("dp", "section"), P(("section", "dp"), None), P("section", None, "dp"), P("section", None, "dp"),
            P("section", "dp"), P("section", "dp", None), P("section", "dp", None), P("section", "dp", None),
            P("section", "dp", None), P("dp", "section"),
        ),
        check_vma=False,
    )
```

```python
import functools
import jax
import jax.numpy as jnp
from jax import lax
from jax.experimental import pallas as pl
from jax.experimental.pallas import tpu as pltpu
from jax.sharding import PartitionSpec as P

HEADS = 8
LANES = 128
EPSILON = 1e-05
MASKED = -1e30
ROOT_HALF = 0.7071067811865476
DENSITY_SCALE = 0.3989422804014327
MESH = pl.DeviceIdType.MESH
F32 = jnp.float32
BF16 = jnp.bfloat16
MICRO = 128
VMEM_BYTES = 60 * 2**20


def dot_nn(left, right):
    return lax.dot_general(left, right, (((1,), (0,)), ((), ())), preferred_element_type=F32)


def dot_nt(left, right):
    return lax.dot_general(left, right, (((1,), (1,)), ((), ())), preferred_element_type=F32)


def dot_tn(left, right):
    return lax.dot_general(left, right, (((0,), (0,)), ((), ())), preferred_element_type=F32)


def statistics(values):
    centered = values - jnp.mean(values, axis=-1, keepdims=True)
    inverse = lax.rsqrt(jnp.mean(centered * centered, axis=-1, keepdims=True) + EPSILON)
    return centered * inverse, inverse


def norm_backward(weighted, normed, inverse):
    return inverse * (
        weighted
        - jnp.mean(weighted, axis=-1, keepdims=True)
        - normed * jnp.mean(weighted * normed, axis=-1, keepdims=True)
    )


def column_sum(values):
    return jnp.sum(values, axis=0, keepdims=True)


def entry_masks():
    lane = lax.broadcasted_iota(jnp.int32, (8, LANES), 1) // 8
    return [lane == e for e in range(LANES // 8)]


def compress(tall, masks):
    tall = tall.reshape(2, LANES // 8, 8, LANES)
    kept = []
    for h in range(2):
        one = tall[h, 0]
        for e in range(1, LANES // 8):
            one = jnp.where(masks[e], tall[h, e], one)
        kept.append(one)
    return kept


def expand(flat, masks):
    zero = jnp.zeros_like(flat)
    return jnp.concatenate([jnp.where(mask, flat, zero) for mask in masks], axis=0).astype(BF16)


def half_masks():
    lane = lax.broadcasted_iota(jnp.int32, (1, LANES), 1)
    low = jnp.where(lane < LANES // 2, 1.0, 0.0)
    return low.astype(BF16), (1.0 - low).astype(BF16)


def by_head(pair, halves):
    return jnp.concatenate([pair * halves[0], pair * halves[1]], axis=0)


def head_mask(count_row):
    return lax.broadcasted_iota(jnp.int32, (8, LANES), 0) < count_row


def pool_matrix(count_row):
    lane = lax.broadcasted_iota(jnp.int32, (LANES // 8, LANES), 1)
    entry = lax.broadcasted_iota(jnp.int32, (LANES // 8, LANES), 0)
    return jnp.where((lane // 8 == entry) & (lane % 8 < count_row), 1.0, 0.0)


def trunk_kernel(
    micros, width, hidden,
    x0, counts, pool_grad, *refs
):
    own, theirs, refs = refs[:7], refs[7:14], refs[14:]
    trunk_body(micros, width, hidden, x0, counts, pool_grad, own, theirs, *refs)


def trunk_body(
    micros, width, hidden, x0, counts, pool_grad, own, theirs,
    a_out, dqkv_out, att_out, dbr_out, h_out, dpre_out, act_out, dy_out, dx_out, pooled_out, vec_out, upb_out,
    gains, shifts, up_bias, w_qkv, w_out, w_up, w_down, x_in, x_mid, resid, prob, y_out, dy_in,
    f_send, f_recv, b_send, b_recv, p_sem,
):
    section = lax.axis_index("section")
    column = lax.axis_index("dp")
    stage = section // 2
    other = (lax.rem(section + 2, 4), column)
    blocks = MICRO // LANES
    score_scale = (width // HEADS) ** (-0.5)
    tiles = hidden // width

    core = lax.rem(section, 2)
    params = (gains, shifts, up_bias, w_qkv, w_out, w_up, w_down)

    def fetch(i, source, layer):
        return pltpu.make_async_copy(source[i].at[0], params[i].at[layer], p_sem.at[i, layer])

    for first in range(2):
        @pl.when(core == first)
        def _(first=first):
            for layer in range(2):
                for i in range(len(params)):
                    fetch(i, own if layer == first else theirs, layer).start()

    def need(m, layer, *indices):
        @pl.when(m == 0)
        def _():
            for i in indices:
                fetch(i, own, layer).wait()

    barrier = pltpu.get_barrier_semaphore()
    pl.semaphore_signal(barrier, inc=1, device_id=other, device_id_type=MESH)
    pl.semaphore_wait(barrier, 1)

    def rows_of(m):
        return pl.ds(pl.multiple_of(m * MICRO, MICRO), MICRO)

    def forward_copy(m):
        return pltpu.make_async_remote_copy(
            y_out.at[rows_of(m)], x_in.at[rows_of(m)], f_send.at[m], f_recv.at[m],
            device_id=other, device_id_type=MESH)

    def backward_copy(m):
        return pltpu.make_async_remote_copy(
            y_out.at[rows_of(m)], dy_in.at[rows_of(m)], b_send.at[m], b_recv.at[m],
            device_id=other, device_id_type=MESH)

    def count_row(m, b):
        return counts[pl.ds(m * blocks + b, 1), :]

    vec_out[...] = jnp.zeros_like(vec_out)
    upb_out[...] = jnp.zeros_like(upb_out)

    def layer_forward(layer, m, x):
        rows = rows_of(m)
        masks, halves = entry_masks(), half_masks()
        xf = x.astype(F32)
        normed, _ = statistics(xf)
        need(m, layer, 0, 1, 3)
        a = (normed * gains[layer, pl.ds(0, 1), :] + shifts[layer, pl.ds(0, 1), :]).astype(BF16)
        a_out[layer, rows, :] = a
        for t in range(3):
            cols = slice(t * width, (t + 1) * width)
            dqkv_out[layer, rows, cols] = dot_nn(a, w_qkv[layer, :, cols]).astype(BF16)
        for b in range(blocks):
            block = pl.ds(pl.multiple_of(m * MICRO + b * LANES, LANES), LANES)
            keys_on = head_mask(count_row(m, b))
            for pair in range(HEADS // 2):
                cols = slice(pair * LANES, (pair + 1) * LANES)
                q = dqkv_out[layer, block, cols]
                k = dqkv_out[layer, block, slice(width + pair * LANES, width + (pair + 1) * LANES)]
                v = dqkv_out[layer, block, slice(2 * width + pair * LANES, 2 * width + (pair + 1) * LANES)]
                flats = compress(dot_nt(by_head(k, halves), q), masks)
                wide = []
                for h in range(2):
                    s = jnp.where(keys_on, flats[h] * score_scale, MASKED)
                    e = jnp.exp(s - jnp.max(s, axis=0, keepdims=True))
                    p = e / jnp.sum(e, axis=0, keepdims=True)
                    prob[layer, m * blocks + b, pl.ds((2 * pair + h) * 8, 8), :] = p
                    wide.append(expand(p, masks))
                mixed = dot_tn(jnp.concatenate(wide, axis=0), by_head(v, halves))
                att_out[layer, block, cols] = mixed.astype(BF16)
        need(m, layer, 4)
        res = xf + dot_nn(att_out[layer, rows, :], w_out[layer]) + shifts[layer, pl.ds(1, 1), :]
        resid[layer, rows, :] = res
        normed_two, _ = statistics(res)
        h_in = (normed_two * gains[layer, pl.ds(1, 1), :] + shifts[layer, pl.ds(2, 1), :]).astype(BF16)
        h_out[layer, rows, :] = h_in
        need(m, layer, 2, 5, 6)
        total = res + shifts[layer, pl.ds(3, 1), :]
        for t in range(tiles):
            cols = slice(t * width, (t + 1) * width)
            pre = dot_nn(h_in, w_up[layer, :, cols]) + up_bias[layer, :, cols]
            dpre_out[layer, rows, cols] = pre.astype(BF16)
            act = (pre * (0.5 * (1.0 + lax.erf(pre * ROOT_HALF)))).astype(BF16)
            total = total + dot_nn(act, w_down[layer, cols, :])
        return total.astype(BF16)

    def layer_backward(layer, m, dy):
        rows = rows_of(m)
        masks, halves = entry_masks(), half_masks()
        dyf = dy.astype(F32)
        vec_out[layer, pl.ds(5, 1), :] += column_sum(dyf)
        d_hidden = jnp.zeros((MICRO, width), F32)
        for t in range(tiles):
            cols = slice(t * width, (t + 1) * width)
            d_act = dot_nt(dy, w_down[layer, cols, :])
            pre = dpre_out[layer, rows, cols].astype(F32)
            phi = 0.5 * (1.0 + lax.erf(pre * ROOT_HALF))
            density = jnp.exp(-0.5 * pre * pre) * DENSITY_SCALE
            act_out[layer, rows, cols] = (pre * phi).astype(BF16)
            d_pre = (d_act * (phi + pre * density)).astype(BF16)
            dpre_out[layer, rows, cols] = d_pre
            upb_out[layer, :, cols] += column_sum(d_pre.astype(F32))
            d_hidden = d_hidden + dot_nt(d_pre, w_up[layer, :, cols])
        normed_two, inverse_two = statistics(resid[layer, rows, :])
        vec_out[layer, pl.ds(1, 1), :] += column_sum(d_hidden * normed_two)
        vec_out[layer, pl.ds(4, 1), :] += column_sum(d_hidden)
        d_resid = dyf + norm_backward(d_hidden * gains[layer, pl.ds(1, 1), :], normed_two, inverse_two)
        d_branch = d_resid.astype(BF16)
        dbr_out[layer, rows, :] = d_branch
        vec_out[layer, pl.ds(3, 1), :] += column_sum(d_branch.astype(F32))
        d_att = dot_nt(d_branch, w_out[layer]).astype(BF16)
        for b in range(blocks):
            block = pl.ds(pl.multiple_of(m * MICRO + b * LANES, LANES), LANES)
            for pair in range(HEADS // 2):
                c_q = slice(pair * LANES, (pair + 1) * LANES)
                c_k = slice(width + pair * LANES, width + (pair + 1) * LANES)
                c_v = slice(2 * width + pair * LANES, 2 * width + (pair + 1) * LANES)
                q = dqkv_out[layer, block, c_q]
                k = dqkv_out[layer, block, c_k]
                v = dqkv_out[layer, block, c_v]
                da = d_att[b * LANES:(b + 1) * LANES, c_q]
                flats = compress(dot_nt(by_head(v, halves), da), masks)
                wide_p, wide_s = [], []
                for h in range(2):
                    p = prob[layer, m * blocks + b, pl.ds((2 * pair + h) * 8, 8), :]
                    ds = p * (flats[h] - jnp.sum(flats[h] * p, axis=0, keepdims=True))
                    wide_p.append(expand(p, masks))
                    wide_s.append(expand(ds, masks))
                d_v = dot_nn(jnp.concatenate(wide_p, axis=1), by_head(da, halves))
                d_k = dot_nn(jnp.concatenate(wide_s, axis=1), by_head(q, halves)) * score_scale
                d_q = dot_tn(jnp.concatenate(wide_s, axis=0), by_head(k, halves)) * score_scale
                dqkv_out[layer, block, c_q] = d_q.astype(BF16)
                dqkv_out[layer, block, c_k] = d_k.astype(BF16)
                dqkv_out[layer, block, c_v] = d_v.astype(BF16)
        d_a = jnp.zeros((MICRO, width), F32)
        for t in range(3):
            cols = slice(t * width, (t + 1) * width)
            d_a = d_a + dot_nt(dqkv_out[layer, rows, cols], w_qkv[layer, :, cols])
        x = jnp.where(layer == 0, x_in[rows, :], x_mid[rows, :])
        normed, inverse = statistics(x.astype(F32))
        vec_out[layer, pl.ds(0, 1), :] += column_sum(d_a * normed)
        vec_out[layer, pl.ds(2, 1), :] += column_sum(d_a)
        dx = d_resid + norm_backward(d_a * gains[layer, pl.ds(0, 1), :], normed, inverse)
        return dx.astype(BF16)

    @pl.when(stage == 0)
    def _():
        x_in[...] = x0[...]

    def forward_step(m, carry):
        rows = rows_of(m)

        @pl.when(stage == 1)
        def _():
            forward_copy(m).wait_recv()

        x = lax.fori_loop(0, 2, lambda layer, x: forward_layer(layer, m, x), x_in[rows, :])
        y_out[rows, :] = x

        @pl.when(stage == 0)
        def _():
            forward_copy(m).start()

        @pl.when(stage == 1)
        def _():
            for b in range(blocks):
                matrix = pool_matrix(count_row(m, b))
                summed = dot_nn(matrix.astype(BF16), x[b * LANES:(b + 1) * LANES, :])
                mean = summed / jnp.sum(matrix, axis=1, keepdims=True)
                entries = pl.ds(pl.multiple_of((m * blocks + b) * (LANES // 8), LANES // 8), LANES // 8)
                pooled_out[entries, :] = mean.astype(BF16)
        return carry

    def forward_layer(layer, m, x):
        @pl.when(layer == 1)
        def _():
            x_mid[rows_of(m), :] = x

        return layer_forward(layer, m, x)

    lax.fori_loop(0, micros, forward_step, 0)

    @pl.when(stage == 0)
    def _():
        for m in range(micros):
            forward_copy(m).wait_send()

    def backward_step(m, carry):
        rows = rows_of(m)

        @pl.when(stage == 0)
        def _():
            backward_copy(m).wait_recv()
            dy_out[1, rows, :] = dy_in[rows, :]

        @pl.when(stage == 1)
        def _():
            for b in range(blocks):
                matrix = pool_matrix(count_row(m, b))
                entries = pl.ds(pl.multiple_of((m * blocks + b) * (LANES // 8), LANES // 8), LANES // 8)
                share = (pool_grad[entries, :] / jnp.sum(matrix, axis=1, keepdims=True)).astype(BF16)
                block = pl.ds(pl.multiple_of(m * MICRO + b * LANES, LANES), LANES)
                dy_out[1, block, :] = dot_tn(matrix.astype(BF16), share).astype(BF16)

        def step(i, dy):
            layer = 1 - i

            @pl.when(i == 1)
            def _():
                dy_out[0, rows, :] = dy

            return layer_backward(layer, m, dy)

        dx = lax.fori_loop(0, 2, step, dy_out[1, rows, :])
        dx_out[rows, :] = dx

        @pl.when(stage == 1)
        def _():
            y_out[rows, :] = dx
            backward_copy(m).start()
        return carry

    lax.fori_loop(0, micros, backward_step, 0)

    @pl.when(stage == 1)
    def _():
        for m in range(micros):
            backward_copy(m).wait_send()


def trunk(x0, counts, pool_grad, own, theirs):
    rows, width = x0.shape
    hidden = own[5].shape[2]
    micros = rows // MICRO
    vmem = pl.BlockSpec(memory_space=pltpu.VMEM)
    shape = jax.ShapeDtypeStruct
    outs = [
        shape((2, rows, width), BF16), shape((2, rows, 3 * width), BF16), shape((2, rows, width), BF16),
        shape((2, rows, width), BF16), shape((2, rows, width), BF16), shape((2, rows, hidden), BF16),
        shape((2, rows, hidden), BF16), shape((2, rows, width), BF16), shape((rows, width), BF16),
        shape((rows // 8, width), BF16), shape((2, 8, width), F32), shape((2, 1, hidden), F32),
    ]
    return pl.pallas_call(
        functools.partial(trunk_kernel, micros, width, hidden),
        out_shape=outs,
        in_specs=[vmem] * 3 + [pl.BlockSpec(memory_space=pl.ANY)] * 14,
        out_specs=[vmem] * len(outs),
        scratch_shapes=[pltpu.VMEM((2,) + p.shape[1:], p.dtype) for p in own] + [
            pltpu.VMEM((rows, width), BF16), pltpu.VMEM((rows, width), BF16), pltpu.VMEM((2, rows, width), F32),
            pltpu.VMEM((2, rows // LANES, 8 * HEADS, LANES), F32), pltpu.VMEM((rows, width), BF16),
            pltpu.VMEM((rows, width), BF16),
        ] + [pltpu.SemaphoreType.DMA((micros,))] * 4 + [pltpu.SemaphoreType.DMA((7, 2))],
        compiler_params=pltpu.CompilerParams(collective_id=1, has_side_effects=True, vmem_limit_bytes=VMEM_BYTES),
    )(x0, counts, pool_grad, *own, *theirs)


def capacity_of(slots, owners):
    return max(16, -(-2 * slots // owners // 16) * 16)


def ones_where(condition):
    return jnp.where(condition, 1.0, 0.0).astype(BF16)


def iota(shape, axis):
    return lax.broadcasted_iota(jnp.int32, shape, axis)


def positions(used, chunks):
    rows = LANES
    through = ones_where(iota((LANES, LANES), 0) <= iota((LANES, LANES), 1))
    above = ones_where(
        (iota((rows, rows), 0) // 8 == iota((rows, rows), 1) // 8) & (iota((rows, rows), 1) < iota((rows, rows), 0)))
    every = jnp.ones((LANES, LANES), BF16)
    out = []
    for chunk in range(chunks):
        part = used[chunk * rows:(chunk + 1) * rows, :].astype(BF16)
        before = dot_nn(dot_nn(above, part).astype(BF16), every)
        out.append(dot_nn(part, through) + before)
    return jnp.concatenate(out, axis=0)


def in_round(place, used, turn, capacity):
    place = place - (turn * capacity).astype(F32)
    return jnp.where((used > 0) & (place >= 1) & (place <= capacity), place, 0.0)


def owner_plan(ids_all, picks, used_rows, base, span, turn, capacity, lists):
    slots = ids_all.shape[2]
    blocks = -(-span // LANES)

    def count(d, carry):
        rel = ids_all[d // 2, pl.ds(lax.rem(d, 2), 1), :] - base
        high = jnp.where((rel >= 0) & (rel < span), rel >> 7, -1)
        counts = dot_nt(ones_where(iota((8, slots), 0) == high), ones_where(iota((LANES, slots), 0) == (rel & 127)))
        used_rows[pl.ds(pl.multiple_of(d * 8, 8), 8), :] = jnp.where(counts > 0, 1.0, 0.0)
        return carry

    lax.fori_loop(0, lists, count, 0)
    used = used_rows[pl.ds(0, lists * 8), :]
    used_rows[pl.ds(0, lists * 8), :] = in_round(positions(used, lists * 8 // LANES), used, turn, capacity)

    def spread(d, carry):
        place = used_rows[pl.ds(pl.multiple_of(d * 8, 8), 8), :]
        wanted = (iota((capacity, LANES), 0) + 1).astype(F32)
        for block in range(blocks):
            picks[pl.ds(pl.multiple_of(d * capacity, 16), capacity), block * LANES:(block + 1) * LANES] = ones_where(
                place[block:block + 1, :] == wanted)
        return carry

    lax.fori_loop(0, lists, spread, 0)


def slot_codes(ids_row, span):
    value = ids_row.astype(F32)
    owner = jnp.floor((value + 0.5) * (1.0 / span))
    rel = value - owner * span
    high = jnp.floor(rel * (1.0 / LANES))
    return owner, owner * 8 + high, rel - high * LANES


def owner_counts(ids_row, span, owners):
    slots = ids_row.shape[1]
    owner, row, lane = slot_codes(ids_row, span)
    rows = ones_where(iota((owners * 8, slots), 0).astype(F32) == row)
    lanes = ones_where(iota((LANES, slots), 0).astype(F32) == lane)
    return owner, rows, lanes, jnp.where(dot_nt(rows, lanes) > 0, 1.0, 0.0)


def slot_plan(ids_row, match, span, owners, turn, capacity):
    slots = ids_row.shape[1]
    owner, rows, lanes, used = owner_counts(ids_row, span, owners)
    place = in_round(positions(used, owners * 8 // LANES), used, turn, capacity)
    mine = jnp.sum(dot_tn(place.astype(BF16), rows) * lanes.astype(F32), axis=0, keepdims=True)
    target = jnp.where(mine > 0, owner * capacity + mine - 1, -1.0)
    for owner_at in range(0, owners, 4):
        index = (iota((4 * capacity, slots), 0) + owner_at * capacity).astype(F32)
        match[owner_at * capacity:(owner_at + 4) * capacity, :] = ones_where(index == target)


def most_distinct(ids_all, span, owners, lists):
    def one(d, most):
        _, _, _, used = owner_counts(ids_all[d // 2, pl.ds(lax.rem(d, 2), 1), :], span, owners)
        per_row = jnp.sum(used, axis=1, keepdims=True)
        per_owner = jnp.sum(per_row.reshape(owners, 8, 1), axis=1)
        return jnp.maximum(most, jnp.max(per_owner))

    return lax.fori_loop(0, lists, one, jnp.float32(0))


def device_at(index, columns):
    return (index // columns, lax.rem(index, columns))


def remote(src, dst, send, recv, peer):
    return pltpu.make_async_remote_copy(src, dst, send, recv, device_id=peer, device_id_type=MESH)


def lookup_rounds(columns, me, packed, landed, send, recv):
    lists, owners = 2 * columns, 4 * columns

    def target(d):
        return lax.rem(d, 2) * columns + d // 2

    def copy(d):
        return remote(packed.at[d], landed.at[me], send.at[d], recv.at[me], device_at(target(d), columns))

    def start(i, carry):
        d = lax.rem(i + 2 * lax.rem(me, columns), lists)

        @pl.when(target(d) != me)
        def _():
            copy(d).start()

        @pl.when(target(d) == me)
        def _():
            landed[me] = packed[d]
        return carry

    def arrive(o, carry):
        @pl.when(o != me)
        def _():
            remote(packed.at[0], landed.at[o], send.at[0], recv.at[o], device_at(o, columns)).wait_recv()
        return carry

    def left(d, carry):
        @pl.when(target(d) != me)
        def _():
            copy(d).wait_send()
        return carry

    return (lambda: lax.fori_loop(0, lists, start, 0), lambda: lax.fori_loop(0, owners, arrive, 0),
            lambda: lax.fori_loop(0, lists, left, 0))


def return_rounds(columns, me, parts, landed, send, recv):
    lists, owners = 2 * columns, 4 * columns
    slot = lax.rem(me, columns) * 2 + me // columns

    def copy(o):
        return remote(parts.at[o], landed.at[slot], send.at[o], recv.at[slot], device_at(o, columns))

    def start(i, carry):
        o = lax.rem(i + me, owners)

        @pl.when(o != me)
        def _():
            copy(o).start()

        @pl.when(o == me)
        def _():
            landed[slot] = parts[me]
        return carry

    def arrive(d, carry):
        source = lax.rem(d, 2) * columns + d // 2

        @pl.when(source != me)
        def _():
            remote(parts.at[0], landed.at[d], send.at[0], recv.at[d], device_at(source, columns)).wait_recv()
        return carry

    def left(o, carry):
        @pl.when(o != me)
        def _():
            copy(o).wait_send()
        return carry

    return (lambda: lax.fori_loop(0, owners, start, 0), lambda: lax.fori_loop(0, lists, arrive, 0),
            lambda: lax.fori_loop(0, owners, left, 0))


def greet_all(columns, me, others):
    barrier = pltpu.get_barrier_semaphore()

    def greet(o, carry):
        @pl.when(o != me)
        def _():
            pl.semaphore_signal(barrier, inc=1, device_id=device_at(o, columns), device_id_type=MESH)
        return carry

    lax.fori_loop(0, others, greet, 0)
    return barrier


def pack_rows(table, padded, picks, packed, span, capacity, lists):
    padded[pl.ds(0, span), :] = table[...]
    for d in range(0, lists, 4):
        rows = dot_nn(picks[d * capacity:(d + 4) * capacity, :], padded[...]).astype(BF16)
        packed[d:d + 4] = rows.reshape(4, capacity, rows.shape[1])


def lookup_kernel(
    columns, capacity,
    ids, table, cot_in, proj, vocab, gain_in, shift_in, bias_in, qkv_in, out_in, up_in, down_in,
    x_out, match, picks, ids_all, most_out, pool_out, gain_all, shift_all, bias_all, qkv_all, out_all, up_all, down_all,
    used_rows, padded, packed, landed, pool_send, pool_parts,
    i_send, i_recv, t_send, t_recv, w_send, w_recv, g_send, g_recv,
):
    section = lax.axis_index("section")
    column = lax.axis_index("dp")
    core = lax.rem(section, 2)
    me = section * columns + column
    owners, lists = 4 * columns, 2 * columns
    span, width = table.shape
    entries = cot_in.shape[0]
    core_peer = (section + 1 - 2 * core, column)
    barrier = greet_all(columns, me, owners)
    ids_all[column] = ids[...]
    padded[...] = jnp.zeros_like(padded)
    pl.semaphore_wait(barrier, owners - 1)

    def ids_copy(d):
        return remote(ids, ids_all.at[column], i_send.at[d - 1], i_recv.at[column],
                      (section, lax.rem(column + d, columns)))

    for d in range(1, columns):
        ids_copy(d).start()
    pairs = ((gain_in, gain_all), (shift_in, shift_all), (bias_in, bias_all),
             (qkv_in, qkv_all), (out_in, out_all), (up_in, up_all), (down_in, down_all))
    weight_copies = [
        remote(src, dst, w_send.at[i], w_recv.at[i], core_peer) for i, (src, dst) in enumerate(pairs)]
    for copy in weight_copies:
        copy.start()

    position = column * entries + iota((entries, cot_in.shape[1]), 0)
    cot = jnp.where(position < vocab[0], cot_in[...].astype(F32), 0.0).astype(BF16)
    part = dot_nt(cot, proj[...]).astype(BF16)
    pool_send[...] = part.reshape(2, entries // 2, width)

    def pool_copy(k):
        return remote(pool_send.at[k], pool_parts.at[section], g_send.at[k], g_recv.at[section], (2 + k, column))

    for k in range(2):
        @pl.when(section != 2 + k)
        def _(k=k):
            pool_copy(k).start()

        @pl.when(section == 2 + k)
        def _(k=k):
            pool_parts[section] = pool_send[k]

    for d in range(1, columns):
        source = lax.rem(column + d, columns)
        remote(ids, ids_all.at[source], i_send.at[d - 1], i_recv.at[source], (section, source)).wait_recv()
    turn = jnp.int32(0)
    owner_plan(ids_all, picks, used_rows, me * span, span, turn, capacity, lists)
    pack_rows(table, padded, picks, packed, span, capacity, lists)
    start, arrive, left = lookup_rounds(columns, me, packed, landed, t_send, t_recv)
    start()

    @pl.when(section < 2)
    def _():
        slot_plan(ids_all[column, pl.ds(core, 1), :], match, span, owners, turn, capacity)

    most_out[...] = jnp.full(most_out.shape, most_distinct(ids_all, span, owners, lists), F32)

    @pl.when(section >= 2)
    def _():
        total = pool_parts[section].astype(F32)
        for d in range(1, 4):
            source = lax.rem(section + d, 4)
            remote(pool_send.at[0], pool_parts.at[source], g_send.at[0], g_recv.at[source],
                   (source, column)).wait_recv()
            total = total + pool_parts[source].astype(F32)
        pool_out[...] = total

    @pl.when(section < 2)
    def _():
        arrive()
        x_out[...] = dot_tn(match[...], landed[...].reshape(owners * capacity, width)).astype(BF16)

    left()
    for k in range(2):
        @pl.when(section != 2 + k)
        def _(k=k):
            pool_copy(k).wait_send()
    for d in range(1, columns):
        ids_copy(d).wait_send()
    for copy in weight_copies:
        copy.wait()


def lookup(columns, ids, table, cot, proj, vocab, gain, shift, bias, w_qkv, w_out, w_up, w_down):
    slots = ids.shape[1]
    span, width = table.shape
    owners, lists = 4 * columns, 2 * columns
    capacity = capacity_of(slots, owners)
    padded_span = -(-span // LANES) * LANES
    entries = cot.shape[0]
    vmem = pl.BlockSpec(memory_space=pltpu.VMEM)
    smem = pl.BlockSpec(memory_space=pltpu.SMEM)
    hbm = pl.BlockSpec(memory_space=pl.ANY)
    shape = jax.ShapeDtypeStruct
    params = (gain, shift, bias, w_qkv, w_out, w_up, w_down)
    outs = [
        shape((slots, width), BF16), shape((owners * capacity, slots), BF16),
        shape((lists * capacity, padded_span), BF16), shape((columns, 2, slots), jnp.int32), shape((8, LANES), F32),
        shape((entries // 2, width), F32),
    ] + [shape(p.shape, p.dtype) for p in params]
    sem = pltpu.SemaphoreType.DMA
    return pl.pallas_call(
        functools.partial(lookup_kernel, columns, capacity),
        out_shape=outs,
        in_specs=[vmem] * 4 + [smem] + [hbm] * 7,
        out_specs=[vmem] * 6 + [hbm] * 7,
        scratch_shapes=[
            pltpu.VMEM((max(lists, owners) * 8, LANES), F32), pltpu.VMEM((padded_span, width), BF16),
            pltpu.VMEM((lists, capacity, width), BF16), pltpu.VMEM((owners, capacity, width), BF16),
            pltpu.VMEM((2, entries // 2, width), BF16), pltpu.VMEM((4, entries // 2, width), BF16),
            sem((columns - 1,)), sem((columns,)), sem((lists,)), sem((owners,)), sem((7,)), sem((7,)),
            sem((2,)), sem((4,)),
        ],
        compiler_params=pltpu.CompilerParams(collective_id=3, has_side_effects=True, vmem_limit_bytes=VMEM_BYTES),
    )(ids, table, cot, proj, vocab, *params)


def more_lookup_kernel(columns, capacity, turn, ids_all, table, x_out, match, picks, used_rows, padded, packed, landed,
                       t_send, t_recv):
    section = lax.axis_index("section")
    column = lax.axis_index("dp")
    me = section * columns + column
    owners, lists = 4 * columns, 2 * columns
    span, width = table.shape
    barrier = pltpu.get_barrier_semaphore()

    @pl.when(section < 2)
    def _():
        greet_all(columns, me, owners)
        pl.semaphore_wait(barrier, lists - 1)

    @pl.when(section >= 2)
    def _():
        pl.semaphore_wait(barrier, lists)

    padded[...] = jnp.zeros_like(padded)
    owner_plan(ids_all, picks, used_rows, me * span, span, turn[0], capacity, lists)
    pack_rows(table, padded, picks, packed, span, capacity, lists)
    start, arrive, left = lookup_rounds(columns, me, packed, landed, t_send, t_recv)
    start()
    x_out[...] = jnp.zeros_like(x_out)

    @pl.when(section < 2)
    def _():
        slot_plan(ids_all[column, pl.ds(lax.rem(section, 2), 1), :], match, span, owners, turn[0], capacity)
        arrive()
        x_out[...] = dot_tn(match[...], landed[...].reshape(owners * capacity, width)).astype(BF16)

    left()


def more_lookup(columns, turn, ids_all, table):
    slots = ids_all.shape[2]
    span, width = table.shape
    owners, lists = 4 * columns, 2 * columns
    capacity = capacity_of(slots, owners)
    padded_span = -(-span // LANES) * LANES
    vmem = pl.BlockSpec(memory_space=pltpu.VMEM)
    sem = pltpu.SemaphoreType.DMA
    return pl.pallas_call(
        functools.partial(more_lookup_kernel, columns, capacity),
        out_shape=jax.ShapeDtypeStruct((slots, width), BF16),
        in_specs=[pl.BlockSpec(memory_space=pltpu.SMEM), vmem, vmem],
        out_specs=vmem,
        scratch_shapes=[
            pltpu.VMEM((owners * capacity, slots), BF16), pltpu.VMEM((lists * capacity, padded_span), BF16),
            pltpu.VMEM((max(lists, owners) * 8, LANES), F32), pltpu.VMEM((padded_span, width), BF16),
            pltpu.VMEM((lists, capacity, width), BF16), pltpu.VMEM((owners, capacity, width), BF16),
            sem((lists,)), sem((owners,)),
        ],
        compiler_params=pltpu.CompilerParams(collective_id=4, has_side_effects=True, vmem_limit_bytes=VMEM_BYTES),
    )(turn, ids_all, table)


def return_parts(match, dx, parts, owners, capacity):
    for o in range(0, owners, 4):
        rows = dot_nn(match[o * capacity:(o + 4) * capacity, :], dx[...]).astype(BF16)
        parts[o:o + 4] = rows.reshape(4, capacity, rows.shape[1])


def more_return_kernel(columns, capacity, turn, ids_all, dx, held, grad_out, match, picks, used_rows, parts, landed,
                       t_send, t_recv):
    section = lax.axis_index("section")
    column = lax.axis_index("dp")
    me = section * columns + column
    owners, lists = 4 * columns, 2 * columns
    span, width = held.shape
    slots = ids_all.shape[2]
    barrier = greet_all(columns, me, lists)

    @pl.when(section < 2)
    def _():
        pl.semaphore_wait(barrier, owners - 1)

    start, arrive, left = return_rounds(columns, me, parts, landed, t_send, t_recv)

    @pl.when(section < 2)
    def _():
        slot_plan(ids_all[column, pl.ds(lax.rem(section, 2), 1), :], match, span, owners, turn[0], capacity)
        return_parts(match, dx, parts, owners, capacity)
        start()

    owner_plan(ids_all, picks, used_rows, me * span, span, turn[0], capacity, lists)
    arrive()
    grad = dot_tn(picks[...], landed[...].reshape(lists * capacity, width))
    grad_out[...] = held[...] + grad[:span]

    @pl.when(section < 2)
    def _():
        left()


def more_return(columns, turn, ids_all, dx, held):
    slots = ids_all.shape[2]
    span, width = held.shape
    owners, lists = 4 * columns, 2 * columns
    capacity = capacity_of(slots, owners)
    padded_span = -(-span // LANES) * LANES
    vmem = pl.BlockSpec(memory_space=pltpu.VMEM)
    sem = pltpu.SemaphoreType.DMA
    return pl.pallas_call(
        functools.partial(more_return_kernel, columns, capacity),
        out_shape=jax.ShapeDtypeStruct((span, width), F32),
        in_specs=[pl.BlockSpec(memory_space=pltpu.SMEM), vmem, vmem, vmem],
        out_specs=vmem,
        scratch_shapes=[
            pltpu.VMEM((owners * capacity, slots), BF16), pltpu.VMEM((lists * capacity, padded_span), BF16),
            pltpu.VMEM((max(lists, owners) * 8, LANES), F32),
            pltpu.VMEM((owners, capacity, width), BF16), pltpu.VMEM((lists, capacity, width), BF16),
            sem((owners,)), sem((lists,)),
        ],
        compiler_params=pltpu.CompilerParams(collective_id=5, has_side_effects=True, vmem_limit_bytes=VMEM_BYTES),
    )(turn, ids_all, dx, held)


LAG_X = 2
LAG_Z = 4
TABLE_STEP = 9


def reduce_kernel(
    columns, width, hidden,
    a, dqkv, att, dbr, h_in, dpre, act, dy, vec, upb, pooled, cot_in, proj, dx, match, picks, vocab,
    emb_out, gain_out, shift_out, upb_out, qkv_out, out_out, up_out, down_out, proj_out, table_out,
    s0_send, s0_recv, sums, s1_recv, z_recv, v_buf, pool_all, cot, parts, landed,
    c_send, c_recv, x_send, x_recv, zs_send, zs_recv, v_send, v_recv, p_send, p_recv, t_send, t_recv,
):
    section = lax.axis_index("section")
    column = lax.axis_index("dp")
    core = lax.rem(section, 2)
    depth = columns // 2
    side, place = lax.rem(column, 2), column // 2
    piece = width // columns
    tiles = hidden // width
    units = 3 + 1 + tiles + tiles
    core_peer = (section + 1 - 2 * core, column)
    side_peer = (section, column + 1 - 2 * side)

    def place_at(d):
        return lax.rem(place + d, depth)

    def place_peer(d):
        return (section, place_at(d) * 2 + side)

    def section_peer(d):
        return (lax.rem(section + d, 4), column)

    owners, lists = 4 * columns, 2 * columns
    capacity = parts.shape[1]
    me = section * columns + column
    barrier = greet_all(columns, me, owners)
    pl.semaphore_wait(barrier, owners - 1)
    start, arrive, left = return_rounds(columns, me, parts, landed, t_send, t_recv)

    @pl.when(section < 2)
    def _():
        return_parts(match, dx, parts, owners, capacity)
        start()

    def pool_copy(d):
        return remote(pooled, pool_all.at[core], p_send.at[d - 1], p_recv.at[core], section_peer(d))

    def pool_arrival(k):
        return remote(pooled, pool_all.at[k], p_send.at[0], p_recv.at[k], core_peer)

    @pl.when(section >= 2)
    def _():
        for d in range(1, 4):
            pool_copy(d).start()
        pool_all[core] = pooled[...]

    def vec_copy(slot, peer, index):
        return remote(v_buf.at[slot], v_buf.at[index], v_send.at[index], v_recv.at[index], peer)

    def vec_of(layer):
        return vec[layer], upb[layer]

    def put_vec(slot, layer):
        rows, bias = vec_of(layer)
        v_buf[slot, :, slice(0, width)] = rows
        for t in range(2):
            v_buf[slot, pl.ds(6 + t, 1), :] = bias[:, t * (hidden // 2):(t + 1) * (hidden // 2)]

    put_vec(0, 1 - core)
    vec_copy(0, core_peer, 2).start()
    put_vec(1, core)

    def core_copy(u):
        return remote(s0_send.at[u], s0_recv.at[u], c_send.at[u], c_recv.at[u], core_peer)

    def side_copy(u):
        return remote(sums.at[u, 1 - side], s1_recv.at[u], x_send.at[u], x_recv.at[u], side_peer)

    def place_copy(u, d):
        return remote(s1_recv.at[u, place_at(d)], z_recv.at[u, d - 1], zs_send.at[u, d - 1], zs_recv.at[u, d - 1],
                      place_peer(d))

    def cut(value, q):
        return value[q * piece:(q + 1) * piece, :]

    def product(layer, u):
        if u < 3:
            return dot_tn(a[layer], dqkv[layer, :, u * width:(u + 1) * width])
        if u == 3:
            return dot_tn(att[layer], dbr[layer])
        t = u - 4
        return dot_tn(h_in[layer], dpre[layer, :, t * width:(t + 1) * width])

    def send_other(u):
        value = product(1 - core, u).astype(BF16)
        for q in range(columns):
            s0_send[u, q % 2, q // 2] = cut(value, q)
        core_copy(u).start()

    def add_own(u):
        value = product(core, u)
        core_copy(u).wait_recv()
        for q in range(columns):
            sums[u, q % 2, q // 2] = (cut(value, q) + s0_recv[u, q % 2, q // 2].astype(F32)).astype(BF16)

    first_down = 4 + tiles

    def down_product(layer, i):
        return dot_tn(act[layer, :, i * width:(i + 1) * width], dy[layer])

    def down_parts(i):
        for j in range(columns):
            yield j, first_down + j % tiles, i * columns // tiles + j // tiles

    def down_other():
        for i in range(tiles):
            value = down_product(1 - core, i).astype(BF16)
            for j, u, q in down_parts(i):
                s0_send[u, q % 2, q // 2] = cut(value, j)
        for u in range(first_down, units):
            core_copy(u).start()

    def down_own():
        for i in range(tiles):
            value = down_product(core, i)
            if i == 0:
                for u in range(first_down, units):
                    core_copy(u).wait_recv()
            for j, u, q in down_parts(i):
                sums[u, q % 2, q // 2] = (cut(value, j) + s0_recv[u, q % 2, q // 2].astype(F32)).astype(BF16)

    def project():
        @pl.when(section >= 2)
        def _():
            pool_arrival(1 - core).wait_recv()

        @pl.when(section < 2)
        def _():
            pool_arrival(0).wait_recv()
            pool_arrival(1).wait_recv()

        entries = cot_in.shape[0]
        position = column * entries + lax.broadcasted_iota(jnp.int32, (entries, width), 0)
        live = position < vocab[0]
        cot[...] = jnp.where(live, cot_in[...].astype(F32), 0.0).astype(BF16)
        rows = pool_all[...].reshape(entries, width)
        emb_out[...] = jnp.where(live, dot_nn(rows, proj[...]), 0.0)
        value = dot_tn(rows, cot[...]).astype(BF16)
        for q in range(columns):
            sums[units, q % 2, q // 2] = cut(value, q)

    def middle(u):
        side_copy(u).wait_recv()
        s1_recv[u] = (s1_recv[u].astype(F32) + sums[u, side].astype(F32)).astype(BF16)
        for d in range(1, depth):
            place_copy(u, d).start()

    def finish(u):
        total = s1_recv[u, place].astype(F32)
        for d in range(1, depth):
            place_copy(u, d).wait_recv()
            total = total + z_recv[u, d - 1].astype(F32)
        if u < 3:
            qkv_out[0, :, u * width:(u + 1) * width] = total
        elif u == 3:
            out_out[0] = total
        elif u < first_down:
            up_out[0, :, (u - 4) * width:(u - 3) * width] = total
        elif u < units:
            t = u - first_down
            down_out[0, t * piece:(t + 1) * piece, :] = total
        else:
            proj_out[...] = total

    def vec_step(k):
        if k == 0:
            vec_copy(0, core_peer, 2).wait_recv()
            v_buf[1] = v_buf[1] + v_buf[2]
            vec_copy(1, side_peer, 3).start()
        if k == 1:
            vec_copy(1, side_peer, 3).wait_recv()
            v_buf[4] = v_buf[1] + v_buf[3]
            for d in range(1, depth):
                vec_copy(4, place_peer(d), 4 + d).start()
        if k == 2:
            total = v_buf[4]
            for d in range(1, depth):
                vec_copy(4, place_peer(d), 4 + d).wait_recv()
                total = total + v_buf[4 + d]
            lanes = width // columns
            share = hidden // columns
            for q in range(columns):
                @pl.when(column == q)
                def _(q=q):
                    gain_out[0] = total[0:2, q * lanes:(q + 1) * lanes]
                    shift_out[0] = total[2:6, q * lanes:(q + 1) * lanes]
                    row, start = divmod(q * share, hidden // 2)
                    upb_out[...] = total[6 + row:7 + row, start:start + share]

    for step in range(units + 1 + LAG_Z):
        if step < first_down:
            send_other(step)
            add_own(step)
        elif step == first_down:
            down_other()
            down_own()
        elif step == units:
            project()
        if step <= units:
            side_copy(step).start()
        if step == TABLE_STEP:
            arrive()
            grad = dot_tn(picks[...], landed[...].reshape(lists * capacity, width))
            table_out[...] = grad[:table_out.shape[0]]
        if step in (1, 3, 5):
            vec_step((step - 1) // 2)
        if 0 <= step - LAG_X <= units:
            middle(step - LAG_X)
        if 0 <= step - LAG_Z <= units:
            finish(step - LAG_Z)

    @pl.when(section < 2)
    def _():
        left()

    vec_copy(0, core_peer, 2).wait_send()
    vec_copy(1, side_peer, 3).wait_send()
    for d in range(1, depth):
        vec_copy(4, place_peer(d), 4 + d).wait_send()
    for u in range(units):
        core_copy(u).wait_send()
    for u in range(units + 1):
        side_copy(u).wait_send()
        for d in range(1, depth):
            place_copy(u, d).wait_send()

    @pl.when(section >= 2)
    def _():
        for d in range(1, 4):
            pool_copy(d).wait_send()


def reduce_all(columns, a, dqkv, att, dbr, h_in, dpre, act, dy, vec, upb, pooled, cot, proj, dx, match, picks, span, vocab):
    width, hidden = a.shape[2], dpre.shape[2]
    entries, out_width = cot.shape
    piece, depth, tiles = width // columns, columns // 2, hidden // width
    units = 4 + 2 * tiles
    capacity = match.shape[0] // (4 * columns)
    vmem = pl.BlockSpec(memory_space=pltpu.VMEM)
    smem = pl.BlockSpec(memory_space=pltpu.SMEM)
    shape = jax.ShapeDtypeStruct
    outs = [
        shape((entries, out_width), F32), shape((1, 2, piece), F32), shape((1, 4, piece), F32),
        shape((1, hidden // columns), F32), shape((1, piece, 3 * width), F32), shape((1, piece, width), F32),
        shape((1, piece, hidden), F32), shape((1, tiles * piece, width), F32), shape((piece, out_width), F32),
        shape((span, width), F32),
    ]
    sem = pltpu.SemaphoreType.DMA
    return pl.pallas_call(
        functools.partial(reduce_kernel, columns, width, hidden),
        out_shape=outs,
        in_specs=[vmem] * 16 + [smem],
        out_specs=[vmem] * len(outs),
        scratch_shapes=[
            pltpu.VMEM((units, 2, depth, piece, width), BF16), pltpu.VMEM((units, 2, depth, piece, width), BF16),
            pltpu.VMEM((units + 1, 2, depth, piece, width), BF16), pltpu.VMEM((units + 1, depth, piece, width), BF16),
            pltpu.VMEM((units + 1, depth - 1, piece, width), BF16), pltpu.VMEM((4 + depth, 8, hidden // 2), F32),
            pltpu.VMEM((2, entries // 2, width), BF16), pltpu.VMEM((entries, out_width), BF16),
            pltpu.VMEM((4 * columns, capacity, width), BF16), pltpu.VMEM((2 * columns, capacity, width), BF16),
            sem((units,)), sem((units,)), sem((units + 1,)), sem((units + 1,)),
            sem((units + 1, depth - 1)), sem((units + 1, depth - 1)), sem((4 + depth,)), sem((4 + depth,)),
            sem((3,)), sem((2,)), sem((4 * columns,)), sem((2 * columns,)),
        ],
        compiler_params=pltpu.CompilerParams(collective_id=2, has_side_effects=True, vmem_limit_bytes=VMEM_BYTES),
    )(a, dqkv, att, dbr, h_in, dpre, act, dy, vec, upb, pooled, cot, proj, dx, match, picks, vocab)


def local(table, piece_ids, piece_counts, vocab_size, norm_gain, shift_bias, up_bias, qkv_weight, out_weight,
          up_weight, down_weight, proj_weight, embed_cotangent):
    section = lax.axis_index("section")
    columns = lax.axis_size("dp")
    core = lax.rem(section, 2)
    entries, pieces = piece_ids.shape
    half = entries // 2
    ids = piece_ids.reshape(2, half * pieces)
    my_counts = lax.dynamic_slice_in_dim(piece_counts, core * half, half, 0)
    count_rows = jnp.repeat(my_counts, pieces).reshape(-1, LANES)
    own = (norm_gain, shift_bias, up_bias[:, None, :], qkv_weight, out_weight, up_weight, down_weight)
    x0, match, picks, ids_all, most, pool_grad, *theirs = lookup(
        columns, ids, table, embed_cotangent, proj_weight, vocab_size, *own)
    capacity = match.shape[0] // (4 * columns)
    turns = (most[0, 0].astype(jnp.int32) + capacity - 1) // capacity
    x0 = lax.fori_loop(
        1, turns, lambda turn, x: x + more_lookup(columns, turn.reshape(1), ids_all, table), x0)
    a, dqkv, att, dbr, h, dpre, act, dy, dx, pooled, vec, upb = trunk(
        x0, count_rows, pool_grad, own, theirs)
    emb, g_gain, g_shift, g_bias, g_qkv, g_out, g_up, g_down, g_proj, g_table = reduce_all(
        columns, a, dqkv, att, dbr, h, dpre, act, dy, vec, upb, pooled, embed_cotangent, proj_weight, dx, match, picks,
        table.shape[0], vocab_size)
    g_table = lax.fori_loop(
        1, turns, lambda turn, held: more_return(columns, turn.reshape(1), ids_all, dx, held), g_table)
    return emb, g_table, g_gain, g_shift, g_bias, g_qkv, g_out, g_up, g_down, g_proj


def solution(mesh):
    return jax.shard_map(
        local,
        mesh=mesh,
        in_specs=(
            P(("section", "dp"), None), P("dp", None), P("dp"), P(), P("section", None, None),
            P("section", None, None), P("section", None), P("section", None, None), P("section", None, None),
            P("section", None, None), P("section", None, None), P(None, "section"), P("dp", "section"),
        ),
        out_specs=(
            P("dp", "section"), P(("section", "dp"), None), P("section", None, "dp"), P("section", None, "dp"),
            P("section", "dp"), P("section", "dp", None), P("section", "dp", None), P("section", "dp", None),
            P("section", "dp", None), P("dp", "section"),
        ),
        check_vma=False,
    )
```

```python
import functools
import jax
import jax.numpy as jnp
from jax import lax
from jax.experimental import pallas as pl
from jax.experimental.pallas import tpu as pltpu
from jax.sharding import PartitionSpec as P

HEADS = 8
LANES = 128
EPSILON = 1e-05
MASKED = -1e30
ROOT_HALF = 0.7071067811865476
DENSITY_SCALE = 0.3989422804014327
MESH = pl.DeviceIdType.MESH
F32 = jnp.float32
BF16 = jnp.bfloat16
MICRO = 256
VMEM_BYTES = 60 * 2**20


def dot_nn(left, right):
    return lax.dot_general(left, right, (((1,), (0,)), ((), ())), preferred_element_type=F32)


def dot_nt(left, right):
    return lax.dot_general(left, right, (((1,), (1,)), ((), ())), preferred_element_type=F32)


def dot_tn(left, right):
    return lax.dot_general(left, right, (((0,), (0,)), ((), ())), preferred_element_type=F32)


def statistics(values):
    centered = values - jnp.mean(values, axis=-1, keepdims=True)
    inverse = lax.rsqrt(jnp.mean(centered * centered, axis=-1, keepdims=True) + EPSILON)
    return centered * inverse, inverse


def norm_backward(weighted, normed, inverse):
    return inverse * (
        weighted
        - jnp.mean(weighted, axis=-1, keepdims=True)
        - normed * jnp.mean(weighted * normed, axis=-1, keepdims=True)
    )


def column_sum(values):
    return jnp.sum(values, axis=0, keepdims=True)


def entry_masks():
    lane = lax.broadcasted_iota(jnp.int32, (8, LANES), 1) // 8
    return [lane == e for e in range(LANES // 8)]


def compress(tall, masks):
    tall = tall.reshape(2, LANES // 8, 8, LANES)
    kept = []
    for h in range(2):
        one = tall[h, 0]
        for e in range(1, LANES // 8):
            one = jnp.where(masks[e], tall[h, e], one)
        kept.append(one)
    return kept


def expand(flat, masks):
    zero = jnp.zeros_like(flat)
    return jnp.concatenate([jnp.where(mask, flat, zero) for mask in masks], axis=0).astype(BF16)


def half_masks():
    lane = lax.broadcasted_iota(jnp.int32, (1, LANES), 1)
    low = jnp.where(lane < LANES // 2, 1.0, 0.0)
    return low.astype(BF16), (1.0 - low).astype(BF16)


def by_head(pair, halves):
    return jnp.concatenate([pair * halves[0], pair * halves[1]], axis=0)


def head_mask(count_row):
    return lax.broadcasted_iota(jnp.int32, (8, LANES), 0) < count_row


def pool_matrix(count_row):
    lane = lax.broadcasted_iota(jnp.int32, (LANES // 8, LANES), 1)
    entry = lax.broadcasted_iota(jnp.int32, (LANES // 8, LANES), 0)
    return jnp.where((lane // 8 == entry) & (lane % 8 < count_row), 1.0, 0.0)


def capacity_of(slots, owners):
    return max(16, -(-2 * slots // owners // 16) * 16)


def ones_where(condition):
    return jnp.where(condition, 1.0, 0.0).astype(BF16)


def iota(shape, axis):
    return lax.broadcasted_iota(jnp.int32, shape, axis)


def positions(used):
    rows = min(LANES, used.shape[0])
    chunks = used.shape[0] // rows
    through = ones_where(iota((LANES, LANES), 0) <= iota((LANES, LANES), 1))
    above = ones_where(
        (iota((rows, rows), 0) // 8 == iota((rows, rows), 1) // 8) & (iota((rows, rows), 1) < iota((rows, rows), 0)))
    every = jnp.ones((LANES, LANES), BF16)
    out = []
    for chunk in range(chunks):
        part = used[chunk * rows:(chunk + 1) * rows, :].astype(BF16)
        before = dot_nn(dot_nn(above, part).astype(BF16), every)
        out.append(dot_nn(part, through) + before)
    return jnp.concatenate(out, axis=0)


def in_round(place, used, turn, capacity):
    place = place - (turn * capacity).astype(F32)
    return jnp.where((used > 0) & (place >= 1) & (place <= capacity), place, 0.0)


def owner_plan(ids_all, picks, used_rows, base, span, turn, capacity, lists):
    slots = ids_all.shape[2]
    blocks = -(-span // LANES)

    def count(d, carry):
        rel = ids_all[d // 2, pl.ds(lax.rem(d, 2), 1), :] - base
        high = jnp.where((rel >= 0) & (rel < span), rel >> 7, -1)
        counts = dot_nt(ones_where(iota((8, slots), 0) == high), ones_where(iota((LANES, slots), 0) == (rel & 127)))
        used_rows[pl.ds(pl.multiple_of(d * 8, 8), 8), :] = jnp.where(counts > 0, 1.0, 0.0)
        return carry

    lax.fori_loop(0, lists, count, 0)
    used = used_rows[pl.ds(0, lists * 8), :]
    used_rows[pl.ds(0, lists * 8), :] = in_round(positions(used), used, turn, capacity)

    def spread(d, carry):
        place = used_rows[pl.ds(pl.multiple_of(d * 8, 8), 8), :]
        wanted = (iota((capacity, LANES), 0) + 1).astype(F32)
        for block in range(blocks):
            picks[pl.ds(pl.multiple_of(d * capacity, 16), capacity), block * LANES:(block + 1) * LANES] = ones_where(
                place[block:block + 1, :] == wanted)
        return carry

    lax.fori_loop(0, lists, spread, 0)


def slot_codes(ids_row, span, first):
    value = ids_row.astype(F32)
    owner = jnp.floor((value + 0.5) * (1.0 / span))
    rel = value - owner * span
    high = jnp.floor(rel * (1.0 / LANES))
    owner = owner - first
    return owner, owner * 8 + high, rel - high * LANES


def owner_counts(ids_row, span, first, owners):
    slots = ids_row.shape[1]
    owner, row, lane = slot_codes(ids_row, span, first.astype(F32))
    rows = ones_where(iota((owners * 8, slots), 0).astype(F32) == row)
    lanes = ones_where(iota((LANES, slots), 0).astype(F32) == lane)
    return owner, rows, lanes, jnp.where(dot_nt(rows, lanes) > 0, 1.0, 0.0)


def slot_plan(ids_row, match, span, first, owners, turn, capacity):
    slots = ids_row.shape[1]
    owner, rows, lanes, used = owner_counts(ids_row, span, first, owners)
    place = in_round(positions(used), used, turn, capacity)
    mine = jnp.sum(dot_tn(place.astype(BF16), rows) * lanes.astype(F32), axis=0, keepdims=True)
    target = jnp.where(mine > 0, owner * capacity + mine - 1, -1.0)
    for owner_at in range(0, owners, 4):
        index = (iota((4 * capacity, slots), 0) + owner_at * capacity).astype(F32)
        match[owner_at * capacity:(owner_at + 4) * capacity, :] = ones_where(index == target)


def most_distinct(ids_all, span, owners, lists):
    def one(d, most):
        _, _, _, used = owner_counts(ids_all[d // 2, pl.ds(lax.rem(d, 2), 1), :], span, jnp.int32(0), owners)
        per_row = jnp.sum(used, axis=1, keepdims=True)
        per_owner = jnp.sum(per_row.reshape(owners, 8, 1), axis=1)
        return jnp.maximum(most, jnp.max(per_owner))

    return lax.fori_loop(0, lists, one, jnp.float32(0))


def device_at(index, columns):
    return (index // columns, lax.rem(index, columns))


def remote(src, dst, send, recv, peer):
    return pltpu.make_async_remote_copy(src, dst, send, recv, device_id=peer, device_id_type=MESH)


def lookup_rounds(columns, me, packed, landed, send, recv):
    lists, owners = 2 * columns, 4 * columns

    def target(d):
        return lax.rem(d, 2) * columns + d // 2

    def copy(d):
        return remote(packed.at[d], landed.at[me], send.at[d], recv.at[me], device_at(target(d), columns))

    def start(i, carry):
        d = lax.rem(i + 2 * lax.rem(me, columns), lists)

        @pl.when(target(d) != me)
        def _():
            copy(d).start()

        @pl.when(target(d) == me)
        def _():
            landed[me] = packed[d]
        return carry

    def arrive(o, carry):
        @pl.when(o != me)
        def _():
            remote(packed.at[0], landed.at[o], send.at[0], recv.at[o], device_at(o, columns)).wait_recv()
        return carry

    def left(d, carry):
        @pl.when(target(d) != me)
        def _():
            copy(d).wait_send()
        return carry

    return (lambda: lax.fori_loop(0, lists, start, 0), lambda: lax.fori_loop(0, owners, arrive, 0),
            lambda: lax.fori_loop(0, lists, left, 0))


def return_rounds(columns, me, parts, landed, send, recv):
    lists, owners = 2 * columns, 4 * columns
    slot = lax.rem(me, columns) * 2 + me // columns

    def copy(o):
        return remote(parts.at[o], landed.at[slot], send.at[o], recv.at[slot], device_at(o, columns))

    def start(i, carry):
        o = lax.rem(i + me, owners)

        @pl.when(o != me)
        def _():
            copy(o).start()

        @pl.when(o == me)
        def _():
            landed[slot] = parts[me]
        return carry

    def arrive(d, carry):
        source = lax.rem(d, 2) * columns + d // 2

        @pl.when(source != me)
        def _():
            remote(parts.at[0], landed.at[d], send.at[0], recv.at[d], device_at(source, columns)).wait_recv()
        return carry

    def left(o, carry):
        @pl.when(o != me)
        def _():
            copy(o).wait_send()
        return carry

    return (lambda: lax.fori_loop(0, owners, start, 0), lambda: lax.fori_loop(0, lists, arrive, 0),
            lambda: lax.fori_loop(0, owners, left, 0))


def greet_all(columns, me, others):
    barrier = pltpu.get_barrier_semaphore()

    def greet(o, carry):
        @pl.when(o != me)
        def _():
            pl.semaphore_signal(barrier, inc=1, device_id=device_at(o, columns), device_id_type=MESH)
        return carry

    lax.fori_loop(0, others, greet, 0)
    return barrier


def pack_rows(table, padded, picks, packed, span, capacity, lists):
    padded[pl.ds(0, span), :] = table[...]
    for d in range(0, lists, 4):
        rows = dot_nn(picks[d * capacity:(d + 4) * capacity, :], padded[...]).astype(BF16)
        packed[d:d + 4] = rows.reshape(4, capacity, rows.shape[1])


def lookup_kernel(
    columns, capacity,
    ids, table, cot_in, proj, vocab, gain_in, shift_in, bias_in, qkv_in, out_in, up_in, down_in,
    x_out, picks, ids_all, most_out, pool_out, gain_all, shift_all, bias_all, qkv_all, out_all, up_all, down_all,
    match, used_rows, padded, packed, landed, pool_send, pool_parts,
    i_send, i_recv, t_send, t_recv, w_send, w_recv, g_send, g_recv,
):
    section = lax.axis_index("section")
    column = lax.axis_index("dp")
    core = lax.rem(section, 2)
    me = section * columns + column
    owners, lists = 4 * columns, 2 * columns
    span, width = table.shape
    entries = cot_in.shape[0]
    core_peer = (section + 1 - 2 * core, column)
    barrier = greet_all(columns, me, owners)
    ids_all[column] = ids[...]
    padded[...] = jnp.zeros_like(padded)
    pl.semaphore_wait(barrier, owners - 1)

    def ids_copy(d):
        return remote(ids, ids_all.at[column], i_send.at[d - 1], i_recv.at[column],
                      (section, lax.rem(column + d, columns)))

    for d in range(1, columns):
        ids_copy(d).start()
    pairs = ((gain_in, gain_all), (shift_in, shift_all), (bias_in, bias_all),
             (qkv_in, qkv_all), (out_in, out_all), (up_in, up_all), (down_in, down_all))
    weight_copies = [
        remote(src, dst, w_send.at[i], w_recv.at[i], core_peer) for i, (src, dst) in enumerate(pairs)]
    for copy in weight_copies:
        copy.start()

    position = column * entries + iota((entries, cot_in.shape[1]), 0)
    cot = jnp.where(position < vocab[0], cot_in[...].astype(F32), 0.0).astype(BF16)
    part = dot_nt(cot, proj[...]).astype(BF16)
    pool_send[...] = part.reshape(2, entries // 2, width)

    def pool_copy(k):
        return remote(pool_send.at[k], pool_parts.at[section], g_send.at[k], g_recv.at[section], (2 + k, column))

    for k in range(2):
        @pl.when(section != 2 + k)
        def _(k=k):
            pool_copy(k).start()

        @pl.when(section == 2 + k)
        def _(k=k):
            pool_parts[section] = pool_send[k]

    for d in range(1, columns):
        source = lax.rem(column + d, columns)
        remote(ids, ids_all.at[source], i_send.at[d - 1], i_recv.at[source], (section, source)).wait_recv()
    turn = jnp.int32(0)
    owner_plan(ids_all, picks, used_rows, me * span, span, turn, capacity, lists)
    pack_rows(table, padded, picks, packed, span, capacity, lists)
    start, arrive, left = lookup_rounds(columns, me, packed, landed, t_send, t_recv)
    start()

    @pl.when(section < 2)
    def _():
        slot_plan(ids_all[column, pl.ds(core, 1), :], match, span, jnp.int32(0), owners, turn, capacity)

    most_out[...] = jnp.full(most_out.shape, most_distinct(ids_all, span, owners, lists), F32)

    @pl.when(section >= 2)
    def _():
        total = pool_parts[section].astype(F32)
        for d in range(1, 4):
            source = lax.rem(section + d, 4)
            remote(pool_send.at[0], pool_parts.at[source], g_send.at[0], g_recv.at[source],
                   (source, column)).wait_recv()
            total = total + pool_parts[source].astype(F32)
        pool_out[...] = total

    @pl.when(section < 2)
    def _():
        arrive()
        x_out[...] = dot_tn(match[...], landed[...].reshape(owners * capacity, width)).astype(BF16)

    left()
    for k in range(2):
        @pl.when(section != 2 + k)
        def _(k=k):
            pool_copy(k).wait_send()
    for d in range(1, columns):
        ids_copy(d).wait_send()
    for copy in weight_copies:
        copy.wait()


def lookup(columns, ids, table, cot, proj, vocab, gain, shift, bias, w_qkv, w_out, w_up, w_down):
    slots = ids.shape[1]
    span, width = table.shape
    owners, lists = 4 * columns, 2 * columns
    capacity = capacity_of(slots, owners)
    padded_span = -(-span // LANES) * LANES
    entries = cot.shape[0]
    vmem = pl.BlockSpec(memory_space=pltpu.VMEM)
    smem = pl.BlockSpec(memory_space=pltpu.SMEM)
    hbm = pl.BlockSpec(memory_space=pl.ANY)
    shape = jax.ShapeDtypeStruct
    params = (gain, shift, bias, w_qkv, w_out, w_up, w_down)
    outs = [
        shape((slots, width), BF16), shape((lists * capacity, padded_span), BF16), shape((columns, 2, slots), jnp.int32), shape((8, LANES), F32),
        shape((entries // 2, width), F32),
    ] + [shape(p.shape, p.dtype) for p in params]
    sem = pltpu.SemaphoreType.DMA
    return pl.pallas_call(
        functools.partial(lookup_kernel, columns, capacity),
        out_shape=outs,
        in_specs=[vmem] * 4 + [smem] + [hbm] * 7,
        out_specs=[vmem] * 5 + [hbm] * 7,
        scratch_shapes=[
            pltpu.VMEM((owners * capacity, slots), BF16),
            pltpu.VMEM((max(lists, owners) * 8, LANES), F32), pltpu.VMEM((padded_span, width), BF16),
            pltpu.VMEM((lists, capacity, width), BF16), pltpu.VMEM((owners, capacity, width), BF16),
            pltpu.VMEM((2, entries // 2, width), BF16), pltpu.VMEM((4, entries // 2, width), BF16),
            sem((columns - 1,)), sem((columns,)), sem((lists,)), sem((owners,)), sem((7,)), sem((7,)),
            sem((2,)), sem((4,)),
        ],
        compiler_params=pltpu.CompilerParams(collective_id=3, has_side_effects=True, vmem_limit_bytes=VMEM_BYTES),
    )(ids, table, cot, proj, vocab, *params)


def more_lookup_kernel(columns, capacity, turn, ids_all, table, x_out, match, picks, used_rows, padded, packed, landed,
                       t_send, t_recv):
    section = lax.axis_index("section")
    column = lax.axis_index("dp")
    me = section * columns + column
    owners, lists = 4 * columns, 2 * columns
    span, width = table.shape
    barrier = pltpu.get_barrier_semaphore()

    @pl.when(section < 2)
    def _():
        greet_all(columns, me, owners)
        pl.semaphore_wait(barrier, lists - 1)

    @pl.when(section >= 2)
    def _():
        pl.semaphore_wait(barrier, lists)

    padded[...] = jnp.zeros_like(padded)
    owner_plan(ids_all, picks, used_rows, me * span, span, turn[0], capacity, lists)
    pack_rows(table, padded, picks, packed, span, capacity, lists)
    start, arrive, left = lookup_rounds(columns, me, packed, landed, t_send, t_recv)
    start()
    x_out[...] = jnp.zeros_like(x_out)

    @pl.when(section < 2)
    def _():
        slot_plan(ids_all[column, pl.ds(lax.rem(section, 2), 1), :], match, span, jnp.int32(0), owners, turn[0], capacity)
        arrive()
        x_out[...] = dot_tn(match[...], landed[...].reshape(owners * capacity, width)).astype(BF16)

    left()


def more_lookup(columns, turn, ids_all, table):
    slots = ids_all.shape[2]
    span, width = table.shape
    owners, lists = 4 * columns, 2 * columns
    capacity = capacity_of(slots, owners)
    padded_span = -(-span // LANES) * LANES
    vmem = pl.BlockSpec(memory_space=pltpu.VMEM)
    sem = pltpu.SemaphoreType.DMA
    return pl.pallas_call(
        functools.partial(more_lookup_kernel, columns, capacity),
        out_shape=jax.ShapeDtypeStruct((slots, width), BF16),
        in_specs=[pl.BlockSpec(memory_space=pltpu.SMEM), vmem, vmem],
        out_specs=vmem,
        scratch_shapes=[
            pltpu.VMEM((owners * capacity, slots), BF16), pltpu.VMEM((lists * capacity, padded_span), BF16),
            pltpu.VMEM((max(lists, owners) * 8, LANES), F32), pltpu.VMEM((padded_span, width), BF16),
            pltpu.VMEM((lists, capacity, width), BF16), pltpu.VMEM((owners, capacity, width), BF16),
            sem((lists,)), sem((owners,)),
        ],
        compiler_params=pltpu.CompilerParams(collective_id=4, has_side_effects=True, vmem_limit_bytes=VMEM_BYTES),
    )(turn, ids_all, table)


def return_parts(match, dx, parts, owners, capacity):
    for o in range(0, owners, 4):
        rows = dot_nn(match[o * capacity:(o + 4) * capacity, :], dx[...]).astype(BF16)
        parts[o:o + 4] = rows.reshape(4, capacity, rows.shape[1])


def more_return_kernel(columns, capacity, turn, ids_all, dx, held, grad_out, match, picks, used_rows, parts, landed,
                       t_send, t_recv):
    section = lax.axis_index("section")
    column = lax.axis_index("dp")
    me = section * columns + column
    owners, lists = 4 * columns, 2 * columns
    span, width = held.shape
    slots = ids_all.shape[2]
    barrier = greet_all(columns, me, lists)

    @pl.when(section < 2)
    def _():
        pl.semaphore_wait(barrier, owners - 1)

    start, arrive, left = return_rounds(columns, me, parts, landed, t_send, t_recv)

    @pl.when(section < 2)
    def _():
        slot_plan(ids_all[column, pl.ds(lax.rem(section, 2), 1), :], match, span, jnp.int32(0), owners, turn[0], capacity)
        return_parts(match, dx, parts, owners, capacity)
        start()

    owner_plan(ids_all, picks, used_rows, me * span, span, turn[0], capacity, lists)
    arrive()
    grad = dot_tn(picks[...], landed[...].reshape(lists * capacity, width))
    grad_out[...] = held[...] + grad[:span]

    @pl.when(section < 2)
    def _():
        left()


def more_return(columns, turn, ids_all, dx, held):
    slots = ids_all.shape[2]
    span, width = held.shape
    owners, lists = 4 * columns, 2 * columns
    capacity = capacity_of(slots, owners)
    padded_span = -(-span // LANES) * LANES
    vmem = pl.BlockSpec(memory_space=pltpu.VMEM)
    sem = pltpu.SemaphoreType.DMA
    return pl.pallas_call(
        functools.partial(more_return_kernel, columns, capacity),
        out_shape=jax.ShapeDtypeStruct((span, width), F32),
        in_specs=[pl.BlockSpec(memory_space=pltpu.SMEM), vmem, vmem, vmem],
        out_specs=vmem,
        scratch_shapes=[
            pltpu.VMEM((owners * capacity, slots), BF16), pltpu.VMEM((lists * capacity, padded_span), BF16),
            pltpu.VMEM((max(lists, owners) * 8, LANES), F32),
            pltpu.VMEM((owners, capacity, width), BF16), pltpu.VMEM((lists, capacity, width), BF16),
            sem((owners,)), sem((lists,)),
        ],
        compiler_params=pltpu.CompilerParams(collective_id=5, has_side_effects=True, vmem_limit_bytes=VMEM_BYTES),
    )(turn, ids_all, dx, held)


PHASE_LAG = 2
PROJECT_AFTER = 5
ADD_LAG = 2
VEC_GAP = 3
SEND_NEAR = 1
SEND_FAR = 8
TABLE_STEP = 13
SWAPPED = (3, 7, 11)


def unit_order(u, bits):
    order = list(range(bits))
    if u in SWAPPED and bits > 1:
        order[0], order[1] = 1, 0
    return order


def slot_in(order, q):
    slot = 0
    for bit in order:
        slot = slot * 2 + (q >> bit) % 2
    return slot


def trunk_kernel(columns, width, hidden, micros, *refs):
    (x0, counts, pool_grad), refs = refs[:3], refs[3:]
    own, theirs, refs = refs[:7], refs[7:14], refs[14:]
    (cot_in, proj, picks, ids_all, vocab), refs = refs[:5], refs[5:]
    (emb_out, gain_out, shift_out, upb_out, qkv_out, out_out, up_out, down_out, proj_out, table_out, dx_out), refs = (
        refs[:11], refs[11:])
    bits = columns.bit_length() - 1
    recv, refs = refs[:bits], refs[bits:]
    (gains, shifts, up_bias, w_all, a, dqkv, att, dbr, h_in_all, dpre, act_all, dy_all,
     x_in, x_mid, resid, prob, y_out, dy_in, vec, upb, pooled,
     wide, s0_recv, proj_sums, v_buf, pool_all, cot, match, dxs, parts, landed,
     f_send, f_recv, b_send, b_recv, p_sem,
     c_send, c_recv, h_send, h_recv, v_send, v_recv, q_send, q_recv, t_send, t_recv, d_send, d_recv) = refs
    section = lax.axis_index("section")
    column = lax.axis_index("dp")
    core = lax.rem(section, 2)
    stage = section // 2
    core_peer = (section + 1 - 2 * core, column)
    far_peer = (lax.rem(section + 2, 4), column)
    blocks = MICRO // LANES
    score_scale = (width // HEADS) ** (-0.5)
    piece = width // columns
    tiles = hidden // width
    units = 4 + 2 * tiles
    first_down = 4 + tiles
    capacity = parts.shape[1] // 2
    lists = 2 * columns

    def tile_of(source, u):
        if u < 3:
            return source[3].at[0, :, u * width:(u + 1) * width]
        if u == 3:
            return source[4].at[0]
        if u < first_down:
            return source[5].at[0, :, (u - 4) * width:(u - 3) * width]
        return source[6].at[0, (u - first_down) * width:(u - first_down + 1) * width, :]

    def fetch(i, source, layer):
        src = source[i].at[0] if i < 3 else tile_of(source, i - 3)
        dst = (gains, shifts, up_bias)[i].at[layer] if i < 3 else w_all.at[layer, i - 3]
        return pltpu.make_async_copy(src, dst, p_sem.at[i, layer])

    for first in range(2):
        @pl.when(core == first)
        def _(first=first):
            for layer in range(2):
                for i in (0, 1, 3, 4, 5, 6, 2, *range(7, 3 + units)):
                    fetch(i, own if layer == first else theirs, layer).start()

    def need(m, layer, *indices):
        @pl.when(m == 0)
        def _():
            for i in indices:
                fetch(i, own, layer).wait()

    def section_peer(d):
        return (lax.rem(section + d, 4), column)

    def column_peer(d):
        return (section, lax.rem(column + d, columns))

    peers = [section_peer(d) for d in range(1, 4)] + [column_peer(d) for d in range(1, columns)]
    barrier = pltpu.get_barrier_semaphore()
    for peer in peers:
        pl.semaphore_signal(barrier, inc=1, device_id=peer, device_id_type=MESH)
    vec[...] = jnp.zeros_like(vec)
    upb[...] = jnp.zeros_like(upb)

    @pl.when(stage == 0)
    def _():
        x_in[...] = x0[...]

    pl.semaphore_wait(barrier, len(peers))

    def rows_of(m):
        return pl.ds(pl.multiple_of(m * MICRO, MICRO), MICRO)

    def forward_copy(m):
        return remote(y_out.at[rows_of(m)], x_in.at[rows_of(m)], f_send.at[m], f_recv.at[m], far_peer)

    def backward_copy(m):
        return remote(y_out.at[rows_of(m)], dy_in.at[rows_of(m)], b_send.at[m], b_recv.at[m], far_peer)

    def count_row(m, b):
        return counts[pl.ds(m * blocks + b, 1), :]

    def layer_forward(layer, m, x):
        rows = rows_of(m)
        masks, halves = entry_masks(), half_masks()
        xf = x.astype(F32)
        normed, _ = statistics(xf)
        need(m, layer, 0, 1, 3, 4, 5)
        a_low = (normed * gains[layer, pl.ds(0, 1), :] + shifts[layer, pl.ds(0, 1), :]).astype(BF16)
        a[layer, rows, :] = a_low
        for t in range(3):
            cols = slice(t * width, (t + 1) * width)
            dqkv[layer, rows, cols] = dot_nn(a_low, w_all[layer, t]).astype(BF16)
        for b in range(blocks):
            block = pl.ds(pl.multiple_of(m * MICRO + b * LANES, LANES), LANES)
            keys_on = head_mask(count_row(m, b))
            for pair in range(HEADS // 2):
                cols = slice(pair * LANES, (pair + 1) * LANES)
                q = dqkv[layer, block, cols]
                k = dqkv[layer, block, slice(width + pair * LANES, width + (pair + 1) * LANES)]
                v = dqkv[layer, block, slice(2 * width + pair * LANES, 2 * width + (pair + 1) * LANES)]
                flats = compress(dot_nt(by_head(k, halves), q), masks)
                wide = []
                for h in range(2):
                    s = jnp.where(keys_on, flats[h] * score_scale, MASKED)
                    e = jnp.exp(s - jnp.max(s, axis=0, keepdims=True))
                    p = e / jnp.sum(e, axis=0, keepdims=True)
                    prob[layer, m * blocks + b, pl.ds((2 * pair + h) * 8, 8), :] = p
                    wide.append(expand(p, masks))
                mixed = dot_tn(jnp.concatenate(wide, axis=0), by_head(v, halves))
                att[layer, block, cols] = mixed.astype(BF16)
        need(m, layer, 6)
        res = xf + dot_nn(att[layer, rows, :], w_all[layer, 3]) + shifts[layer, pl.ds(1, 1), :]
        resid[layer, rows, :] = res
        normed_two, _ = statistics(res)
        h_in = (normed_two * gains[layer, pl.ds(1, 1), :] + shifts[layer, pl.ds(2, 1), :]).astype(BF16)
        h_in_all[layer, rows, :] = h_in
        need(m, layer, 2, *range(7, 3 + units))
        total = res + shifts[layer, pl.ds(3, 1), :]
        for t in range(tiles):
            cols = slice(t * width, (t + 1) * width)
            pre = dot_nn(h_in, w_all[layer, 4 + t]) + up_bias[layer, :, cols]
            dpre[layer, rows, cols] = pre.astype(BF16)
            act = (pre * (0.5 * (1.0 + lax.erf(pre * ROOT_HALF)))).astype(BF16)
            total = total + dot_nn(act, w_all[layer, first_down + t])
        return total.astype(BF16)

    def layer_backward(layer, m, dy):
        rows = rows_of(m)
        masks, halves = entry_masks(), half_masks()
        dyf = dy.astype(F32)
        vec[layer, pl.ds(5, 1), :] += column_sum(dyf)
        d_hidden = jnp.zeros((MICRO, width), F32)
        for t in range(tiles):
            cols = slice(t * width, (t + 1) * width)
            d_act = dot_nt(dy, w_all[layer, first_down + t])
            pre = dpre[layer, rows, cols].astype(F32)
            phi = 0.5 * (1.0 + lax.erf(pre * ROOT_HALF))
            density = jnp.exp(-0.5 * pre * pre) * DENSITY_SCALE
            act_all[layer, rows, cols] = (pre * phi).astype(BF16)
            d_pre = (d_act * (phi + pre * density)).astype(BF16)
            dpre[layer, rows, cols] = d_pre
            upb[layer, :, cols] += column_sum(d_pre.astype(F32))
            d_hidden = d_hidden + dot_nt(d_pre, w_all[layer, 4 + t])
        normed_two, inverse_two = statistics(resid[layer, rows, :])
        vec[layer, pl.ds(1, 1), :] += column_sum(d_hidden * normed_two)
        vec[layer, pl.ds(4, 1), :] += column_sum(d_hidden)
        d_resid = dyf + norm_backward(d_hidden * gains[layer, pl.ds(1, 1), :], normed_two, inverse_two)
        d_branch = d_resid.astype(BF16)
        dbr[layer, rows, :] = d_branch
        vec[layer, pl.ds(3, 1), :] += column_sum(d_branch.astype(F32))
        d_att = dot_nt(d_branch, w_all[layer, 3]).astype(BF16)
        for b in range(blocks):
            block = pl.ds(pl.multiple_of(m * MICRO + b * LANES, LANES), LANES)
            for pair in range(HEADS // 2):
                c_q = slice(pair * LANES, (pair + 1) * LANES)
                c_k = slice(width + pair * LANES, width + (pair + 1) * LANES)
                c_v = slice(2 * width + pair * LANES, 2 * width + (pair + 1) * LANES)
                q = dqkv[layer, block, c_q]
                k = dqkv[layer, block, c_k]
                v = dqkv[layer, block, c_v]
                da = d_att[b * LANES:(b + 1) * LANES, c_q]
                flats = compress(dot_nt(by_head(v, halves), da), masks)
                wide_p, wide_s = [], []
                for h in range(2):
                    p = prob[layer, m * blocks + b, pl.ds((2 * pair + h) * 8, 8), :]
                    ds = p * (flats[h] - jnp.sum(flats[h] * p, axis=0, keepdims=True))
                    wide_p.append(expand(p, masks))
                    wide_s.append(expand(ds, masks))
                d_v = dot_nn(jnp.concatenate(wide_p, axis=1), by_head(da, halves))
                d_k = dot_nn(jnp.concatenate(wide_s, axis=1), by_head(q, halves)) * score_scale
                d_q = dot_tn(jnp.concatenate(wide_s, axis=0), by_head(k, halves)) * score_scale
                dqkv[layer, block, c_q] = d_q.astype(BF16)
                dqkv[layer, block, c_k] = d_k.astype(BF16)
                dqkv[layer, block, c_v] = d_v.astype(BF16)
        d_a = jnp.zeros((MICRO, width), F32)
        for t in range(3):
            cols = slice(t * width, (t + 1) * width)
            d_a = d_a + dot_nt(dqkv[layer, rows, cols], w_all[layer, t])
        x = jnp.where(layer == 0, x_in[rows, :], x_mid[rows, :])
        normed, inverse = statistics(x.astype(F32))
        vec[layer, pl.ds(0, 1), :] += column_sum(d_a * normed)
        vec[layer, pl.ds(2, 1), :] += column_sum(d_a)
        dx = d_resid + norm_backward(d_a * gains[layer, pl.ds(0, 1), :], normed, inverse)
        return dx.astype(BF16)


    def forward_layer(layer, m, x):
        @pl.when(layer == 1)
        def _():
            x_mid[rows_of(m), :] = x

        return layer_forward(layer, m, x)

    def forward_step(m, carry):
        rows = rows_of(m)

        @pl.when(stage == 1)
        def _():
            forward_copy(m).wait_recv()

        x = lax.fori_loop(0, 2, lambda layer, x: forward_layer(layer, m, x), x_in[rows, :])
        y_out[rows, :] = x

        @pl.when(stage == 0)
        def _():
            forward_copy(m).start()

        @pl.when(stage == 1)
        def _():
            for b in range(blocks):
                matrix = pool_matrix(count_row(m, b))
                summed = dot_nn(matrix.astype(BF16), x[b * LANES:(b + 1) * LANES, :])
                mean = summed / jnp.sum(matrix, axis=1, keepdims=True)
                entries = pl.ds(pl.multiple_of((m * blocks + b) * (LANES // 8), LANES // 8), LANES // 8)
                pooled[entries, :] = mean.astype(BF16)
        return carry

    lax.fori_loop(0, micros, forward_step, 0)

    def my_bit(b):
        return lax.rem(column // (1 << b), 2)

    def bit_peer(b):
        return (section, column + (1 << b) - my_bit(b) * (2 << b))

    def pool_copy(d):
        return remote(pooled, pool_all.at[core], q_send.at[d - 1], q_recv.at[core], section_peer(d))

    def pool_arrival(k):
        return remote(pooled, pool_all.at[k], q_send.at[0], q_recv.at[k], core_peer)

    @pl.when(stage == 1)
    def _():
        for d in range(1, 4):
            pool_copy(d).start()
        pool_all[core] = pooled[...]

    @pl.when(stage == 0)
    def _():
        for m in range(micros):
            forward_copy(m).wait_send()

    def core_copy(u):
        return remote(w_all.at[1 - core, u], s0_recv.at[u], c_send.at[u], c_recv.at[u], core_peer)

    def is_wide(k):
        return k < bits and (columns >> (k + 1)) * piece < 16

    def source_of(u, k):
        if is_wide(k):
            return wide.at[u]
        if k > 0:
            return recv[k - 1].at[u]
        return w_all.at[core, u] if u < units else proj_sums

    def side_rows(k, side):
        size = (columns >> (k + 1)) * piece
        return pl.ds(pl.multiple_of(side * size, size), size)

    def halving_copy(u, k):
        bit = unit_order(u, bits)[k]
        return remote(source_of(u, k).at[side_rows(k, 1 - my_bit(bit))], recv[k].at[u], h_send.at[k, u],
                      h_recv.at[k, u], bit_peer(bit))

    def absorb(u, k):
        halving_copy(u, k).wait_recv()
        bit = unit_order(u, bits)[k]
        return recv[k][u].astype(F32) + source_of(u, k)[side_rows(k, my_bit(bit)), :].astype(F32)

    def advance(u, k):
        if k < bits - 1:
            if is_wide(k + 1):
                wide[u] = absorb(u, k)
            else:
                recv[k][u] = absorb(u, k).astype(BF16)
            halving_copy(u, k + 1).start()
        else:
            finish(u, absorb(u, k))

    def cut(value, q):
        return value[q * piece:(q + 1) * piece, :]

    def rows_at(u, q):
        slot = slot_in(unit_order(u, bits), q)
        return slice(slot * piece, (slot + 1) * piece)

    def product(layer, u):
        if u < 3:
            return dot_tn(a[layer], dqkv[layer, :, u * width:(u + 1) * width])
        if u == 3:
            return dot_tn(att[layer], dbr[layer])
        t = u - 4
        return dot_tn(h_in_all[layer], dpre[layer, :, t * width:(t + 1) * width])

    def send_or_add(layer, u):
        @pl.when(core != layer)
        def _():
            core_copy(u).start()

        if u >= ADD_LAG:
            @pl.when(core == layer)
            def _():
                add_own(u - ADD_LAG)

    def add_own(u):
        core_copy(u).wait_recv()
        w_all[core, u] = (w_all[core, u].astype(F32) + s0_recv[u].astype(F32)).astype(BF16)
        halving_copy(u, 0).start()

    def weight_gradients(layer):
        for u in range(first_down):
            value = product(layer, u).astype(BF16)
            for q in range(columns):
                w_all[layer, u, rows_at(u, q), :] = cut(value, q)
            send_or_add(layer, u)
        for i in range(tiles):
            value = dot_tn(act_all[layer, :, i * width:(i + 1) * width], dy_all[layer]).astype(BF16)
            for j in range(columns):
                u, q = first_down + j % tiles, i * columns // tiles + j // tiles
                w_all[layer, u, rows_at(u, q), :] = cut(value, j)
        for u in range(first_down, units):
            send_or_add(layer, u)

        @pl.when(core == layer)
        def _():
            for u in range(units - ADD_LAG, units):
                add_own(u)

    def project():
        @pl.when(section >= 2)
        def _():
            pool_arrival(1 - core).wait_recv()

        @pl.when(section < 2)
        def _():
            pool_arrival(0).wait_recv()
            pool_arrival(1).wait_recv()

        entries = cot_in.shape[0]
        position = column * entries + iota((entries, cot_in.shape[1]), 0)
        live = position < vocab[0]
        cot[...] = jnp.where(live, cot_in[...].astype(F32), 0.0).astype(BF16)
        rows = pool_all[...].reshape(entries, width)
        emb_out[...] = jnp.where(live, dot_nn(rows, proj[...]), 0.0)
        value = dot_tn(rows, cot[...]).astype(BF16)
        for q in range(columns):
            proj_sums[rows_at(units, q), :] = cut(value, q)

        halving_copy(units, 0).start()

    def project_now():
        project()
        for k in range(bits):
            advance(units, k)

    def put_vec(slot, layer):
        v_buf[slot, :, slice(0, width)] = vec[layer]
        for t in range(2):
            v_buf[slot, pl.ds(6 + t, 1), :] = upb[layer, :, t * (hidden // 2):(t + 1) * (hidden // 2)]

    def vec_copy(src, index, peer):
        return remote(v_buf.at[src], v_buf.at[index], v_send.at[index], v_recv.at[index], peer)

    def vec_peer_copy(k):
        return vec_copy(1 + 2 * k + (k > 0), 3 + 2 * k, bit_peer(k))

    def share_copy(half, way, peer):
        return remote(dxs.at[half], dxs.at[half], d_send.at[way], d_recv.at[half], peer)

    def finish(u, total):
        if u < 3:
            qkv_out[0, :, u * width:(u + 1) * width] = total
        elif u == 3:
            out_out[0] = total
        elif u < first_down:
            up_out[0, :, (u - 4) * width:(u - 3) * width] = total
        elif u < units:
            t = u - first_down
            down_out[0, t * piece:(t + 1) * piece, :] = total
        else:
            proj_out[...] = total

    def vec_step(k):
        if k == 0:
            put_vec(0, 1 - core)
            put_vec(1, core)
            vec_copy(0, 2, core_peer).start()
            vec_copy(0, 2, core_peer).wait_recv()
            v_buf[1] = v_buf[1] + v_buf[2]
            vec_peer_copy(0).start()
            return
        vec_peer_copy(k - 1).wait_recv()
        source = 1 + 2 * (k - 1) + (k > 1)
        total = v_buf[source] + v_buf[3 + 2 * (k - 1)]
        if k < bits:
            v_buf[2 * k + 2] = total
            vec_peer_copy(k).start()
            return
        lanes = width // columns
        share = hidden // columns
        for q in range(columns):
            @pl.when(column == q)
            def _(q=q):
                gain_out[0] = total[0:2, q * lanes:(q + 1) * lanes]
                shift_out[0] = total[2:6, q * lanes:(q + 1) * lanes]
                row, start = divmod(q * share, hidden // 2)
                upb_out[...] = total[6 + row:7 + row, start:start + share]

    def table_copy(d):
        peer = column_peer(d)
        return remote(parts.at[peer[1]], landed.at[column], t_send.at[d - 1], t_recv.at[column], peer)

    def table_parts():
        share_copy(1 - core, 0, core_peer).wait_recv()
        for half in range(2):
            slot_plan(ids_all[column, pl.ds(half, 1), :], match, table_out.shape[0], section * columns, columns,
                      jnp.int32(0), capacity)
            rows = dot_nn(match[...], dxs[half]).astype(BF16)
            parts[:, half * capacity:(half + 1) * capacity, :] = rows.reshape(columns, capacity, width)
        for d in range(1, columns):
            table_copy(d).start()
        landed[column] = parts[column]

    def table_finish():
        for d in range(1, columns):
            source = lax.rem(column + d, columns)
            remote(parts.at[0], landed.at[source], t_send.at[0], t_recv.at[source], (section, source)).wait_recv()
        grad = dot_tn(picks[...], landed[...].reshape(lists * capacity, width))
        table_out[...] = grad[:table_out.shape[0]]

    pl.when(stage == 0)(project_now)

    def seed(m):
        rows = rows_of(m)

        @pl.when(stage == 0)
        def _():
            backward_copy(m).wait_recv()
            dy_all[1, rows, :] = dy_in[rows, :]

        @pl.when(stage == 1)
        def _():
            for b in range(blocks):
                matrix = pool_matrix(count_row(m, b))
                entries = pl.ds(pl.multiple_of((m * blocks + b) * (LANES // 8), LANES // 8), LANES // 8)
                share = (pool_grad[entries, :] / jnp.sum(matrix, axis=1, keepdims=True)).astype(BF16)
                block = pl.ds(pl.multiple_of(m * MICRO + b * LANES, LANES), LANES)
                dy_all[1, block, :] = dot_tn(matrix.astype(BF16), share).astype(BF16)

    def backward(layer, m):
        rows = rows_of(m)
        dx = layer_backward(layer, m, dy_all[layer, rows, :])

        @pl.when(layer == 1)
        def _():
            dy_all[0, rows, :] = dx

        @pl.when(layer == 0)
        def _():
            dx_out[rows, :] = dx
            dxs[core, rows, :] = dx

        @pl.when((layer == 0) & (stage == 1))
        def _():
            y_out[rows, :] = dx
            backward_copy(m).start()

    last = micros - 1

    def backward_step(i, carry):
        m, turn = jnp.minimum(i // 2, last), i - 2 * jnp.minimum(i // 2, last)

        @pl.when(turn == 0)
        def _():
            seed(m)

        @pl.when(turn < 2)
        def _():
            backward(1 - turn, m)

        layer = 1 - turn + stage

        @pl.when((m == last) & (turn == 1) & (stage == 0))
        def _():
            share_copy(core, 0, core_peer).start()
            share_copy(core, 1, far_peer).start()

        @pl.when((m == last) & (layer >= 0) & (layer < 2))
        def _():
            weight_gradients(layer)
        return carry

    lax.fori_loop(0, 2 * micros + 1, backward_step, 0)

    lags = [PHASE_LAG * k for k in range(bits)]
    for step in range(units + lags[-1]):
        if step == SEND_NEAR:
            pl.when(section < 2)(table_parts)
        if step == SEND_FAR - 1:
            @pl.when(section >= 2)
            def _():
                share_copy(core, 0, far_peer).wait_recv()
                share_copy(core, 0, core_peer).start()
        if step == SEND_FAR:
            pl.when(section >= 2)(table_parts)
        if step == TABLE_STEP:
            table_finish()
        if step % VEC_GAP == 0 and step // VEC_GAP <= bits:
            vec_step(step // VEC_GAP)
        if step == 0:
            pl.when(stage == 1)(project)
        for k in range(bits):
            u = step - lags[k]
            if 0 <= u < units:
                advance(u, k)
            if u == PROJECT_AFTER:
                @pl.when(stage == 1)
                def _(k=k):
                    advance(units, k)
    for k in range((units + lags[-1] - 1) // VEC_GAP + 1, bits + 1):
        vec_step(k)

    @pl.when(stage == 1)
    def _():
        for m in range(micros):
            backward_copy(m).wait_send()

    vec_copy(0, 2, core_peer).wait_send()
    for k in range(bits):
        vec_peer_copy(k).wait_send()
    for u in range(units):
        core_copy(u).wait_send()
    for u in range(units + 1):
        for k in range(bits):
            halving_copy(u, k).wait_send()
    for d in range(1, columns):
        table_copy(d).wait_send()
    share_copy(core, 0, core_peer).wait_send()

    @pl.when(section < 2)
    def _():
        share_copy(core, 1, far_peer).wait_send()

    @pl.when(section >= 2)
    def _():
        for d in range(1, 4):
            pool_copy(d).wait_send()


def trunk(columns, x0, counts, pool_grad, own, theirs, cot, proj, picks, ids_all, span, vocab):
    rows, width = x0.shape
    hidden = own[5].shape[2]
    micros = rows // MICRO
    entries, out_width = cot.shape
    piece, tiles = width // columns, hidden // width
    bits = columns.bit_length() - 1
    units = 4 + 2 * tiles
    sizes = [(columns >> (k + 1)) * piece for k in range(bits)]
    capacity = picks.shape[0] // (2 * columns)
    vmem = pl.BlockSpec(memory_space=pltpu.VMEM)
    smem = pl.BlockSpec(memory_space=pltpu.SMEM)
    hbm = pl.BlockSpec(memory_space=pl.ANY)
    shape, sem, space = jax.ShapeDtypeStruct, pltpu.SemaphoreType.DMA, pltpu.VMEM
    outs = [
        shape((entries, out_width), F32), shape((1, 2, piece), F32), shape((1, 4, piece), F32),
        shape((1, hidden // columns), F32), shape((1, piece, 3 * width), F32), shape((1, piece, width), F32),
        shape((1, piece, hidden), F32), shape((1, tiles * piece, width), F32), shape((piece, out_width), F32),
        shape((span, width), F32), shape((rows, width), BF16),
    ]
    return pl.pallas_call(
        functools.partial(trunk_kernel, columns, width, hidden, micros),
        out_shape=outs,
        in_specs=[vmem] * 3 + [hbm] * 14 + [vmem] * 4 + [smem],
        out_specs=[vmem] * len(outs),
        scratch_shapes=[space((units + 1, size, width), BF16 if size >= 16 else F32) for size in sizes] + [
            space((2,) + p.shape[1:], p.dtype) for p in own[:3]] + [
            space((2, units, width, width), BF16),
            space((2, rows, width), BF16), space((2, rows, 3 * width), BF16), space((2, rows, width), BF16),
            space((2, rows, width), BF16), space((2, rows, width), BF16), space((2, rows, hidden), BF16),
            space((2, rows, hidden), BF16), space((2, rows, width), BF16),
            space((rows, width), BF16), space((rows, width), BF16), space((2, rows, width), F32),
            space((2, rows // LANES, 8 * HEADS, LANES), F32), space((rows, width), BF16), space((rows, width), BF16),
            space((2, 8, width), F32), space((2, 1, hidden), F32), space((rows // 8, width), BF16),
            space((units + 1, 2 * piece, width) if sizes[-1] < 16 else (8, LANES), F32),
            space((units, width, width), BF16), space((width, width), BF16),
            space((3 + 2 * bits, 8, hidden // 2), F32), space((2, entries // 2, width), BF16),
            space((entries, out_width), BF16), space((columns * capacity, rows), BF16), space((2, rows, width), BF16),
            space((columns, 2 * capacity, width), BF16), space((columns, 2 * capacity, width), BF16),
            sem((micros,)), sem((micros,)), sem((micros,)), sem((micros,)), sem((3 + units, 2)),
            sem((units,)), sem((units,)), sem((bits, units + 1)), sem((bits, units + 1)),
            sem((3 + 2 * bits,)), sem((3 + 2 * bits,)), sem((3,)), sem((2,)), sem((columns - 1,)), sem((columns,)),
            sem((2,)), sem((2,)),
        ],
        compiler_params=pltpu.CompilerParams(collective_id=1, has_side_effects=True, vmem_limit_bytes=VMEM_BYTES),
    )(x0, counts, pool_grad, *own, *theirs, cot, proj, picks, ids_all, vocab)


def local(table, piece_ids, piece_counts, vocab_size, norm_gain, shift_bias, up_bias, qkv_weight, out_weight,
          up_weight, down_weight, proj_weight, embed_cotangent):
    section = lax.axis_index("section")
    columns = lax.axis_size("dp")
    core = lax.rem(section, 2)
    entries, pieces = piece_ids.shape
    half = entries // 2
    ids = piece_ids.reshape(2, half * pieces)
    my_counts = lax.dynamic_slice_in_dim(piece_counts, core * half, half, 0)
    count_rows = jnp.repeat(my_counts, pieces).reshape(-1, LANES)
    own = (norm_gain, shift_bias, up_bias[:, None, :], qkv_weight, out_weight, up_weight, down_weight)
    x0, picks, ids_all, most, pool_grad, *theirs = lookup(
        columns, ids, table, embed_cotangent, proj_weight, vocab_size, *own)
    capacity = picks.shape[0] // (2 * columns)
    turns = (most[0, 0].astype(jnp.int32) + capacity - 1) // capacity
    x0 = lax.fori_loop(
        1, turns, lambda turn, x: x + more_lookup(columns, turn.reshape(1), ids_all, table), x0)
    emb, g_gain, g_shift, g_bias, g_qkv, g_out, g_up, g_down, g_proj, g_table, dx = trunk(
        columns, x0, count_rows, pool_grad, own, theirs, embed_cotangent, proj_weight, picks, ids_all, table.shape[0],
        vocab_size)
    g_table = lax.fori_loop(
        1, turns, lambda turn, held: more_return(columns, turn.reshape(1), ids_all, dx, held), g_table)
    return emb, g_table, g_gain, g_shift, g_bias, g_qkv, g_out, g_up, g_down, g_proj


def solution(mesh):
    return jax.shard_map(
        local,
        mesh=mesh,
        in_specs=(
            P(("section", "dp"), None), P("dp", None), P("dp"), P(), P("section", None, None),
            P("section", None, None), P("section", None), P("section", None, None), P("section", None, None),
            P("section", None, None), P("section", None, None), P(None, "section"), P("dp", "section"),
        ),
        out_specs=(
            P("dp", "section"), P(("section", "dp"), None), P("section", None, "dp"), P("section", None, "dp"),
            P("section", "dp"), P("section", "dp", None), P("section", "dp", None), P("section", "dp", None),
            P("section", "dp", None), P("dp", "section"),
        ),
        check_vma=False,
    )
```

```python
import functools
import jax
import jax.numpy as jnp
from jax import lax
from jax.experimental import pallas as pl
from jax.experimental.pallas import tpu as pltpu
from jax.sharding import PartitionSpec as P

HEADS = 8
LANES = 128
EPSILON = 1e-05
MASKED = -1e30
ROOT_HALF = 0.7071067811865476
DENSITY_SCALE = 0.3989422804014327
MESH = pl.DeviceIdType.MESH
F32 = jnp.float32
BF16 = jnp.bfloat16
MICRO = 256
VMEM_BYTES = 60 * 2**20


def dot_nn(left, right):
    return lax.dot_general(left, right, (((1,), (0,)), ((), ())), preferred_element_type=F32)


def dot_nt(left, right):
    return lax.dot_general(left, right, (((1,), (1,)), ((), ())), preferred_element_type=F32)


def dot_tn(left, right):
    return lax.dot_general(left, right, (((0,), (0,)), ((), ())), preferred_element_type=F32)


def statistics(values):
    centered = values - jnp.mean(values, axis=-1, keepdims=True)
    inverse = lax.rsqrt(jnp.mean(centered * centered, axis=-1, keepdims=True) + EPSILON)
    return centered * inverse, inverse


def norm_backward(weighted, normed, inverse):
    return inverse * (
        weighted
        - jnp.mean(weighted, axis=-1, keepdims=True)
        - normed * jnp.mean(weighted * normed, axis=-1, keepdims=True)
    )


def column_sum(values):
    return jnp.sum(values, axis=0, keepdims=True)


def entry_masks():
    lane = lax.broadcasted_iota(jnp.int32, (8, LANES), 1) // 8
    return [lane == e for e in range(LANES // 8)]


def compress(tall, masks):
    tall = tall.reshape(2, LANES // 8, 8, LANES)
    kept = []
    for h in range(2):
        one = tall[h, 0]
        for e in range(1, LANES // 8):
            one = jnp.where(masks[e], tall[h, e], one)
        kept.append(one)
    return kept


def expand(flat, masks):
    zero = jnp.zeros_like(flat)
    return jnp.concatenate([jnp.where(mask, flat, zero) for mask in masks], axis=0).astype(BF16)


def half_masks():
    lane = lax.broadcasted_iota(jnp.int32, (1, LANES), 1)
    low = jnp.where(lane < LANES // 2, 1.0, 0.0)
    return low.astype(BF16), (1.0 - low).astype(BF16)


def by_head(pair, halves):
    return jnp.concatenate([pair * halves[0], pair * halves[1]], axis=0)


def head_mask(count_row):
    return lax.broadcasted_iota(jnp.int32, (8, LANES), 0) < count_row


def pool_matrix(count_row):
    lane = lax.broadcasted_iota(jnp.int32, (LANES // 8, LANES), 1)
    entry = lax.broadcasted_iota(jnp.int32, (LANES // 8, LANES), 0)
    return jnp.where((lane // 8 == entry) & (lane % 8 < count_row), 1.0, 0.0)


def capacity_of(slots, owners):
    return max(16, -(-2 * slots // owners // 16) * 16)


def ones_where(condition):
    return jnp.where(condition, 1.0, 0.0).astype(BF16)


def iota(shape, axis):
    return lax.broadcasted_iota(jnp.int32, shape, axis)


def positions(used):
    rows = min(LANES, used.shape[0])
    chunks = used.shape[0] // rows
    through = ones_where(iota((LANES, LANES), 0) <= iota((LANES, LANES), 1))
    above = ones_where(
        (iota((rows, rows), 0) // 8 == iota((rows, rows), 1) // 8) & (iota((rows, rows), 1) < iota((rows, rows), 0)))
    every = jnp.ones((LANES, LANES), BF16)
    out = []
    for chunk in range(chunks):
        part = used[chunk * rows:(chunk + 1) * rows, :].astype(BF16)
        before = dot_nn(dot_nn(above, part).astype(BF16), every)
        out.append(dot_nn(part, through) + before)
    return jnp.concatenate(out, axis=0)


def in_round(place, used, turn, capacity):
    place = place - (turn * capacity).astype(F32)
    return jnp.where((used > 0) & (place >= 1) & (place <= capacity), place, 0.0)


def owner_plan(ids_all, picks, used_rows, base, span, turn, capacity, lists):
    slots = ids_all.shape[2]
    blocks = -(-span // LANES)

    def count(d, carry):
        rel = ids_all[d // 2, pl.ds(lax.rem(d, 2), 1), :] - base
        high = jnp.where((rel >= 0) & (rel < span), rel >> 7, -1)
        counts = dot_nt(ones_where(iota((8, slots), 0) == high), ones_where(iota((LANES, slots), 0) == (rel & 127)))
        used_rows[pl.ds(pl.multiple_of(d * 8, 8), 8), :] = jnp.where(counts > 0, 1.0, 0.0)
        return carry

    lax.fori_loop(0, lists, count, 0)
    used = used_rows[pl.ds(0, lists * 8), :]
    used_rows[pl.ds(0, lists * 8), :] = in_round(positions(used), used, turn, capacity)

    def spread(d, carry):
        place = used_rows[pl.ds(pl.multiple_of(d * 8, 8), 8), :]
        wanted = (iota((capacity, LANES), 0) + 1).astype(F32)
        for block in range(blocks):
            picks[pl.ds(pl.multiple_of(d * capacity, 16), capacity), block * LANES:(block + 1) * LANES] = ones_where(
                place[block:block + 1, :] == wanted)
        return carry

    lax.fori_loop(0, lists, spread, 0)


def slot_codes(ids_row, span, first):
    value = ids_row.astype(F32)
    owner = jnp.floor((value + 0.5) * (1.0 / span))
    rel = value - owner * span
    high = jnp.floor(rel * (1.0 / LANES))
    owner = owner - first
    return owner, owner * 8 + high, rel - high * LANES


def owner_counts(ids_row, span, first, owners):
    slots = ids_row.shape[1]
    owner, row, lane = slot_codes(ids_row, span, first.astype(F32))
    rows = ones_where(iota((owners * 8, slots), 0).astype(F32) == row)
    lanes = ones_where(iota((LANES, slots), 0).astype(F32) == lane)
    return owner, rows, lanes, jnp.where(dot_nt(rows, lanes) > 0, 1.0, 0.0)


def slot_plan(ids_row, match, span, first, owners, turn, capacity):
    slots = ids_row.shape[1]
    owner, rows, lanes, used = owner_counts(ids_row, span, first, owners)
    place = in_round(positions(used), used, turn, capacity)
    mine = jnp.sum(dot_tn(place.astype(BF16), rows) * lanes.astype(F32), axis=0, keepdims=True)
    target = jnp.where(mine > 0, owner * capacity + mine - 1, -1.0)
    for owner_at in range(0, owners, 4):
        index = (iota((4 * capacity, slots), 0) + owner_at * capacity).astype(F32)
        match[owner_at * capacity:(owner_at + 4) * capacity, :] = ones_where(index == target)


def most_distinct(ids_all, span, owners, lists):
    def one(d, most):
        _, _, _, used = owner_counts(ids_all[d // 2, pl.ds(lax.rem(d, 2), 1), :], span, jnp.int32(0), owners)
        per_row = jnp.sum(used, axis=1, keepdims=True)
        per_owner = jnp.sum(per_row.reshape(owners, 8, 1), axis=1)
        return jnp.maximum(most, jnp.max(per_owner))

    return lax.fori_loop(0, lists, one, jnp.float32(0))


def device_at(index, columns):
    return (index // columns, lax.rem(index, columns))


def remote(src, dst, send, recv, peer):
    return pltpu.make_async_remote_copy(src, dst, send, recv, device_id=peer, device_id_type=MESH)


def lookup_rounds(columns, me, packed, landed, send, recv):
    lists, owners = 2 * columns, 4 * columns

    def target(d):
        return lax.rem(d, 2) * columns + d // 2

    def copy(d):
        return remote(packed.at[d], landed.at[me], send.at[d], recv.at[me], device_at(target(d), columns))

    def start(i, carry):
        d = lax.rem(i + 2 * lax.rem(me, columns), lists)

        @pl.when(target(d) != me)
        def _():
            copy(d).start()

        @pl.when(target(d) == me)
        def _():
            landed[me] = packed[d]
        return carry

    def arrive(o, carry):
        @pl.when(o != me)
        def _():
            remote(packed.at[0], landed.at[o], send.at[0], recv.at[o], device_at(o, columns)).wait_recv()
        return carry

    def left(d, carry):
        @pl.when(target(d) != me)
        def _():
            copy(d).wait_send()
        return carry

    return (lambda: lax.fori_loop(0, lists, start, 0), lambda: lax.fori_loop(0, owners, arrive, 0),
            lambda: lax.fori_loop(0, lists, left, 0))


def return_rounds(columns, me, parts, landed, send, recv):
    lists, owners = 2 * columns, 4 * columns
    slot = lax.rem(me, columns) * 2 + me // columns

    def copy(o):
        return remote(parts.at[o], landed.at[slot], send.at[o], recv.at[slot], device_at(o, columns))

    def start(i, carry):
        o = lax.rem(i + me, owners)

        @pl.when(o != me)
        def _():
            copy(o).start()

        @pl.when(o == me)
        def _():
            landed[slot] = parts[me]
        return carry

    def arrive(d, carry):
        source = lax.rem(d, 2) * columns + d // 2

        @pl.when(source != me)
        def _():
            remote(parts.at[0], landed.at[d], send.at[0], recv.at[d], device_at(source, columns)).wait_recv()
        return carry

    def left(o, carry):
        @pl.when(o != me)
        def _():
            copy(o).wait_send()
        return carry

    return (lambda: lax.fori_loop(0, owners, start, 0), lambda: lax.fori_loop(0, lists, arrive, 0),
            lambda: lax.fori_loop(0, owners, left, 0))


def greet_all(columns, me, others):
    barrier = pltpu.get_barrier_semaphore()

    def greet(o, carry):
        @pl.when(o != me)
        def _():
            pl.semaphore_signal(barrier, inc=1, device_id=device_at(o, columns), device_id_type=MESH)
        return carry

    lax.fori_loop(0, others, greet, 0)
    return barrier


def pack_rows(table, padded, picks, packed, span, capacity, lists):
    padded[pl.ds(0, span), :] = table[...]
    for d in range(0, lists, 4):
        rows = dot_nn(picks[d * capacity:(d + 4) * capacity, :], padded[...]).astype(BF16)
        packed[d:d + 4] = rows.reshape(4, capacity, rows.shape[1])


def lookup_kernel(
    columns, capacity,
    ids, table, cot_in, proj, vocab, gain_in, shift_in, bias_in, qkv_in, out_in, up_in, down_in,
    x_out, picks, ids_all, most_out, pool_out, gain_all, shift_all, bias_all, qkv_all, out_all, up_all, down_all,
    match, used_rows, padded, packed, landed, pool_send, pool_parts,
    i_send, i_recv, t_send, t_recv, w_send, w_recv, g_send, g_recv,
):
    section = lax.axis_index("section")
    column = lax.axis_index("dp")
    core = lax.rem(section, 2)
    me = section * columns + column
    owners, lists = 4 * columns, 2 * columns
    span, width = table.shape
    entries = cot_in.shape[0]
    core_peer = (section + 1 - 2 * core, column)
    barrier = greet_all(columns, me, owners)
    ids_all[column] = ids[...]
    padded[...] = jnp.zeros_like(padded)
    pl.semaphore_wait(barrier, owners - 1)

    def ids_copy(d):
        return remote(ids, ids_all.at[column], i_send.at[d - 1], i_recv.at[column],
                      (section, lax.rem(column + d, columns)))

    for d in range(1, columns):
        ids_copy(d).start()
    pairs = ((gain_in, gain_all), (shift_in, shift_all), (bias_in, bias_all),
             (qkv_in, qkv_all), (out_in, out_all), (up_in, up_all), (down_in, down_all))
    weight_copies = [
        remote(src, dst, w_send.at[i], w_recv.at[i], core_peer) for i, (src, dst) in enumerate(pairs)]
    for copy in weight_copies:
        copy.start()

    position = column * entries + iota((entries, cot_in.shape[1]), 0)
    cot = jnp.where(position < vocab[0], cot_in[...].astype(F32), 0.0).astype(BF16)
    part = dot_nt(cot, proj[...]).astype(BF16)
    pool_send[...] = part.reshape(2, entries // 2, width)

    def pool_copy(k):
        return remote(pool_send.at[k], pool_parts.at[section], g_send.at[k], g_recv.at[section], (2 + k, column))

    for k in range(2):
        @pl.when(section != 2 + k)
        def _(k=k):
            pool_copy(k).start()

        @pl.when(section == 2 + k)
        def _(k=k):
            pool_parts[section] = pool_send[k]

    for d in range(1, columns):
        source = lax.rem(column + d, columns)
        remote(ids, ids_all.at[source], i_send.at[d - 1], i_recv.at[source], (section, source)).wait_recv()
    turn = jnp.int32(0)
    owner_plan(ids_all, picks, used_rows, me * span, span, turn, capacity, lists)
    pack_rows(table, padded, picks, packed, span, capacity, lists)
    start, arrive, left = lookup_rounds(columns, me, packed, landed, t_send, t_recv)
    start()

    @pl.when(section < 2)
    def _():
        slot_plan(ids_all[column, pl.ds(core, 1), :], match, span, jnp.int32(0), owners, turn, capacity)

    most_out[0] = most_distinct(ids_all, span, owners, lists).astype(jnp.int32)

    @pl.when(section >= 2)
    def _():
        total = pool_parts[section].astype(F32)
        for d in range(1, 4):
            source = lax.rem(section + d, 4)
            remote(pool_send.at[0], pool_parts.at[source], g_send.at[0], g_recv.at[source],
                   (source, column)).wait_recv()
            total = total + pool_parts[source].astype(F32)
        pool_out[...] = total

    @pl.when(section < 2)
    def _():
        arrive()
        x_out[...] = dot_tn(match[...], landed[...].reshape(owners * capacity, width)).astype(BF16)

    left()
    for k in range(2):
        @pl.when(section != 2 + k)
        def _(k=k):
            pool_copy(k).wait_send()
    for d in range(1, columns):
        ids_copy(d).wait_send()
    for copy in weight_copies:
        copy.wait()


def lookup(columns, ids, table, cot, proj, vocab, gain, shift, bias, w_qkv, w_out, w_up, w_down):
    slots = ids.shape[1]
    span, width = table.shape
    owners, lists = 4 * columns, 2 * columns
    capacity = capacity_of(slots, owners)
    padded_span = -(-span // LANES) * LANES
    entries = cot.shape[0]
    vmem = pl.BlockSpec(memory_space=pltpu.VMEM)
    smem = pl.BlockSpec(memory_space=pltpu.SMEM)
    hbm = pl.BlockSpec(memory_space=pl.ANY)
    shape = jax.ShapeDtypeStruct
    params = (gain, shift, bias, w_qkv, w_out, w_up, w_down)
    outs = [
        shape((slots, width), BF16), shape((lists * capacity, padded_span), BF16), shape((columns, 2, slots), jnp.int32), shape((1,), jnp.int32),
        shape((entries // 2, width), F32),
    ] + [shape(p.shape, p.dtype) for p in params]
    sem = pltpu.SemaphoreType.DMA
    return pl.pallas_call(
        functools.partial(lookup_kernel, columns, capacity),
        out_shape=outs,
        in_specs=[vmem] * 4 + [smem] + [hbm] * 7,
        out_specs=[vmem] * 3 + [smem, vmem] + [hbm] * 7,
        scratch_shapes=[
            pltpu.VMEM((owners * capacity, slots), BF16),
            pltpu.VMEM((max(lists, owners) * 8, LANES), F32), pltpu.VMEM((padded_span, width), BF16),
            pltpu.VMEM((lists, capacity, width), BF16), pltpu.VMEM((owners, capacity, width), BF16),
            pltpu.VMEM((2, entries // 2, width), BF16), pltpu.VMEM((4, entries // 2, width), BF16),
            sem((columns - 1,)), sem((columns,)), sem((lists,)), sem((owners,)), sem((7,)), sem((7,)),
            sem((2,)), sem((4,)),
        ],
        compiler_params=pltpu.CompilerParams(collective_id=3, has_side_effects=True, vmem_limit_bytes=VMEM_BYTES),
    )(ids, table, cot, proj, vocab, *params)


def more_lookup_kernel(columns, capacity, turn, ids_all, table, x_out, match, picks, used_rows, padded, packed, landed,
                       t_send, t_recv):
    section = lax.axis_index("section")
    column = lax.axis_index("dp")
    me = section * columns + column
    owners, lists = 4 * columns, 2 * columns
    span, width = table.shape
    barrier = pltpu.get_barrier_semaphore()

    @pl.when(section < 2)
    def _():
        greet_all(columns, me, owners)
        pl.semaphore_wait(barrier, lists - 1)

    @pl.when(section >= 2)
    def _():
        pl.semaphore_wait(barrier, lists)

    padded[...] = jnp.zeros_like(padded)
    owner_plan(ids_all, picks, used_rows, me * span, span, turn[0], capacity, lists)
    pack_rows(table, padded, picks, packed, span, capacity, lists)
    start, arrive, left = lookup_rounds(columns, me, packed, landed, t_send, t_recv)
    start()
    x_out[...] = jnp.zeros_like(x_out)

    @pl.when(section < 2)
    def _():
        slot_plan(ids_all[column, pl.ds(lax.rem(section, 2), 1), :], match, span, jnp.int32(0), owners, turn[0], capacity)
        arrive()
        x_out[...] = dot_tn(match[...], landed[...].reshape(owners * capacity, width)).astype(BF16)

    left()


def more_lookup(columns, turn, ids_all, table):
    slots = ids_all.shape[2]
    span, width = table.shape
    owners, lists = 4 * columns, 2 * columns
    capacity = capacity_of(slots, owners)
    padded_span = -(-span // LANES) * LANES
    vmem = pl.BlockSpec(memory_space=pltpu.VMEM)
    sem = pltpu.SemaphoreType.DMA
    return pl.pallas_call(
        functools.partial(more_lookup_kernel, columns, capacity),
        out_shape=jax.ShapeDtypeStruct((slots, width), BF16),
        in_specs=[pl.BlockSpec(memory_space=pltpu.SMEM), vmem, vmem],
        out_specs=vmem,
        scratch_shapes=[
            pltpu.VMEM((owners * capacity, slots), BF16), pltpu.VMEM((lists * capacity, padded_span), BF16),
            pltpu.VMEM((max(lists, owners) * 8, LANES), F32), pltpu.VMEM((padded_span, width), BF16),
            pltpu.VMEM((lists, capacity, width), BF16), pltpu.VMEM((owners, capacity, width), BF16),
            sem((lists,)), sem((owners,)),
        ],
        compiler_params=pltpu.CompilerParams(collective_id=4, has_side_effects=True, vmem_limit_bytes=VMEM_BYTES),
    )(turn, ids_all, table)


def return_parts(match, dx, parts, owners, capacity):
    for o in range(0, owners, 4):
        rows = dot_nn(match[o * capacity:(o + 4) * capacity, :], dx[...]).astype(BF16)
        parts[o:o + 4] = rows.reshape(4, capacity, rows.shape[1])


def more_return_kernel(columns, capacity, turn, ids_all, dx, held, grad_out, match, picks, used_rows, parts, landed,
                       t_send, t_recv):
    section = lax.axis_index("section")
    column = lax.axis_index("dp")
    me = section * columns + column
    owners, lists = 4 * columns, 2 * columns
    span, width = held.shape
    slots = ids_all.shape[2]
    barrier = greet_all(columns, me, lists)

    @pl.when(section < 2)
    def _():
        pl.semaphore_wait(barrier, owners - 1)

    start, arrive, left = return_rounds(columns, me, parts, landed, t_send, t_recv)

    @pl.when(section < 2)
    def _():
        slot_plan(ids_all[column, pl.ds(lax.rem(section, 2), 1), :], match, span, jnp.int32(0), owners, turn[0], capacity)
        return_parts(match, dx, parts, owners, capacity)
        start()

    owner_plan(ids_all, picks, used_rows, me * span, span, turn[0], capacity, lists)
    arrive()
    grad = dot_tn(picks[...], landed[...].reshape(lists * capacity, width))
    grad_out[...] = held[...] + grad[:span]

    @pl.when(section < 2)
    def _():
        left()


def more_return(columns, turn, ids_all, dx, held):
    slots = ids_all.shape[2]
    span, width = held.shape
    owners, lists = 4 * columns, 2 * columns
    capacity = capacity_of(slots, owners)
    padded_span = -(-span // LANES) * LANES
    vmem = pl.BlockSpec(memory_space=pltpu.VMEM)
    sem = pltpu.SemaphoreType.DMA
    return pl.pallas_call(
        functools.partial(more_return_kernel, columns, capacity),
        out_shape=jax.ShapeDtypeStruct((span, width), F32),
        in_specs=[pl.BlockSpec(memory_space=pltpu.SMEM), vmem, vmem, vmem],
        out_specs=vmem,
        scratch_shapes=[
            pltpu.VMEM((owners * capacity, slots), BF16), pltpu.VMEM((lists * capacity, padded_span), BF16),
            pltpu.VMEM((max(lists, owners) * 8, LANES), F32),
            pltpu.VMEM((owners, capacity, width), BF16), pltpu.VMEM((lists, capacity, width), BF16),
            sem((owners,)), sem((lists,)),
        ],
        compiler_params=pltpu.CompilerParams(collective_id=5, has_side_effects=True, vmem_limit_bytes=VMEM_BYTES),
    )(turn, ids_all, dx, held)


PHASE_LAG = 2
PROJECT_AFTER = 5
ADD_LAG = 1
VEC_GAP = 4
SEND_NEAR = 1
SEND_FAR = 8
TABLE_STEP = 13
SWAPPED = (3, 7, 11)


def unit_order(u, bits):
    order = list(range(bits))
    if u in SWAPPED and bits > 1:
        order[0], order[1] = 1, 0
    return order


def slot_in(order, q):
    slot = 0
    for bit in order:
        slot = slot * 2 + (q >> bit) % 2
    return slot


def trunk_kernel(columns, width, hidden, micros, *refs):
    (x0, counts, pool_grad), refs = refs[:3], refs[3:]
    own, theirs, refs = refs[:7], refs[7:14], refs[14:]
    (cot_in, proj, picks, ids_all, vocab), refs = refs[:5], refs[5:]
    (emb_out, gain_out, shift_out, upb_out, qkv_out, out_out, up_out, down_out, proj_out, table_out, dx_out), refs = (
        refs[:11], refs[11:])
    bits = columns.bit_length() - 1
    recv, refs = refs[:bits], refs[bits:]
    (gains, shifts, up_bias, w_all, a, dqkv, att, dbr, h_in_all, dpre, act_all, dy_all,
     x_in, x_mid, resid, prob, y_out, dy_in, vec, upb, pooled,
     wide, s0_recv, proj_sums, v_buf, pool_all, cot, match, dxs, parts, landed,
     f_send, f_recv, b_send, b_recv, p_sem,
     c_send, c_recv, h_send, h_recv, v_send, v_recv, q_send, q_recv, t_send, t_recv, d_send, d_recv) = refs
    section = lax.axis_index("section")
    column = lax.axis_index("dp")
    core = lax.rem(section, 2)
    stage = section // 2
    core_peer = (section + 1 - 2 * core, column)
    far_peer = (lax.rem(section + 2, 4), column)
    blocks = MICRO // LANES
    score_scale = (width // HEADS) ** (-0.5)
    piece = width // columns
    tiles = hidden // width
    units = 4 + 2 * tiles
    first_down = 4 + tiles
    capacity = parts.shape[1] // 2
    lists = 2 * columns

    def tile_of(source, u):
        if u < 3:
            return source[3].at[0, :, u * width:(u + 1) * width]
        if u == 3:
            return source[4].at[0]
        if u < first_down:
            return source[5].at[0, :, (u - 4) * width:(u - 3) * width]
        return source[6].at[0, (u - first_down) * width:(u - first_down + 1) * width, :]

    def fetch(i, source, layer):
        src = source[i].at[0] if i < 3 else tile_of(source, i - 3)
        dst = (gains, shifts, up_bias)[i].at[layer] if i < 3 else w_all.at[layer, i - 3]
        return pltpu.make_async_copy(src, dst, p_sem.at[i, layer])

    for first in range(2):
        @pl.when(core == first)
        def _(first=first):
            for layer in range(2):
                for i in (0, 1, 3, 4, 5, 6, 2, *range(7, 3 + units)):
                    fetch(i, own if layer == first else theirs, layer).start()

    def need(m, layer, *indices):
        @pl.when(m == 0)
        def _():
            for i in indices:
                fetch(i, own, layer).wait()

    def section_peer(d):
        return (lax.rem(section + d, 4), column)

    def column_peer(d):
        return (section, lax.rem(column + d, columns))

    peers = [section_peer(d) for d in range(1, 4)] + [column_peer(d) for d in range(1, columns)]
    barrier = pltpu.get_barrier_semaphore()
    for peer in peers:
        pl.semaphore_signal(barrier, inc=1, device_id=peer, device_id_type=MESH)
    vec[...] = jnp.zeros_like(vec)
    upb[...] = jnp.zeros_like(upb)

    @pl.when(stage == 0)
    def _():
        x_in[...] = x0[...]

    pl.semaphore_wait(barrier, len(peers))

    def rows_of(m):
        return pl.ds(pl.multiple_of(m * MICRO, MICRO), MICRO)

    def forward_copy(m):
        return remote(y_out.at[rows_of(m)], x_in.at[rows_of(m)], f_send.at[m], f_recv.at[m], far_peer)

    def backward_copy(m):
        return remote(y_out.at[rows_of(m)], dy_in.at[rows_of(m)], b_send.at[m], b_recv.at[m], far_peer)

    def count_row(m, b):
        return counts[pl.ds(m * blocks + b, 1), :]

    def layer_forward(layer, m, x):
        rows = rows_of(m)
        masks, halves = entry_masks(), half_masks()
        xf = x.astype(F32)
        normed, _ = statistics(xf)
        need(m, layer, 0, 1, 3, 4, 5)
        a_low = (normed * gains[layer, pl.ds(0, 1), :] + shifts[layer, pl.ds(0, 1), :]).astype(BF16)
        a[layer, rows, :] = a_low
        for t in range(3):
            cols = slice(t * width, (t + 1) * width)
            dqkv[layer, rows, cols] = dot_nn(a_low, w_all[layer, t]).astype(BF16)
        for b in range(blocks):
            block = pl.ds(pl.multiple_of(m * MICRO + b * LANES, LANES), LANES)
            keys_on = head_mask(count_row(m, b))
            for pair in range(HEADS // 2):
                cols = slice(pair * LANES, (pair + 1) * LANES)
                q = dqkv[layer, block, cols]
                k = dqkv[layer, block, slice(width + pair * LANES, width + (pair + 1) * LANES)]
                v = dqkv[layer, block, slice(2 * width + pair * LANES, 2 * width + (pair + 1) * LANES)]
                flats = compress(dot_nt(by_head(k, halves), q), masks)
                wide = []
                for h in range(2):
                    s = jnp.where(keys_on, flats[h] * score_scale, MASKED)
                    e = jnp.exp(s - jnp.max(s, axis=0, keepdims=True))
                    p = e / jnp.sum(e, axis=0, keepdims=True)
                    prob[layer, m * blocks + b, pl.ds((2 * pair + h) * 8, 8), :] = p
                    wide.append(expand(p, masks))
                mixed = dot_tn(jnp.concatenate(wide, axis=0), by_head(v, halves))
                att[layer, block, cols] = mixed.astype(BF16)
        need(m, layer, 6)
        res = xf + dot_nn(att[layer, rows, :], w_all[layer, 3]) + shifts[layer, pl.ds(1, 1), :]
        resid[layer, rows, :] = res
        normed_two, _ = statistics(res)
        h_in = (normed_two * gains[layer, pl.ds(1, 1), :] + shifts[layer, pl.ds(2, 1), :]).astype(BF16)
        h_in_all[layer, rows, :] = h_in
        need(m, layer, 2, *range(7, 3 + units))
        total = res + shifts[layer, pl.ds(3, 1), :]
        for t in range(tiles):
            cols = slice(t * width, (t + 1) * width)
            pre = dot_nn(h_in, w_all[layer, 4 + t]) + up_bias[layer, :, cols]
            dpre[layer, rows, cols] = pre.astype(BF16)
            act = (pre * (0.5 * (1.0 + lax.erf(pre * ROOT_HALF)))).astype(BF16)
            total = total + dot_nn(act, w_all[layer, first_down + t])
        return total.astype(BF16)

    def layer_backward(layer, m, dy):
        rows = rows_of(m)
        masks, halves = entry_masks(), half_masks()
        dyf = dy.astype(F32)
        vec[layer, pl.ds(5, 1), :] += column_sum(dyf)
        d_hidden = jnp.zeros((MICRO, width), F32)
        for t in range(tiles):
            cols = slice(t * width, (t + 1) * width)
            d_act = dot_nt(dy, w_all[layer, first_down + t])
            pre = dpre[layer, rows, cols].astype(F32)
            phi = 0.5 * (1.0 + lax.erf(pre * ROOT_HALF))
            density = jnp.exp(-0.5 * pre * pre) * DENSITY_SCALE
            act_all[layer, rows, cols] = (pre * phi).astype(BF16)
            d_pre = (d_act * (phi + pre * density)).astype(BF16)
            dpre[layer, rows, cols] = d_pre
            upb[layer, :, cols] += column_sum(d_pre.astype(F32))
            d_hidden = d_hidden + dot_nt(d_pre, w_all[layer, 4 + t])
        normed_two, inverse_two = statistics(resid[layer, rows, :])
        vec[layer, pl.ds(1, 1), :] += column_sum(d_hidden * normed_two)
        vec[layer, pl.ds(4, 1), :] += column_sum(d_hidden)
        d_resid = dyf + norm_backward(d_hidden * gains[layer, pl.ds(1, 1), :], normed_two, inverse_two)
        d_branch = d_resid.astype(BF16)
        dbr[layer, rows, :] = d_branch
        vec[layer, pl.ds(3, 1), :] += column_sum(d_branch.astype(F32))
        d_att = dot_nt(d_branch, w_all[layer, 3]).astype(BF16)
        for b in range(blocks):
            block = pl.ds(pl.multiple_of(m * MICRO + b * LANES, LANES), LANES)
            for pair in range(HEADS // 2):
                c_q = slice(pair * LANES, (pair + 1) * LANES)
                c_k = slice(width + pair * LANES, width + (pair + 1) * LANES)
                c_v = slice(2 * width + pair * LANES, 2 * width + (pair + 1) * LANES)
                q = dqkv[layer, block, c_q]
                k = dqkv[layer, block, c_k]
                v = dqkv[layer, block, c_v]
                da = d_att[b * LANES:(b + 1) * LANES, c_q]
                flats = compress(dot_nt(by_head(v, halves), da), masks)
                wide_p, wide_s = [], []
                for h in range(2):
                    p = prob[layer, m * blocks + b, pl.ds((2 * pair + h) * 8, 8), :]
                    ds = p * (flats[h] - jnp.sum(flats[h] * p, axis=0, keepdims=True))
                    wide_p.append(expand(p, masks))
                    wide_s.append(expand(ds, masks))
                d_v = dot_nn(jnp.concatenate(wide_p, axis=1), by_head(da, halves))
                d_k = dot_nn(jnp.concatenate(wide_s, axis=1), by_head(q, halves)) * score_scale
                d_q = dot_tn(jnp.concatenate(wide_s, axis=0), by_head(k, halves)) * score_scale
                dqkv[layer, block, c_q] = d_q.astype(BF16)
                dqkv[layer, block, c_k] = d_k.astype(BF16)
                dqkv[layer, block, c_v] = d_v.astype(BF16)
        d_a = jnp.zeros((MICRO, width), F32)
        for t in range(3):
            cols = slice(t * width, (t + 1) * width)
            d_a = d_a + dot_nt(dqkv[layer, rows, cols], w_all[layer, t])
        x = jnp.where(layer == 0, x_in[rows, :], x_mid[rows, :])
        normed, inverse = statistics(x.astype(F32))
        vec[layer, pl.ds(0, 1), :] += column_sum(d_a * normed)
        vec[layer, pl.ds(2, 1), :] += column_sum(d_a)
        dx = d_resid + norm_backward(d_a * gains[layer, pl.ds(0, 1), :], normed, inverse)
        return dx.astype(BF16)


    def forward_layer(layer, m, x):
        @pl.when(layer == 1)
        def _():
            x_mid[rows_of(m), :] = x

        return layer_forward(layer, m, x)

    def forward_step(m, carry):
        rows = rows_of(m)

        @pl.when(stage == 1)
        def _():
            forward_copy(m).wait_recv()

        x = lax.fori_loop(0, 2, lambda layer, x: forward_layer(layer, m, x), x_in[rows, :])
        y_out[rows, :] = x

        @pl.when(stage == 0)
        def _():
            forward_copy(m).start()

        @pl.when(stage == 1)
        def _():
            for b in range(blocks):
                matrix = pool_matrix(count_row(m, b))
                summed = dot_nn(matrix.astype(BF16), x[b * LANES:(b + 1) * LANES, :])
                mean = summed / jnp.sum(matrix, axis=1, keepdims=True)
                entries = pl.ds(pl.multiple_of((m * blocks + b) * (LANES // 8), LANES // 8), LANES // 8)
                pooled[entries, :] = mean.astype(BF16)
        return carry

    lax.fori_loop(0, micros, forward_step, 0)

    def my_bit(b):
        return lax.rem(column // (1 << b), 2)

    def bit_peer(b):
        return (section, column + (1 << b) - my_bit(b) * (2 << b))

    def pool_copy(d):
        return remote(pooled, pool_all.at[core], q_send.at[d - 1], q_recv.at[core], section_peer(d))

    def pool_arrival(k):
        return remote(pooled, pool_all.at[k], q_send.at[0], q_recv.at[k], core_peer)

    @pl.when(stage == 1)
    def _():
        for d in range(1, 4):
            pool_copy(d).start()
        pool_all[core] = pooled[...]

    @pl.when(stage == 0)
    def _():
        for m in range(micros):
            forward_copy(m).wait_send()

    def core_copy(u):
        return remote(w_all.at[1 - core, u], s0_recv.at[u], c_send.at[u], c_recv.at[u], core_peer)

    def is_wide(k):
        return k < bits and (columns >> (k + 1)) * piece < 16

    def source_of(u, k):
        if is_wide(k):
            return wide.at[u]
        if k > 0:
            return recv[k - 1].at[u]
        return w_all.at[core, u] if u < units else proj_sums

    def side_rows(k, side):
        size = (columns >> (k + 1)) * piece
        return pl.ds(pl.multiple_of(side * size, size), size)

    def halving_copy(u, k):
        bit = unit_order(u, bits)[k]
        return remote(source_of(u, k).at[side_rows(k, 1 - my_bit(bit))], recv[k].at[u], h_send.at[k, u],
                      h_recv.at[k, u], bit_peer(bit))

    def absorb(u, k):
        halving_copy(u, k).wait_recv()
        bit = unit_order(u, bits)[k]
        return recv[k][u].astype(F32) + source_of(u, k)[side_rows(k, my_bit(bit)), :].astype(F32)

    def advance(u, k):
        if k < bits - 1:
            if is_wide(k + 1):
                wide[u] = absorb(u, k)
            else:
                recv[k][u] = absorb(u, k).astype(BF16)
            halving_copy(u, k + 1).start()
        else:
            finish(u, absorb(u, k))

    def cut(value, q):
        return value[q * piece:(q + 1) * piece, :]

    def rows_at(u, q):
        slot = slot_in(unit_order(u, bits), q)
        return slice(slot * piece, (slot + 1) * piece)

    def product(layer, u):
        if u < 3:
            return dot_tn(a[layer], dqkv[layer, :, u * width:(u + 1) * width])
        if u == 3:
            return dot_tn(att[layer], dbr[layer])
        t = u - 4
        return dot_tn(h_in_all[layer], dpre[layer, :, t * width:(t + 1) * width])

    def send_or_add(layer, u):
        @pl.when(core != layer)
        def _():
            core_copy(u).start()

        if u >= ADD_LAG:
            @pl.when(core == layer)
            def _():
                add_own(u - ADD_LAG)

    def add_own(u):
        core_copy(u).wait_recv()
        w_all[core, u] = (w_all[core, u].astype(F32) + s0_recv[u].astype(F32)).astype(BF16)
        halving_copy(u, 0).start()

    def weight_gradients(layer):
        for u in range(first_down):
            value = product(layer, u).astype(BF16)
            for q in range(columns):
                w_all[layer, u, rows_at(u, q), :] = cut(value, q)
            send_or_add(layer, u)
        for i in range(tiles):
            value = dot_tn(act_all[layer, :, i * width:(i + 1) * width], dy_all[layer]).astype(BF16)
            for j in range(columns):
                u, q = first_down + j % tiles, i * columns // tiles + j // tiles
                w_all[layer, u, rows_at(u, q), :] = cut(value, j)
        for u in range(first_down, units):
            send_or_add(layer, u)

        @pl.when(core == layer)
        def _():
            for u in range(units - ADD_LAG, units):
                add_own(u)

    def project():
        @pl.when(section >= 2)
        def _():
            pool_arrival(1 - core).wait_recv()

        @pl.when(section < 2)
        def _():
            pool_arrival(0).wait_recv()
            pool_arrival(1).wait_recv()

        entries = cot_in.shape[0]
        position = column * entries + iota((entries, cot_in.shape[1]), 0)
        live = position < vocab[0]
        cot[...] = jnp.where(live, cot_in[...].astype(F32), 0.0).astype(BF16)
        rows = pool_all[...].reshape(entries, width)
        emb_out[...] = jnp.where(live, dot_nn(rows, proj[...]), 0.0)
        value = dot_tn(rows, cot[...]).astype(BF16)
        for q in range(columns):
            proj_sums[rows_at(units, q), :] = cut(value, q)

        halving_copy(units, 0).start()

    def project_now():
        project()
        for k in range(bits):
            advance(units, k)

    def put_vec(slot, layer):
        v_buf[slot, :, slice(0, width)] = vec[layer]
        for t in range(2):
            v_buf[slot, pl.ds(6 + t, 1), :] = upb[layer, :, t * (hidden // 2):(t + 1) * (hidden // 2)]

    def vec_copy(src, index, peer):
        return remote(v_buf.at[src], v_buf.at[index], v_send.at[index], v_recv.at[index], peer)

    def vec_peer_copy(k):
        return vec_copy(1 + 2 * k + (k > 0), 3 + 2 * k, bit_peer(k))

    def share_copy(half, way, peer):
        return remote(dxs.at[half], dxs.at[half], d_send.at[way], d_recv.at[half], peer)

    def finish(u, total):
        if u < 3:
            qkv_out[0, :, u * width:(u + 1) * width] = total
        elif u == 3:
            out_out[0] = total
        elif u < first_down:
            up_out[0, :, (u - 4) * width:(u - 3) * width] = total
        elif u < units:
            t = u - first_down
            down_out[0, t * piece:(t + 1) * piece, :] = total
        else:
            proj_out[...] = total

    def vec_step(k):
        if k == 0:
            put_vec(0, 1 - core)
            put_vec(1, core)
            vec_copy(0, 2, core_peer).start()
            vec_copy(0, 2, core_peer).wait_recv()
            v_buf[1] = v_buf[1] + v_buf[2]
            vec_peer_copy(0).start()
            return
        vec_peer_copy(k - 1).wait_recv()
        source = 1 + 2 * (k - 1) + (k > 1)
        total = v_buf[source] + v_buf[3 + 2 * (k - 1)]
        if k < bits:
            v_buf[2 * k + 2] = total
            vec_peer_copy(k).start()
            return
        lanes = width // columns
        share = hidden // columns
        for q in range(columns):
            @pl.when(column == q)
            def _(q=q):
                gain_out[0] = total[0:2, q * lanes:(q + 1) * lanes]
                shift_out[0] = total[2:6, q * lanes:(q + 1) * lanes]
                row, start = divmod(q * share, hidden // 2)
                upb_out[...] = total[6 + row:7 + row, start:start + share]

    def table_copy(d):
        peer = column_peer(d)
        return remote(parts.at[peer[1]], landed.at[column], t_send.at[d - 1], t_recv.at[column], peer)

    def table_parts():
        share_copy(1 - core, 0, core_peer).wait_recv()
        for half in range(2):
            slot_plan(ids_all[column, pl.ds(half, 1), :], match, table_out.shape[0], section * columns, columns,
                      jnp.int32(0), capacity)
            rows = dot_nn(match[...], dxs[half]).astype(BF16)
            parts[:, half * capacity:(half + 1) * capacity, :] = rows.reshape(columns, capacity, width)
        for d in range(1, columns):
            table_copy(d).start()
        landed[column] = parts[column]

    def table_finish():
        for d in range(1, columns):
            source = lax.rem(column + d, columns)
            remote(parts.at[0], landed.at[source], t_send.at[0], t_recv.at[source], (section, source)).wait_recv()
        grad = dot_tn(picks[...], landed[...].reshape(lists * capacity, width))
        table_out[...] = grad[:table_out.shape[0]]

    pl.when(stage == 0)(project_now)

    def seed(m):
        rows = rows_of(m)

        @pl.when(stage == 0)
        def _():
            backward_copy(m).wait_recv()
            dy_all[1, rows, :] = dy_in[rows, :]

        @pl.when(stage == 1)
        def _():
            for b in range(blocks):
                matrix = pool_matrix(count_row(m, b))
                entries = pl.ds(pl.multiple_of((m * blocks + b) * (LANES // 8), LANES // 8), LANES // 8)
                share = (pool_grad[entries, :] / jnp.sum(matrix, axis=1, keepdims=True)).astype(BF16)
                block = pl.ds(pl.multiple_of(m * MICRO + b * LANES, LANES), LANES)
                dy_all[1, block, :] = dot_tn(matrix.astype(BF16), share).astype(BF16)

    def backward(layer, m):
        rows = rows_of(m)
        dx = layer_backward(layer, m, dy_all[layer, rows, :])

        @pl.when(layer == 1)
        def _():
            dy_all[0, rows, :] = dx

        @pl.when(layer == 0)
        def _():
            dx_out[rows, :] = dx
            dxs[core, rows, :] = dx

        @pl.when((layer == 0) & (stage == 1))
        def _():
            y_out[rows, :] = dx
            backward_copy(m).start()

    last = micros - 1

    def backward_step(i, carry):
        m, turn = jnp.minimum(i // 2, last), i - 2 * jnp.minimum(i // 2, last)

        @pl.when(turn == 0)
        def _():
            seed(m)

        @pl.when(turn < 2)
        def _():
            backward(1 - turn, m)

        layer = 1 - turn + stage

        @pl.when((m == last) & (turn == 1) & (stage == 0))
        def _():
            share_copy(core, 0, core_peer).start()
            share_copy(core, 1, far_peer).start()

        @pl.when((m == last) & (layer >= 0) & (layer < 2))
        def _():
            weight_gradients(layer)
        return carry

    lax.fori_loop(0, 2 * micros + 1, backward_step, 0)

    lags = [PHASE_LAG * k for k in range(bits)]
    for step in range(units + lags[-1]):
        if step == SEND_NEAR:
            pl.when(section < 2)(table_parts)
        if step == SEND_FAR - 1:
            @pl.when(section >= 2)
            def _():
                share_copy(core, 0, far_peer).wait_recv()
                share_copy(core, 0, core_peer).start()
        if step == SEND_FAR:
            pl.when(section >= 2)(table_parts)
        if step == TABLE_STEP:
            table_finish()
        if step % VEC_GAP == 0 and step // VEC_GAP <= bits:
            vec_step(step // VEC_GAP)
        if step == 0:
            pl.when(stage == 1)(project)
        for k in range(bits):
            u = step - lags[k]
            if 0 <= u < units:
                advance(u, k)
            if u == PROJECT_AFTER:
                @pl.when(stage == 1)
                def _(k=k):
                    advance(units, k)
    for k in range((units + lags[-1] - 1) // VEC_GAP + 1, bits + 1):
        vec_step(k)

    @pl.when(stage == 1)
    def _():
        for m in range(micros):
            backward_copy(m).wait_send()

    vec_copy(0, 2, core_peer).wait_send()
    for k in range(bits):
        vec_peer_copy(k).wait_send()
    for u in range(units):
        core_copy(u).wait_send()
    for u in range(units + 1):
        for k in range(bits):
            halving_copy(u, k).wait_send()
    for d in range(1, columns):
        table_copy(d).wait_send()
    share_copy(core, 0, core_peer).wait_send()

    @pl.when(section < 2)
    def _():
        share_copy(core, 1, far_peer).wait_send()

    @pl.when(section >= 2)
    def _():
        for d in range(1, 4):
            pool_copy(d).wait_send()


def deliver_kernel(*refs):
    count = (len(refs) - 2) // 3
    sources, targets, staged = refs[:count], refs[count:2 * count], refs[2 * count:3 * count]
    in_sem, out_sem = refs[3 * count:]
    arrivals = [pltpu.make_async_copy(sources[i], staged[i], in_sem.at[i]) for i in range(count)]
    departures = [pltpu.make_async_copy(staged[i], targets[i], out_sem.at[i]) for i in range(count)]
    for copy in arrivals:
        copy.start()
    for arrival, departure in zip(arrivals, departures):
        arrival.wait()
        departure.start()
    for copy in departures:
        copy.wait()


def deliver(*values):
    count = len(values)
    hbm = pl.BlockSpec(memory_space=pl.ANY)
    size = sum(4 * value.size for value in values)
    return pl.pallas_call(
        deliver_kernel,
        out_shape=[jax.ShapeDtypeStruct(value.shape, value.dtype) for value in values],
        in_specs=[hbm] * count,
        out_specs=[hbm] * count,
        scratch_shapes=[pltpu.VMEM(value.shape, value.dtype) for value in values] + [
            pltpu.SemaphoreType.DMA((count,)), pltpu.SemaphoreType.DMA((count,))],
        cost_estimate=pl.CostEstimate(flops=0, bytes_accessed=2 * size, transcendentals=0),
        compiler_params=pltpu.CompilerParams(vmem_limit_bytes=VMEM_BYTES),
    )(*values)


def trunk(columns, x0, counts, pool_grad, own, theirs, cot, proj, picks, ids_all, span, vocab):
    rows, width = x0.shape
    hidden = own[5].shape[2]
    micros = rows // MICRO
    entries, out_width = cot.shape
    piece, tiles = width // columns, hidden // width
    bits = columns.bit_length() - 1
    units = 4 + 2 * tiles
    sizes = [(columns >> (k + 1)) * piece for k in range(bits)]
    capacity = picks.shape[0] // (2 * columns)
    vmem = pl.BlockSpec(memory_space=pltpu.VMEM)
    smem = pl.BlockSpec(memory_space=pltpu.SMEM)
    hbm = pl.BlockSpec(memory_space=pl.ANY)
    shape, sem, space = jax.ShapeDtypeStruct, pltpu.SemaphoreType.DMA, pltpu.VMEM
    outs = [
        shape((entries, out_width), F32), shape((1, 2, piece), F32), shape((1, 4, piece), F32),
        shape((1, hidden // columns), F32), shape((1, piece, 3 * width), F32), shape((1, piece, width), F32),
        shape((1, piece, hidden), F32), shape((1, tiles * piece, width), F32), shape((piece, out_width), F32),
        shape((span, width), F32), shape((rows, width), BF16),
    ]
    return pl.pallas_call(
        functools.partial(trunk_kernel, columns, width, hidden, micros),
        out_shape=outs,
        in_specs=[vmem] * 3 + [hbm] * 14 + [vmem] * 4 + [smem],
        out_specs=[vmem] * len(outs),
        scratch_shapes=[space((units + 1, size, width), BF16 if size >= 16 else F32) for size in sizes] + [
            space((2,) + p.shape[1:], p.dtype) for p in own[:3]] + [
            space((2, units, width, width), BF16),
            space((2, rows, width), BF16), space((2, rows, 3 * width), BF16), space((2, rows, width), BF16),
            space((2, rows, width), BF16), space((2, rows, width), BF16), space((2, rows, hidden), BF16),
            space((2, rows, hidden), BF16), space((2, rows, width), BF16),
            space((rows, width), BF16), space((rows, width), BF16), space((2, rows, width), F32),
            space((2, rows // LANES, 8 * HEADS, LANES), F32), space((rows, width), BF16), space((rows, width), BF16),
            space((2, 8, width), F32), space((2, 1, hidden), F32), space((rows // 8, width), BF16),
            space((units + 1, 2 * piece, width) if sizes[-1] < 16 else (8, LANES), F32),
            space((units, width, width), BF16), space((width, width), BF16),
            space((3 + 2 * bits, 8, hidden // 2), F32), space((2, entries // 2, width), BF16),
            space((entries, out_width), BF16), space((columns * capacity, rows), BF16), space((2, rows, width), BF16),
            space((columns, 2 * capacity, width), BF16), space((columns, 2 * capacity, width), BF16),
            sem((micros,)), sem((micros,)), sem((micros,)), sem((micros,)), sem((3 + units, 2)),
            sem((units,)), sem((units,)), sem((bits, units + 1)), sem((bits, units + 1)),
            sem((3 + 2 * bits,)), sem((3 + 2 * bits,)), sem((3,)), sem((2,)), sem((columns - 1,)), sem((columns,)),
            sem((2,)), sem((2,)),
        ],
        compiler_params=pltpu.CompilerParams(collective_id=1, has_side_effects=True, vmem_limit_bytes=VMEM_BYTES),
    )(x0, counts, pool_grad, *own, *theirs, cot, proj, picks, ids_all, vocab)


def local(table, piece_ids, piece_counts, vocab_size, norm_gain, shift_bias, up_bias, qkv_weight, out_weight,
          up_weight, down_weight, proj_weight, embed_cotangent):
    section = lax.axis_index("section")
    columns = lax.axis_size("dp")
    core = lax.rem(section, 2)
    entries, pieces = piece_ids.shape
    half = entries // 2
    ids = piece_ids.reshape(2, half * pieces)
    my_counts = lax.dynamic_slice_in_dim(piece_counts, core * half, half, 0)
    count_rows = jnp.repeat(my_counts, pieces).reshape(-1, LANES)
    own = (norm_gain, shift_bias, up_bias[:, None, :], qkv_weight, out_weight, up_weight, down_weight)
    x0, picks, ids_all, most, pool_grad, *theirs = lookup(
        columns, ids, table, embed_cotangent, proj_weight, vocab_size, *own)
    capacity = picks.shape[0] // (2 * columns)
    turns = (most[0] + capacity - 1) // capacity
    x0 = lax.fori_loop(
        1, turns, lambda turn, x: x + more_lookup(columns, turn.reshape(1), ids_all, table), x0)
    emb, g_gain, g_shift, g_bias, g_qkv, g_out, g_up, g_down, g_proj, g_table, dx = trunk(
        columns, x0, count_rows, pool_grad, own, theirs, embed_cotangent, proj_weight, picks, ids_all, table.shape[0],
        vocab_size)
    g_table = lax.fori_loop(
        1, turns, lambda turn, held: more_return(columns, turn.reshape(1), ids_all, dx, held), g_table)
    return tuple(deliver(emb, g_table, g_gain, g_shift, g_bias, g_qkv, g_out, g_up, g_down, g_proj))


def solution(mesh):
    return jax.shard_map(
        local,
        mesh=mesh,
        in_specs=(
            P(("section", "dp"), None), P("dp", None), P("dp"), P(), P("section", None, None),
            P("section", None, None), P("section", None), P("section", None, None), P("section", None, None),
            P("section", None, None), P("section", None, None), P(None, "section"), P("dp", "section"),
        ),
        out_specs=(
            P("dp", "section"), P(("section", "dp"), None), P("section", None, "dp"), P("section", None, "dp"),
            P("section", "dp"), P("section", "dp", None), P("section", "dp", None), P("section", "dp", None),
            P("section", "dp", None), P("dp", "section"),
        ),
        check_vma=False,
    )
```

```python
import functools
import jax
import jax.numpy as jnp
from jax import lax
from jax.experimental import pallas as pl
from jax.experimental.pallas import tpu as pltpu
from jax.sharding import PartitionSpec as P

HEADS = 8
LANES = 128
EPSILON = 1e-05
MASKED = -1e30
ROOT_HALF = 0.7071067811865476
DENSITY_SCALE = 0.3989422804014327
MESH = pl.DeviceIdType.MESH
F32 = jnp.float32
BF16 = jnp.bfloat16
MICRO = 256
VMEM_BYTES = 60 * 2**20


def dot_nn(left, right):
    return lax.dot_general(left, right, (((1,), (0,)), ((), ())), preferred_element_type=F32)


def dot_nt(left, right):
    return lax.dot_general(left, right, (((1,), (1,)), ((), ())), preferred_element_type=F32)


def dot_tn(left, right):
    return lax.dot_general(left, right, (((0,), (0,)), ((), ())), preferred_element_type=F32)


def statistics(values):
    centered = values - jnp.mean(values, axis=-1, keepdims=True)
    inverse = lax.rsqrt(jnp.mean(centered * centered, axis=-1, keepdims=True) + EPSILON)
    return centered * inverse, inverse


def norm_backward(weighted, normed, inverse):
    return inverse * (
        weighted
        - jnp.mean(weighted, axis=-1, keepdims=True)
        - normed * jnp.mean(weighted * normed, axis=-1, keepdims=True)
    )


def column_sum(values):
    return jnp.sum(values, axis=0, keepdims=True)


def entry_masks():
    lane = lax.broadcasted_iota(jnp.int32, (8, LANES), 1) // 8
    return [lane == e for e in range(LANES // 8)]


def compress(tall, masks):
    tall = tall.reshape(2, LANES // 8, 8, LANES)
    kept = []
    for h in range(2):
        one = tall[h, 0]
        for e in range(1, LANES // 8):
            one = jnp.where(masks[e], tall[h, e], one)
        kept.append(one)
    return kept


def expand(flat, masks):
    zero = jnp.zeros_like(flat)
    return jnp.concatenate([jnp.where(mask, flat, zero) for mask in masks], axis=0).astype(BF16)


def half_masks():
    lane = lax.broadcasted_iota(jnp.int32, (1, LANES), 1)
    low = jnp.where(lane < LANES // 2, 1.0, 0.0)
    return low.astype(BF16), (1.0 - low).astype(BF16)


def by_head(pair, halves):
    return jnp.concatenate([pair * halves[0], pair * halves[1]], axis=0)


def head_mask(count_row):
    return lax.broadcasted_iota(jnp.int32, (8, LANES), 0) < count_row


def pool_matrix(count_row):
    lane = lax.broadcasted_iota(jnp.int32, (LANES // 8, LANES), 1)
    entry = lax.broadcasted_iota(jnp.int32, (LANES // 8, LANES), 0)
    return jnp.where((lane // 8 == entry) & (lane % 8 < count_row), 1.0, 0.0)


def capacity_of(slots, owners):
    return max(16, -(-2 * slots // owners // 16) * 16)


def ones_where(condition):
    return jnp.where(condition, 1.0, 0.0).astype(BF16)


def iota(shape, axis):
    return lax.broadcasted_iota(jnp.int32, shape, axis)


def positions(used):
    rows = min(LANES, used.shape[0])
    chunks = used.shape[0] // rows
    through = ones_where(iota((LANES, LANES), 0) <= iota((LANES, LANES), 1))
    above = ones_where(
        (iota((rows, rows), 0) // 8 == iota((rows, rows), 1) // 8) & (iota((rows, rows), 1) < iota((rows, rows), 0)))
    every = jnp.ones((LANES, LANES), BF16)
    out = []
    for chunk in range(chunks):
        part = used[chunk * rows:(chunk + 1) * rows, :].astype(BF16)
        before = dot_nn(dot_nn(above, part).astype(BF16), every)
        out.append(dot_nn(part, through) + before)
    return jnp.concatenate(out, axis=0)


def in_round(place, used, turn, capacity):
    place = place - (turn * capacity).astype(F32)
    return jnp.where((used > 0) & (place >= 1) & (place <= capacity), place, 0.0)


def owner_plan(ids_all, picks, used_rows, base, span, turn, capacity, lists):
    slots = ids_all.shape[2]
    blocks = -(-span // LANES)

    def count(d, carry):
        rel = ids_all[d // 2, pl.ds(lax.rem(d, 2), 1), :] - base
        high = jnp.where((rel >= 0) & (rel < span), rel >> 7, -1)
        counts = dot_nt(ones_where(iota((8, slots), 0) == high), ones_where(iota((LANES, slots), 0) == (rel & 127)))
        used_rows[pl.ds(pl.multiple_of(d * 8, 8), 8), :] = jnp.where(counts > 0, 1.0, 0.0)
        return carry

    lax.fori_loop(0, lists, count, 0, unroll=8)
    used = used_rows[pl.ds(0, lists * 8), :]
    used_rows[pl.ds(0, lists * 8), :] = in_round(positions(used), used, turn, capacity)

    def spread(d, carry):
        place = used_rows[pl.ds(pl.multiple_of(d * 8, 8), 8), :]
        wanted = (iota((capacity, LANES), 0) + 1).astype(F32)
        for block in range(blocks):
            picks[pl.ds(pl.multiple_of(d * capacity, 16), capacity), block * LANES:(block + 1) * LANES] = ones_where(
                place[block:block + 1, :] == wanted)
        return carry

    lax.fori_loop(0, lists, spread, 0, unroll=8)


def slot_codes(ids_row, span, first):
    value = ids_row.astype(F32)
    owner = jnp.floor((value + 0.5) * (1.0 / span))
    rel = value - owner * span
    high = jnp.floor(rel * (1.0 / LANES))
    owner = owner - first
    return owner, owner * 8 + high, rel - high * LANES


def owner_counts(ids_row, span, first, owners):
    slots = ids_row.shape[1]
    owner, row, lane = slot_codes(ids_row, span, first.astype(F32))
    rows = ones_where(iota((owners * 8, slots), 0).astype(F32) == row)
    lanes = ones_where(iota((LANES, slots), 0).astype(F32) == lane)
    return owner, rows, lanes, jnp.where(dot_nt(rows, lanes) > 0, 1.0, 0.0)


def slot_plan(ids_row, match, span, first, owners, turn, capacity):
    slots = ids_row.shape[1]
    owner, rows, lanes, used = owner_counts(ids_row, span, first, owners)
    place = in_round(positions(used), used, turn, capacity)
    mine = jnp.sum(dot_tn(place.astype(BF16), rows) * lanes.astype(F32), axis=0, keepdims=True)
    target = jnp.where(mine > 0, owner * capacity + mine - 1, -1.0)
    for owner_at in range(0, owners, 4):
        index = (iota((4 * capacity, slots), 0) + owner_at * capacity).astype(F32)
        match[owner_at * capacity:(owner_at + 4) * capacity, :] = ones_where(index == target)


def most_distinct(ids_all, span, owners, lists):
    def one(d, most):
        _, _, _, used = owner_counts(ids_all[d // 2, pl.ds(lax.rem(d, 2), 1), :], span, jnp.int32(0), owners)
        per_row = jnp.sum(used, axis=1, keepdims=True)
        per_owner = jnp.sum(per_row.reshape(owners, 8, 1), axis=1)
        return jnp.maximum(most, jnp.max(per_owner))

    return lax.fori_loop(0, lists, one, jnp.float32(0))


def device_at(index, columns):
    return (index // columns, lax.rem(index, columns))


def remote(src, dst, send, recv, peer):
    return pltpu.make_async_remote_copy(src, dst, send, recv, device_id=peer, device_id_type=MESH)


def lookup_rounds(columns, me, packed, landed, send, recv):
    lists, owners = 2 * columns, 4 * columns

    def target(d):
        return lax.rem(d, 2) * columns + d // 2

    def copy(d):
        return remote(packed.at[d], landed.at[me], send.at[d], recv.at[me], device_at(target(d), columns))

    def start(i, carry):
        d = lax.rem(i + 2 * lax.rem(me, columns), lists)

        @pl.when(target(d) != me)
        def _():
            copy(d).start()

        @pl.when(target(d) == me)
        def _():
            landed[me] = packed[d]
        return carry

    def arrive(o, carry):
        @pl.when(o != me)
        def _():
            remote(packed.at[0], landed.at[o], send.at[0], recv.at[o], device_at(o, columns)).wait_recv()
        return carry

    def left(d, carry):
        @pl.when(target(d) != me)
        def _():
            copy(d).wait_send()
        return carry

    return (lambda: lax.fori_loop(0, lists, start, 0), lambda: lax.fori_loop(0, owners, arrive, 0),
            lambda: lax.fori_loop(0, lists, left, 0))


def return_rounds(columns, me, parts, landed, send, recv):
    lists, owners = 2 * columns, 4 * columns
    slot = lax.rem(me, columns) * 2 + me // columns

    def copy(o):
        return remote(parts.at[o], landed.at[slot], send.at[o], recv.at[slot], device_at(o, columns))

    def start(i, carry):
        o = lax.rem(i + me, owners)

        @pl.when(o != me)
        def _():
            copy(o).start()

        @pl.when(o == me)
        def _():
            landed[slot] = parts[me]
        return carry

    def arrive(d, carry):
        source = lax.rem(d, 2) * columns + d // 2

        @pl.when(source != me)
        def _():
            remote(parts.at[0], landed.at[d], send.at[0], recv.at[d], device_at(source, columns)).wait_recv()
        return carry

    def left(o, carry):
        @pl.when(o != me)
        def _():
            copy(o).wait_send()
        return carry

    return (lambda: lax.fori_loop(0, owners, start, 0), lambda: lax.fori_loop(0, lists, arrive, 0),
            lambda: lax.fori_loop(0, owners, left, 0))


def greet_all(columns, me, others):
    barrier = pltpu.get_barrier_semaphore()

    def greet(o, carry):
        @pl.when(o != me)
        def _():
            pl.semaphore_signal(barrier, inc=1, device_id=device_at(o, columns), device_id_type=MESH)
        return carry

    lax.fori_loop(0, others, greet, 0)
    return barrier


def pack_rows(padded, picks, packed, capacity, lists):
    for d in range(0, lists, 4):
        rows = dot_nn(picks[d * capacity:(d + 4) * capacity, :], padded[...]).astype(BF16)
        packed[d:d + 4] = rows.reshape(4, capacity, rows.shape[1])


def lookup_kernel(
    columns, capacity,
    ids, table, cot_in, proj, vocab, gain_in, shift_in, bias_in, qkv_in, out_in, up_in, down_in,
    x_out, picks, ids_all, most_out, pool_out, gain_all, shift_all, bias_all, qkv_all, out_all, up_all, down_all,
    match, used_rows, padded, packed, landed, pool_send, pool_parts,
    i_send, i_recv, t_send, t_recv, w_send, w_recv, g_send, g_recv,
):
    section = lax.axis_index("section")
    column = lax.axis_index("dp")
    core = lax.rem(section, 2)
    me = section * columns + column
    owners, lists = 4 * columns, 2 * columns
    span, width = table.shape
    entries = cot_in.shape[0]
    core_peer = (section + 1 - 2 * core, column)
    barrier = greet_all(columns, me, owners)
    ids_all[column] = ids[...]
    padded[...] = jnp.zeros_like(padded)
    padded[pl.ds(0, span), :] = table[...]
    pl.semaphore_wait(barrier, owners - 1)

    def ids_copy(d):
        return remote(ids, ids_all.at[column], i_send.at[d - 1], i_recv.at[column],
                      (section, lax.rem(column + d, columns)))

    for d in range(1, columns):
        ids_copy(d).start()
    pairs = ((gain_in, gain_all), (shift_in, shift_all), (bias_in, bias_all),
             (qkv_in, qkv_all), (out_in, out_all), (up_in, up_all), (down_in, down_all))
    weight_copies = [
        remote(src, dst, w_send.at[i], w_recv.at[i], core_peer) for i, (src, dst) in enumerate(pairs)]
    for copy in weight_copies:
        copy.start()

    position = column * entries + iota((entries, cot_in.shape[1]), 0)
    cot = jnp.where(position < vocab[0], cot_in[...].astype(F32), 0.0).astype(BF16)
    part = dot_nt(cot, proj[...]).astype(BF16)
    pool_send[...] = part.reshape(2, entries // 2, width)

    def pool_copy(k):
        return remote(pool_send.at[k], pool_parts.at[section], g_send.at[k], g_recv.at[section], (2 + k, column))

    for k in range(2):
        @pl.when(section != 2 + k)
        def _(k=k):
            pool_copy(k).start()

        @pl.when(section == 2 + k)
        def _(k=k):
            pool_parts[section] = pool_send[k]

    for d in range(1, columns):
        source = lax.rem(column + d, columns)
        remote(ids, ids_all.at[source], i_send.at[d - 1], i_recv.at[source], (section, source)).wait_recv()
    turn = jnp.int32(0)
    owner_plan(ids_all, picks, used_rows, me * span, span, turn, capacity, lists)
    pack_rows(padded, picks, packed, capacity, lists)
    start, arrive, left = lookup_rounds(columns, me, packed, landed, t_send, t_recv)
    start()

    @pl.when(section < 2)
    def _():
        slot_plan(ids_all[column, pl.ds(core, 1), :], match, span, jnp.int32(0), owners, turn, capacity)

    most_out[0] = most_distinct(ids_all, span, owners, lists).astype(jnp.int32)

    @pl.when(section >= 2)
    def _():
        total = pool_parts[section].astype(F32)
        for d in range(1, 4):
            source = lax.rem(section + d, 4)
            remote(pool_send.at[0], pool_parts.at[source], g_send.at[0], g_recv.at[source],
                   (source, column)).wait_recv()
            total = total + pool_parts[source].astype(F32)
        pool_out[...] = total

    @pl.when(section < 2)
    def _():
        arrive()
        x_out[...] = dot_tn(match[...], landed[...].reshape(owners * capacity, width)).astype(BF16)

    left()
    for k in range(2):
        @pl.when(section != 2 + k)
        def _(k=k):
            pool_copy(k).wait_send()
    for d in range(1, columns):
        ids_copy(d).wait_send()
    for copy in weight_copies:
        copy.wait()


def lookup(columns, ids, table, cot, proj, vocab, gain, shift, bias, w_qkv, w_out, w_up, w_down):
    slots = ids.shape[1]
    span, width = table.shape
    owners, lists = 4 * columns, 2 * columns
    capacity = capacity_of(slots, owners)
    padded_span = -(-span // LANES) * LANES
    entries = cot.shape[0]
    vmem = pl.BlockSpec(memory_space=pltpu.VMEM)
    smem = pl.BlockSpec(memory_space=pltpu.SMEM)
    hbm = pl.BlockSpec(memory_space=pl.ANY)
    shape = jax.ShapeDtypeStruct
    params = (gain, shift, bias, w_qkv, w_out, w_up, w_down)
    outs = [
        shape((slots, width), BF16), shape((lists * capacity, padded_span), BF16), shape((columns, 2, slots), jnp.int32), shape((1,), jnp.int32),
        shape((entries // 2, width), F32),
    ] + [shape(p.shape, p.dtype) for p in params]
    sem = pltpu.SemaphoreType.DMA
    return pl.pallas_call(
        functools.partial(lookup_kernel, columns, capacity),
        out_shape=outs,
        in_specs=[vmem] * 4 + [smem] + [hbm] * 7,
        out_specs=[vmem] * 3 + [smem, vmem] + [hbm] * 7,
        scratch_shapes=[
            pltpu.VMEM((owners * capacity, slots), BF16),
            pltpu.VMEM((max(lists, owners) * 8, LANES), F32), pltpu.VMEM((padded_span, width), BF16),
            pltpu.VMEM((lists, capacity, width), BF16), pltpu.VMEM((owners, capacity, width), BF16),
            pltpu.VMEM((2, entries // 2, width), BF16), pltpu.VMEM((4, entries // 2, width), BF16),
            sem((columns - 1,)), sem((columns,)), sem((lists,)), sem((owners,)), sem((7,)), sem((7,)),
            sem((2,)), sem((4,)),
        ],
        compiler_params=pltpu.CompilerParams(collective_id=3, has_side_effects=True, vmem_limit_bytes=VMEM_BYTES),
    )(ids, table, cot, proj, vocab, *params)


def more_lookup_kernel(columns, capacity, turn, ids_all, table, x_out, match, picks, used_rows, padded, packed, landed,
                       t_send, t_recv):
    section = lax.axis_index("section")
    column = lax.axis_index("dp")
    me = section * columns + column
    owners, lists = 4 * columns, 2 * columns
    span, width = table.shape
    barrier = pltpu.get_barrier_semaphore()

    @pl.when(section < 2)
    def _():
        greet_all(columns, me, owners)
        pl.semaphore_wait(barrier, lists - 1)

    @pl.when(section >= 2)
    def _():
        pl.semaphore_wait(barrier, lists)

    padded[...] = jnp.zeros_like(padded)
    padded[pl.ds(0, span), :] = table[...]
    owner_plan(ids_all, picks, used_rows, me * span, span, turn[0], capacity, lists)
    pack_rows(padded, picks, packed, capacity, lists)
    start, arrive, left = lookup_rounds(columns, me, packed, landed, t_send, t_recv)
    start()
    x_out[...] = jnp.zeros_like(x_out)

    @pl.when(section < 2)
    def _():
        slot_plan(ids_all[column, pl.ds(lax.rem(section, 2), 1), :], match, span, jnp.int32(0), owners, turn[0], capacity)
        arrive()
        x_out[...] = dot_tn(match[...], landed[...].reshape(owners * capacity, width)).astype(BF16)

    left()


def more_lookup(columns, turn, ids_all, table):
    slots = ids_all.shape[2]
    span, width = table.shape
    owners, lists = 4 * columns, 2 * columns
    capacity = capacity_of(slots, owners)
    padded_span = -(-span // LANES) * LANES
    vmem = pl.BlockSpec(memory_space=pltpu.VMEM)
    sem = pltpu.SemaphoreType.DMA
    return pl.pallas_call(
        functools.partial(more_lookup_kernel, columns, capacity),
        out_shape=jax.ShapeDtypeStruct((slots, width), BF16),
        in_specs=[pl.BlockSpec(memory_space=pltpu.SMEM), vmem, vmem],
        out_specs=vmem,
        scratch_shapes=[
            pltpu.VMEM((owners * capacity, slots), BF16), pltpu.VMEM((lists * capacity, padded_span), BF16),
            pltpu.VMEM((max(lists, owners) * 8, LANES), F32), pltpu.VMEM((padded_span, width), BF16),
            pltpu.VMEM((lists, capacity, width), BF16), pltpu.VMEM((owners, capacity, width), BF16),
            sem((lists,)), sem((owners,)),
        ],
        compiler_params=pltpu.CompilerParams(collective_id=4, has_side_effects=True, vmem_limit_bytes=VMEM_BYTES),
    )(turn, ids_all, table)


def return_parts(match, dx, parts, owners, capacity):
    for o in range(0, owners, 4):
        rows = dot_nn(match[o * capacity:(o + 4) * capacity, :], dx[...]).astype(BF16)
        parts[o:o + 4] = rows.reshape(4, capacity, rows.shape[1])


def more_return_kernel(columns, capacity, turn, ids_all, dx, held, grad_out, match, picks, used_rows, parts, landed,
                       t_send, t_recv):
    section = lax.axis_index("section")
    column = lax.axis_index("dp")
    me = section * columns + column
    owners, lists = 4 * columns, 2 * columns
    span, width = held.shape
    slots = ids_all.shape[2]
    barrier = greet_all(columns, me, lists)

    @pl.when(section < 2)
    def _():
        pl.semaphore_wait(barrier, owners - 1)

    start, arrive, left = return_rounds(columns, me, parts, landed, t_send, t_recv)

    @pl.when(section < 2)
    def _():
        slot_plan(ids_all[column, pl.ds(lax.rem(section, 2), 1), :], match, span, jnp.int32(0), owners, turn[0], capacity)
        return_parts(match, dx, parts, owners, capacity)
        start()

    owner_plan(ids_all, picks, used_rows, me * span, span, turn[0], capacity, lists)
    arrive()
    grad = dot_tn(picks[...], landed[...].reshape(lists * capacity, width))
    grad_out[...] = held[...] + grad[:span]

    @pl.when(section < 2)
    def _():
        left()


def more_return(columns, turn, ids_all, dx, held):
    slots = ids_all.shape[2]
    span, width = held.shape
    owners, lists = 4 * columns, 2 * columns
    capacity = capacity_of(slots, owners)
    padded_span = -(-span // LANES) * LANES
    vmem = pl.BlockSpec(memory_space=pltpu.VMEM)
    sem = pltpu.SemaphoreType.DMA
    return pl.pallas_call(
        functools.partial(more_return_kernel, columns, capacity),
        out_shape=jax.ShapeDtypeStruct((span, width), F32),
        in_specs=[pl.BlockSpec(memory_space=pltpu.SMEM), vmem, vmem, vmem],
        out_specs=vmem,
        scratch_shapes=[
            pltpu.VMEM((owners * capacity, slots), BF16), pltpu.VMEM((lists * capacity, padded_span), BF16),
            pltpu.VMEM((max(lists, owners) * 8, LANES), F32),
            pltpu.VMEM((owners, capacity, width), BF16), pltpu.VMEM((lists, capacity, width), BF16),
            sem((owners,)), sem((lists,)),
        ],
        compiler_params=pltpu.CompilerParams(collective_id=5, has_side_effects=True, vmem_limit_bytes=VMEM_BYTES),
    )(turn, ids_all, dx, held)


PHASE_LAG = 2
PROJECT_AFTER = 5
ADD_LAG = 1
VEC_GAP = 4
SEND_NEAR = 1
SEND_FAR = 8
TABLE_STEP = 13
SWAPPED = (3, 7, 11)


def unit_order(u, bits):
    order = list(range(bits))
    if u in SWAPPED and bits > 1:
        order[0], order[1] = 1, 0
    return order


def slot_in(order, q):
    slot = 0
    for bit in order:
        slot = slot * 2 + (q >> bit) % 2
    return slot


def trunk_kernel(columns, width, hidden, micros, *refs):
    (x0, counts, pool_grad), refs = refs[:3], refs[3:]
    own, theirs, refs = refs[:7], refs[7:14], refs[14:]
    (cot_in, proj, picks, ids_all, vocab), refs = refs[:5], refs[5:]
    (emb_out, gain_out, shift_out, upb_out, qkv_out, out_out, up_out, down_out, proj_out, table_out, dx_out), refs = (
        refs[:11], refs[11:])
    bits = columns.bit_length() - 1
    recv, refs = refs[:bits], refs[bits:]
    (gains, shifts, up_bias, w_all, a, dqkv, att, dbr, h_in_all, dpre, act_all, dy_all,
     x_in, x_mid, resid, prob, y_out, dy_in, vec, upb, pooled,
     wide, s0_recv, proj_sums, v_buf, pool_all, cot, match, dxs, parts, landed,
     f_send, f_recv, b_send, b_recv, p_sem,
     c_send, c_recv, h_send, h_recv, v_send, v_recv, q_send, q_recv, t_send, t_recv, d_send, d_recv) = refs
    section = lax.axis_index("section")
    column = lax.axis_index("dp")
    core = lax.rem(section, 2)
    stage = section // 2
    core_peer = (section + 1 - 2 * core, column)
    far_peer = (lax.rem(section + 2, 4), column)
    blocks = MICRO // LANES
    score_scale = (width // HEADS) ** (-0.5)
    piece = width // columns
    tiles = hidden // width
    units = 4 + 2 * tiles
    first_down = 4 + tiles
    capacity = parts.shape[1] // 2
    lists = 2 * columns

    def tile_of(source, u):
        if u < 3:
            return source[3].at[0, :, u * width:(u + 1) * width]
        if u == 3:
            return source[4].at[0]
        if u < first_down:
            return source[5].at[0, :, (u - 4) * width:(u - 3) * width]
        return source[6].at[0, (u - first_down) * width:(u - first_down + 1) * width, :]

    def fetch(i, source, layer):
        src = source[i].at[0] if i < 3 else tile_of(source, i - 3)
        dst = (gains, shifts, up_bias)[i].at[layer] if i < 3 else w_all.at[layer, i - 3]
        return pltpu.make_async_copy(src, dst, p_sem.at[i, layer])

    for first in range(2):
        @pl.when(core == first)
        def _(first=first):
            for layer in range(2):
                for i in (0, 1, 3, 4, 5, 6, 2, *range(7, 3 + units)):
                    fetch(i, own if layer == first else theirs, layer).start()

    def need(m, layer, *indices):
        @pl.when(m == 0)
        def _():
            for i in indices:
                fetch(i, own, layer).wait()

    def section_peer(d):
        return (lax.rem(section + d, 4), column)

    def column_peer(d):
        return (section, lax.rem(column + d, columns))

    peers = [section_peer(d) for d in range(1, 4)] + [column_peer(d) for d in range(1, columns)]
    barrier = pltpu.get_barrier_semaphore()
    for peer in peers:
        pl.semaphore_signal(barrier, inc=1, device_id=peer, device_id_type=MESH)
    vec[...] = jnp.zeros_like(vec)
    upb[...] = jnp.zeros_like(upb)

    @pl.when(stage == 0)
    def _():
        x_in[...] = x0[...]

    pl.semaphore_wait(barrier, len(peers))

    def rows_of(m):
        return pl.ds(pl.multiple_of(m * MICRO, MICRO), MICRO)

    def forward_copy(m):
        return remote(y_out.at[rows_of(m)], x_in.at[rows_of(m)], f_send.at[m], f_recv.at[m], far_peer)

    def backward_copy(m):
        return remote(y_out.at[rows_of(m)], dy_in.at[rows_of(m)], b_send.at[m], b_recv.at[m], far_peer)

    def count_row(m, b):
        return counts[pl.ds(m * blocks + b, 1), :]

    def layer_forward(layer, m, x):
        rows = rows_of(m)
        masks, halves = entry_masks(), half_masks()
        xf = x.astype(F32)
        normed, _ = statistics(xf)
        need(m, layer, 0, 1, 3, 4, 5)
        a_low = (normed * gains[layer, pl.ds(0, 1), :] + shifts[layer, pl.ds(0, 1), :]).astype(BF16)
        a[layer, rows, :] = a_low
        for t in range(3):
            cols = slice(t * width, (t + 1) * width)
            dqkv[layer, rows, cols] = dot_nn(a_low, w_all[layer, t]).astype(BF16)
        for b in range(blocks):
            block = pl.ds(pl.multiple_of(m * MICRO + b * LANES, LANES), LANES)
            keys_on = head_mask(count_row(m, b))
            for pair in range(HEADS // 2):
                cols = slice(pair * LANES, (pair + 1) * LANES)
                q = dqkv[layer, block, cols]
                k = dqkv[layer, block, slice(width + pair * LANES, width + (pair + 1) * LANES)]
                v = dqkv[layer, block, slice(2 * width + pair * LANES, 2 * width + (pair + 1) * LANES)]
                flats = compress(dot_nt(by_head(k, halves), q), masks)
                wide = []
                for h in range(2):
                    s = jnp.where(keys_on, flats[h] * score_scale, MASKED)
                    e = jnp.exp(s - jnp.max(s, axis=0, keepdims=True))
                    p = e / jnp.sum(e, axis=0, keepdims=True)
                    prob[layer, m * blocks + b, pl.ds((2 * pair + h) * 8, 8), :] = p
                    wide.append(expand(p, masks))
                mixed = dot_tn(jnp.concatenate(wide, axis=0), by_head(v, halves))
                att[layer, block, cols] = mixed.astype(BF16)
        need(m, layer, 6)
        res = xf + dot_nn(att[layer, rows, :], w_all[layer, 3]) + shifts[layer, pl.ds(1, 1), :]
        resid[layer, rows, :] = res
        normed_two, _ = statistics(res)
        h_in = (normed_two * gains[layer, pl.ds(1, 1), :] + shifts[layer, pl.ds(2, 1), :]).astype(BF16)
        h_in_all[layer, rows, :] = h_in
        need(m, layer, 2, *range(7, 3 + units))
        total = res + shifts[layer, pl.ds(3, 1), :]
        for t in range(tiles):
            cols = slice(t * width, (t + 1) * width)
            pre = dot_nn(h_in, w_all[layer, 4 + t]) + up_bias[layer, :, cols]
            dpre[layer, rows, cols] = pre.astype(BF16)
            act = (pre * (0.5 * (1.0 + lax.erf(pre * ROOT_HALF)))).astype(BF16)
            total = total + dot_nn(act, w_all[layer, first_down + t])
        return total.astype(BF16)

    def layer_backward(layer, m, dy):
        rows = rows_of(m)
        masks, halves = entry_masks(), half_masks()
        dyf = dy.astype(F32)
        vec[layer, pl.ds(5, 1), :] += column_sum(dyf)
        d_hidden = jnp.zeros((MICRO, width), F32)
        for t in range(tiles):
            cols = slice(t * width, (t + 1) * width)
            d_act = dot_nt(dy, w_all[layer, first_down + t])
            pre = dpre[layer, rows, cols].astype(F32)
            phi = 0.5 * (1.0 + lax.erf(pre * ROOT_HALF))
            density = jnp.exp(-0.5 * pre * pre) * DENSITY_SCALE
            act_all[layer, rows, cols] = (pre * phi).astype(BF16)
            d_pre = (d_act * (phi + pre * density)).astype(BF16)
            dpre[layer, rows, cols] = d_pre
            upb[layer, :, cols] += column_sum(d_pre.astype(F32))
            d_hidden = d_hidden + dot_nt(d_pre, w_all[layer, 4 + t])
        normed_two, inverse_two = statistics(resid[layer, rows, :])
        vec[layer, pl.ds(1, 1), :] += column_sum(d_hidden * normed_two)
        vec[layer, pl.ds(4, 1), :] += column_sum(d_hidden)
        d_resid = dyf + norm_backward(d_hidden * gains[layer, pl.ds(1, 1), :], normed_two, inverse_two)
        d_branch = d_resid.astype(BF16)
        dbr[layer, rows, :] = d_branch
        vec[layer, pl.ds(3, 1), :] += column_sum(d_branch.astype(F32))
        d_att = dot_nt(d_branch, w_all[layer, 3]).astype(BF16)
        for b in range(blocks):
            block = pl.ds(pl.multiple_of(m * MICRO + b * LANES, LANES), LANES)
            for pair in range(HEADS // 2):
                c_q = slice(pair * LANES, (pair + 1) * LANES)
                c_k = slice(width + pair * LANES, width + (pair + 1) * LANES)
                c_v = slice(2 * width + pair * LANES, 2 * width + (pair + 1) * LANES)
                q = dqkv[layer, block, c_q]
                k = dqkv[layer, block, c_k]
                v = dqkv[layer, block, c_v]
                da = d_att[b * LANES:(b + 1) * LANES, c_q]
                flats = compress(dot_nt(by_head(v, halves), da), masks)
                wide_p, wide_s = [], []
                for h in range(2):
                    p = prob[layer, m * blocks + b, pl.ds((2 * pair + h) * 8, 8), :]
                    ds = p * (flats[h] - jnp.sum(flats[h] * p, axis=0, keepdims=True))
                    wide_p.append(expand(p, masks))
                    wide_s.append(expand(ds, masks))
                d_v = dot_nn(jnp.concatenate(wide_p, axis=1), by_head(da, halves))
                d_k = dot_nn(jnp.concatenate(wide_s, axis=1), by_head(q, halves)) * score_scale
                d_q = dot_tn(jnp.concatenate(wide_s, axis=0), by_head(k, halves)) * score_scale
                dqkv[layer, block, c_q] = d_q.astype(BF16)
                dqkv[layer, block, c_k] = d_k.astype(BF16)
                dqkv[layer, block, c_v] = d_v.astype(BF16)
        d_a = jnp.zeros((MICRO, width), F32)
        for t in range(3):
            cols = slice(t * width, (t + 1) * width)
            d_a = d_a + dot_nt(dqkv[layer, rows, cols], w_all[layer, t])
        x = jnp.where(layer == 0, x_in[rows, :], x_mid[rows, :])
        normed, inverse = statistics(x.astype(F32))
        vec[layer, pl.ds(0, 1), :] += column_sum(d_a * normed)
        vec[layer, pl.ds(2, 1), :] += column_sum(d_a)
        dx = d_resid + norm_backward(d_a * gains[layer, pl.ds(0, 1), :], normed, inverse)
        return dx.astype(BF16)


    def forward_layer(layer, m, x):
        @pl.when(layer == 1)
        def _():
            x_mid[rows_of(m), :] = x

        return layer_forward(layer, m, x)

    def forward_step(m, carry):
        rows = rows_of(m)

        @pl.when(stage == 1)
        def _():
            forward_copy(m).wait_recv()

        x = lax.fori_loop(0, 2, lambda layer, x: forward_layer(layer, m, x), x_in[rows, :])
        y_out[rows, :] = x

        @pl.when(stage == 0)
        def _():
            forward_copy(m).start()

        @pl.when(stage == 1)
        def _():
            for b in range(blocks):
                matrix = pool_matrix(count_row(m, b))
                summed = dot_nn(matrix.astype(BF16), x[b * LANES:(b + 1) * LANES, :])
                mean = summed / jnp.sum(matrix, axis=1, keepdims=True)
                entries = pl.ds(pl.multiple_of((m * blocks + b) * (LANES // 8), LANES // 8), LANES // 8)
                pooled[entries, :] = mean.astype(BF16)
        return carry

    lax.fori_loop(0, micros, forward_step, 0)

    def my_bit(b):
        return lax.rem(column // (1 << b), 2)

    def bit_peer(b):
        return (section, column + (1 << b) - my_bit(b) * (2 << b))

    def pool_copy(d):
        return remote(pooled, pool_all.at[core], q_send.at[d - 1], q_recv.at[core], section_peer(d))

    def pool_arrival(k):
        return remote(pooled, pool_all.at[k], q_send.at[0], q_recv.at[k], core_peer)

    @pl.when(stage == 1)
    def _():
        for d in range(1, 4):
            pool_copy(d).start()
        pool_all[core] = pooled[...]

    @pl.when(stage == 0)
    def _():
        for m in range(micros):
            forward_copy(m).wait_send()

    def core_copy(u):
        return remote(w_all.at[1 - core, u], s0_recv.at[u], c_send.at[u], c_recv.at[u], core_peer)

    def is_wide(k):
        return k < bits and (columns >> (k + 1)) * piece < 16

    def source_of(u, k):
        if is_wide(k):
            return wide.at[u]
        if k > 0:
            return recv[k - 1].at[u]
        return w_all.at[core, u] if u < units else proj_sums

    def side_rows(k, side):
        size = (columns >> (k + 1)) * piece
        return pl.ds(pl.multiple_of(side * size, size), size)

    def halving_copy(u, k):
        bit = unit_order(u, bits)[k]
        return remote(source_of(u, k).at[side_rows(k, 1 - my_bit(bit))], recv[k].at[u], h_send.at[k, u],
                      h_recv.at[k, u], bit_peer(bit))

    def absorb(u, k):
        halving_copy(u, k).wait_recv()
        bit = unit_order(u, bits)[k]
        return recv[k][u].astype(F32) + source_of(u, k)[side_rows(k, my_bit(bit)), :].astype(F32)

    def advance(u, k):
        if k < bits - 1:
            if is_wide(k + 1):
                wide[u] = absorb(u, k)
            else:
                recv[k][u] = absorb(u, k).astype(BF16)
            halving_copy(u, k + 1).start()
        else:
            finish(u, absorb(u, k))

    def cut(value, q):
        return value[q * piece:(q + 1) * piece, :]

    def rows_at(u, q):
        slot = slot_in(unit_order(u, bits), q)
        return slice(slot * piece, (slot + 1) * piece)

    def product(layer, u):
        if u < 3:
            return dot_tn(a[layer], dqkv[layer, :, u * width:(u + 1) * width])
        if u == 3:
            return dot_tn(att[layer], dbr[layer])
        t = u - 4
        return dot_tn(h_in_all[layer], dpre[layer, :, t * width:(t + 1) * width])

    def send_or_add(layer, u):
        @pl.when(core != layer)
        def _():
            core_copy(u).start()

        if u >= ADD_LAG:
            @pl.when(core == layer)
            def _():
                add_own(u - ADD_LAG)

    def add_own(u):
        core_copy(u).wait_recv()
        w_all[core, u] = (w_all[core, u].astype(F32) + s0_recv[u].astype(F32)).astype(BF16)
        halving_copy(u, 0).start()

    def weight_gradients(layer):
        for u in range(first_down):
            value = product(layer, u).astype(BF16)
            for q in range(columns):
                w_all[layer, u, rows_at(u, q), :] = cut(value, q)
            send_or_add(layer, u)
        for i in range(tiles):
            value = dot_tn(act_all[layer, :, i * width:(i + 1) * width], dy_all[layer]).astype(BF16)
            for j in range(columns):
                u, q = first_down + j % tiles, i * columns // tiles + j // tiles
                w_all[layer, u, rows_at(u, q), :] = cut(value, j)
        for u in range(first_down, units):
            send_or_add(layer, u)

        @pl.when(core == layer)
        def _():
            for u in range(units - ADD_LAG, units):
                add_own(u)

    def project():
        @pl.when(section >= 2)
        def _():
            pool_arrival(1 - core).wait_recv()

        @pl.when(section < 2)
        def _():
            pool_arrival(0).wait_recv()
            pool_arrival(1).wait_recv()

        entries = cot_in.shape[0]
        position = column * entries + iota((entries, cot_in.shape[1]), 0)
        live = position < vocab[0]
        cot[...] = jnp.where(live, cot_in[...].astype(F32), 0.0).astype(BF16)
        rows = pool_all[...].reshape(entries, width)
        emb_out[...] = jnp.where(live, dot_nn(rows, proj[...]), 0.0)
        value = dot_tn(rows, cot[...]).astype(BF16)
        for q in range(columns):
            proj_sums[rows_at(units, q), :] = cut(value, q)

        halving_copy(units, 0).start()

    def project_now():
        project()
        for k in range(bits):
            advance(units, k)

    def put_vec(slot, layer):
        v_buf[slot, :, slice(0, width)] = vec[layer]
        for t in range(2):
            v_buf[slot, pl.ds(6 + t, 1), :] = upb[layer, :, t * (hidden // 2):(t + 1) * (hidden // 2)]

    def vec_copy(src, index, peer):
        return remote(v_buf.at[src], v_buf.at[index], v_send.at[index], v_recv.at[index], peer)

    def vec_peer_copy(k):
        return vec_copy(1 + 2 * k + (k > 0), 3 + 2 * k, bit_peer(k))

    def share_copy(half, way, peer):
        return remote(dxs.at[half], dxs.at[half], d_send.at[way], d_recv.at[half], peer)

    def finish(u, total):
        if u < 3:
            qkv_out[0, :, u * width:(u + 1) * width] = total
        elif u == 3:
            out_out[0] = total
        elif u < first_down:
            up_out[0, :, (u - 4) * width:(u - 3) * width] = total
        elif u < units:
            t = u - first_down
            down_out[0, t * piece:(t + 1) * piece, :] = total
        else:
            proj_out[...] = total

    def vec_step(k):
        if k == 0:
            put_vec(0, 1 - core)
            put_vec(1, core)
            vec_copy(0, 2, core_peer).start()
            vec_copy(0, 2, core_peer).wait_recv()
            v_buf[1] = v_buf[1] + v_buf[2]
            vec_peer_copy(0).start()
            return
        vec_peer_copy(k - 1).wait_recv()
        source = 1 + 2 * (k - 1) + (k > 1)
        total = v_buf[source] + v_buf[3 + 2 * (k - 1)]
        if k < bits:
            v_buf[2 * k + 2] = total
            vec_peer_copy(k).start()
            return
        lanes = width // columns
        share = hidden // columns
        for q in range(columns):
            @pl.when(column == q)
            def _(q=q):
                gain_out[0] = total[0:2, q * lanes:(q + 1) * lanes]
                shift_out[0] = total[2:6, q * lanes:(q + 1) * lanes]
                row, start = divmod(q * share, hidden // 2)
                upb_out[...] = total[6 + row:7 + row, start:start + share]

    def table_copy(d):
        peer = column_peer(d)
        return remote(parts.at[peer[1]], landed.at[column], t_send.at[d - 1], t_recv.at[column], peer)

    def table_parts():
        share_copy(1 - core, 0, core_peer).wait_recv()
        for half in range(2):
            slot_plan(ids_all[column, pl.ds(half, 1), :], match, table_out.shape[0], section * columns, columns,
                      jnp.int32(0), capacity)
            rows = dot_nn(match[...], dxs[half]).astype(BF16)
            parts[:, half * capacity:(half + 1) * capacity, :] = rows.reshape(columns, capacity, width)
        for d in range(1, columns):
            table_copy(d).start()
        landed[column] = parts[column]

    def table_finish():
        for d in range(1, columns):
            source = lax.rem(column + d, columns)
            remote(parts.at[0], landed.at[source], t_send.at[0], t_recv.at[source], (section, source)).wait_recv()
        grad = dot_tn(picks[...], landed[...].reshape(lists * capacity, width))
        table_out[...] = grad[:table_out.shape[0]]

    pl.when(stage == 0)(project_now)

    def seed(m):
        rows = rows_of(m)

        @pl.when(stage == 0)
        def _():
            backward_copy(m).wait_recv()
            dy_all[1, rows, :] = dy_in[rows, :]

        @pl.when(stage == 1)
        def _():
            for b in range(blocks):
                matrix = pool_matrix(count_row(m, b))
                entries = pl.ds(pl.multiple_of((m * blocks + b) * (LANES // 8), LANES // 8), LANES // 8)
                share = (pool_grad[entries, :] / jnp.sum(matrix, axis=1, keepdims=True)).astype(BF16)
                block = pl.ds(pl.multiple_of(m * MICRO + b * LANES, LANES), LANES)
                dy_all[1, block, :] = dot_tn(matrix.astype(BF16), share).astype(BF16)

    def backward(layer, m):
        rows = rows_of(m)
        dx = layer_backward(layer, m, dy_all[layer, rows, :])

        @pl.when(layer == 1)
        def _():
            dy_all[0, rows, :] = dx

        @pl.when(layer == 0)
        def _():
            dx_out[rows, :] = dx
            dxs[core, rows, :] = dx

        @pl.when((layer == 0) & (stage == 1))
        def _():
            y_out[rows, :] = dx
            backward_copy(m).start()

    last = micros - 1

    def backward_step(i, carry):
        m, turn = jnp.minimum(i // 2, last), i - 2 * jnp.minimum(i // 2, last)

        @pl.when(turn == 0)
        def _():
            seed(m)

        @pl.when(turn < 2)
        def _():
            backward(1 - turn, m)

        layer = 1 - turn + stage

        @pl.when((m == last) & (turn == 1) & (stage == 0))
        def _():
            share_copy(core, 0, core_peer).start()
            share_copy(core, 1, far_peer).start()

        @pl.when((m == last) & (layer >= 0) & (layer < 2))
        def _():
            weight_gradients(layer)
        return carry

    lax.fori_loop(0, 2 * micros + 1, backward_step, 0)

    lags = [PHASE_LAG * k for k in range(bits)]
    for step in range(units + lags[-1]):
        if step == SEND_NEAR:
            pl.when(section < 2)(table_parts)
        if step == SEND_FAR - 1:
            @pl.when(section >= 2)
            def _():
                share_copy(core, 0, far_peer).wait_recv()
                share_copy(core, 0, core_peer).start()
        if step == SEND_FAR:
            pl.when(section >= 2)(table_parts)
        if step == TABLE_STEP:
            table_finish()
        if step % VEC_GAP == 0 and step // VEC_GAP <= bits:
            vec_step(step // VEC_GAP)
        if step == 0:
            pl.when(stage == 1)(project)
        for k in range(bits):
            u = step - lags[k]
            if 0 <= u < units:
                advance(u, k)
            if u == PROJECT_AFTER:
                @pl.when(stage == 1)
                def _(k=k):
                    advance(units, k)
    for k in range((units + lags[-1] - 1) // VEC_GAP + 1, bits + 1):
        vec_step(k)

    @pl.when(stage == 1)
    def _():
        for m in range(micros):
            backward_copy(m).wait_send()

    vec_copy(0, 2, core_peer).wait_send()
    for k in range(bits):
        vec_peer_copy(k).wait_send()
    for u in range(units):
        core_copy(u).wait_send()
    for u in range(units + 1):
        for k in range(bits):
            halving_copy(u, k).wait_send()
    for d in range(1, columns):
        table_copy(d).wait_send()
    share_copy(core, 0, core_peer).wait_send()

    @pl.when(section < 2)
    def _():
        share_copy(core, 1, far_peer).wait_send()

    @pl.when(section >= 2)
    def _():
        for d in range(1, 4):
            pool_copy(d).wait_send()


def deliver_kernel(*refs):
    count = (len(refs) - 2) // 3
    sources, targets, staged = refs[:count], refs[count:2 * count], refs[2 * count:3 * count]
    in_sem, out_sem = refs[3 * count:]
    arrivals = [pltpu.make_async_copy(sources[i], staged[i], in_sem.at[i]) for i in range(count)]
    departures = [pltpu.make_async_copy(staged[i], targets[i], out_sem.at[i]) for i in range(count)]
    for copy in arrivals:
        copy.start()
    for arrival, departure in zip(arrivals, departures):
        arrival.wait()
        departure.start()
    for copy in departures:
        copy.wait()


def deliver(*values):
    count = len(values)
    hbm = pl.BlockSpec(memory_space=pl.ANY)
    size = sum(4 * value.size for value in values)
    return pl.pallas_call(
        deliver_kernel,
        out_shape=[jax.ShapeDtypeStruct(value.shape, value.dtype) for value in values],
        in_specs=[hbm] * count,
        out_specs=[hbm] * count,
        scratch_shapes=[pltpu.VMEM(value.shape, value.dtype) for value in values] + [
            pltpu.SemaphoreType.DMA((count,)), pltpu.SemaphoreType.DMA((count,))],
        cost_estimate=pl.CostEstimate(flops=0, bytes_accessed=2 * size, transcendentals=0),
        compiler_params=pltpu.CompilerParams(vmem_limit_bytes=VMEM_BYTES),
    )(*values)


def trunk(columns, x0, counts, pool_grad, own, theirs, cot, proj, picks, ids_all, span, vocab):
    rows, width = x0.shape
    hidden = own[5].shape[2]
    micros = rows // MICRO
    entries, out_width = cot.shape
    piece, tiles = width // columns, hidden // width
    bits = columns.bit_length() - 1
    units = 4 + 2 * tiles
    sizes = [(columns >> (k + 1)) * piece for k in range(bits)]
    capacity = picks.shape[0] // (2 * columns)
    vmem = pl.BlockSpec(memory_space=pltpu.VMEM)
    smem = pl.BlockSpec(memory_space=pltpu.SMEM)
    hbm = pl.BlockSpec(memory_space=pl.ANY)
    shape, sem, space = jax.ShapeDtypeStruct, pltpu.SemaphoreType.DMA, pltpu.VMEM
    outs = [
        shape((entries, out_width), F32), shape((1, 2, piece), F32), shape((1, 4, piece), F32),
        shape((1, hidden // columns), F32), shape((1, piece, 3 * width), F32), shape((1, piece, width), F32),
        shape((1, piece, hidden), F32), shape((1, tiles * piece, width), F32), shape((piece, out_width), F32),
        shape((span, width), F32), shape((rows, width), BF16),
    ]
    return pl.pallas_call(
        functools.partial(trunk_kernel, columns, width, hidden, micros),
        out_shape=outs,
        in_specs=[vmem] * 3 + [hbm] * 14 + [vmem] * 4 + [smem],
        out_specs=[vmem] * len(outs),
        scratch_shapes=[space((units + 1, size, width), BF16 if size >= 16 else F32) for size in sizes] + [
            space((2,) + p.shape[1:], p.dtype) for p in own[:3]] + [
            space((2, units, width, width), BF16),
            space((2, rows, width), BF16), space((2, rows, 3 * width), BF16), space((2, rows, width), BF16),
            space((2, rows, width), BF16), space((2, rows, width), BF16), space((2, rows, hidden), BF16),
            space((2, rows, hidden), BF16), space((2, rows, width), BF16),
            space((rows, width), BF16), space((rows, width), BF16), space((2, rows, width), F32),
            space((2, rows // LANES, 8 * HEADS, LANES), F32), space((rows, width), BF16), space((rows, width), BF16),
            space((2, 8, width), F32), space((2, 1, hidden), F32), space((rows // 8, width), BF16),
            space((units + 1, 2 * piece, width) if sizes[-1] < 16 else (8, LANES), F32),
            space((units, width, width), BF16), space((width, width), BF16),
            space((3 + 2 * bits, 8, hidden // 2), F32), space((2, entries // 2, width), BF16),
            space((entries, out_width), BF16), space((columns * capacity, rows), BF16), space((2, rows, width), BF16),
            space((columns, 2 * capacity, width), BF16), space((columns, 2 * capacity, width), BF16),
            sem((micros,)), sem((micros,)), sem((micros,)), sem((micros,)), sem((3 + units, 2)),
            sem((units,)), sem((units,)), sem((bits, units + 1)), sem((bits, units + 1)),
            sem((3 + 2 * bits,)), sem((3 + 2 * bits,)), sem((3,)), sem((2,)), sem((columns - 1,)), sem((columns,)),
            sem((2,)), sem((2,)),
        ],
        compiler_params=pltpu.CompilerParams(collective_id=1, has_side_effects=True, vmem_limit_bytes=VMEM_BYTES),
    )(x0, counts, pool_grad, *own, *theirs, cot, proj, picks, ids_all, vocab)


def local(table, piece_ids, piece_counts, vocab_size, norm_gain, shift_bias, up_bias, qkv_weight, out_weight,
          up_weight, down_weight, proj_weight, embed_cotangent):
    section = lax.axis_index("section")
    columns = lax.axis_size("dp")
    core = lax.rem(section, 2)
    entries, pieces = piece_ids.shape
    half = entries // 2
    ids = piece_ids.reshape(2, half * pieces)
    my_counts = lax.dynamic_slice_in_dim(piece_counts, core * half, half, 0)
    count_rows = jnp.repeat(my_counts, pieces).reshape(-1, LANES)
    own = (norm_gain, shift_bias, up_bias[:, None, :], qkv_weight, out_weight, up_weight, down_weight)
    x0, picks, ids_all, most, pool_grad, *theirs = lookup(
        columns, ids, table, embed_cotangent, proj_weight, vocab_size, *own)
    capacity = picks.shape[0] // (2 * columns)
    turns = (most[0] + capacity - 1) // capacity
    x0 = lax.fori_loop(
        1, turns, lambda turn, x: x + more_lookup(columns, turn.reshape(1), ids_all, table), x0)
    emb, g_gain, g_shift, g_bias, g_qkv, g_out, g_up, g_down, g_proj, g_table, dx = trunk(
        columns, x0, count_rows, pool_grad, own, theirs, embed_cotangent, proj_weight, picks, ids_all, table.shape[0],
        vocab_size)
    g_table = lax.fori_loop(
        1, turns, lambda turn, held: more_return(columns, turn.reshape(1), ids_all, dx, held), g_table)
    return tuple(deliver(emb, g_table, g_gain, g_shift, g_bias, g_qkv, g_out, g_up, g_down, g_proj))


def solution(mesh):
    return jax.shard_map(
        local,
        mesh=mesh,
        in_specs=(
            P(("section", "dp"), None), P("dp", None), P("dp"), P(), P("section", None, None),
            P("section", None, None), P("section", None), P("section", None, None), P("section", None, None),
            P("section", None, None), P("section", None, None), P(None, "section"), P("dp", "section"),
        ),
        out_specs=(
            P("dp", "section"), P(("section", "dp"), None), P("section", None, "dp"), P("section", None, "dp"),
            P("section", "dp"), P("section", "dp", None), P("section", "dp", None), P("section", "dp", None),
            P("section", "dp", None), P("dp", "section"),
        ),
        check_vma=False,
    )
```
